32 devices in a mesh: dp: 8 (over z, x), expert: 4 (over y, core).
Axes of the slice: x: 2, y: 2, z: 4, core: 2. Of those that a mesh axis runs over, the one named last changes fastest.
Arguments:
- tokens: bfloat16 [10240, 1536], P(('dp', 'expert')), may hold values from -6 to 6
- w_query: bfloat16 [1536, 1536], P(('dp', 'expert')), may hold values from -0.15625 to 0.15625
- w_key: bfloat16 [1536, 512], P(('dp', 'expert')), may hold values from -0.15625 to 0.15625
- w_value: bfloat16 [1536, 512], P(('dp', 'expert')), may hold values from -0.15625 to 0.15625
- w_out: bfloat16 [1536, 1536], P(('dp', 'expert')), may hold values from -0.625 to 0.625
- w_router: bfloat16 [1536, 40], P(('dp', 'expert')), may hold values from -0.078125 to 0.078125
- gain_attn: bfloat16 [1536], P(('dp', 'expert')), may hold values from 0.099609375 to 1.8984375
- gain_moe: bfloat16 [1536], P(('dp', 'expert')), may hold values from 0.099609375 to 1.8984375
- w_gate: bfloat16 [40, 1536, 512], P('expert'), may hold values from -0.15625 to 0.15625
- w_up: bfloat16 [40, 1536, 512], P('expert'), may hold values from -0.15625 to 0.15625
- w_down: bfloat16 [40, 512, 1536], P('expert'), may hold values from -0.75 to 0.75
- segments: int32 [10240], P('dp'), may hold values from 0 to 1279, as said below
- routes: int32 [10240, 8], P(('dp', 'expert')), may hold values from 0 to 39, all different within a row
- priority: int32 [10240, 8], P(('dp', 'expert')), may hold values from 0 to 7, each once within a row
- cotangent: bfloat16 [10240, 1536], P(('dp', 'expert')), may hold values from -6 to 6
Outputs:
- outputs: bfloat16 [10240, 1536], P(('dp', 'expert'))
- grad_tokens: float32 [10240, 1536], P(('dp', 'expert'))
- grad_query: float32 [1536, 1536], P(('dp', 'expert'))
- grad_key: float32 [1536, 512], P(('dp', 'expert'))
- grad_value: float32 [1536, 512], P(('dp', 'expert'))
- grad_out: float32 [1536, 1536], P(('dp', 'expert'))
- grad_router: float32 [1536, 40], P(('dp', 'expert'))
- grad_gain_attn: float32 [1536], P(('dp', 'expert'))
- grad_gain_moe: float32 [1536], P(('dp', 'expert'))
- grad_gate: float32 [40, 1536, 512], P('expert', 'dp')
- grad_up: float32 [40, 1536, 512], P('expert', 'dp')
- grad_down: float32 [40, 512, 1536], P('expert', 'dp')
The draws below stay inside these ranges and needn't reach their ends.
Inputs may be any that keep to these rules, and one draw needn't show every extreme that they name: `segments`: within each sequence of 1280 tokens, a token's segment number is the position in that sequence of its segment's first token; the last position of a sequence starts a segment. `routes`: each token names 8 different experts; every expert is named by some token. `priority`: each token's row holds every rank once.
All inputs are finite; a program needn't handle non-finite values.
Results may differ from the reference program's by a relative error of at most 0.017.
Values may be sent and summed in bfloat16 or wider, within the bound.
A program may use at most 320 MiB of HBM per device.

```python
from functools import partial
import jax
import jax.numpy as jnp
from jax import lax

D = 1536
H = 24
KVH = 8
HD = 64
FF = 512
TOPK = 8
TOK_DEV = 320
EXPERTS = 40
CAP = 64
LENGTH = 1280
TOKENS = 10240
N_EXPERT = 4


def segment_row(base_key, length, rows_device):
    first_key, second_key, third_key = jax.random.split(base_key, 3)
    margin = max(rows_device // 2, 2)
    opening = jax.random.randint(first_key, (), 1, margin)
    closing = jax.random.randint(second_key, (), length - margin, length - 1)
    coin_flips = jax.random.randint(third_key, (length,), 0, 16) == 0
    places = jnp.arange(length, dtype=jnp.int32)
    inside = (places > opening) & (places <= closing)
    starts = jnp.where(inside, False, coin_flips) | (places == opening) | (places == closing + 1) | (places == 0) | (places == length - 1)
    return lax.cummax(jnp.where(starts, places, 0), axis=0).astype(jnp.int32)


def draw_segments(key, part):
    key = jax.random.fold_in(key, 11)
    sequence_count = TOKENS // LENGTH
    row_keys = jax.random.split(key, sequence_count)
    return jax.vmap(partial(segment_row, length=LENGTH, rows_device=TOK_DEV))(row_keys).reshape(TOKENS)


def block_levels(stream_key, shape, cuts, low, top_value):
    def one(dim, shards_of):
        heights = jax.random.uniform(jax.random.fold_in(jax.random.fold_in(stream_key, 6), dim), (shards_of,), jnp.float32, low / len(cuts), top_value / len(cuts))
        return jnp.repeat(jnp.exp(heights), shape[dim] // shards_of).reshape((-1,) + (1,) * (len(shape) - dim - 1))

    factor_of = one(*cuts[0])
    for cut in cuts[1:]:
        factor_of = factor_of * one(*cut)
    return factor_of


def choose_distinct(stream_key, rows, amount, top, lift):
    ranking = jax.random.permutation(jax.random.fold_in(stream_key, 1), amount)
    boost = ranking
    for power in range(3):
        boost = boost * boost // amount
    boost = boost * lift // amount
    chance = jax.random.randint(jax.random.fold_in(stream_key, 2), (rows, amount), 0, 4096) + boost
    holders = jax.random.permutation(jax.random.fold_in(stream_key, 3), rows)[jnp.arange(amount) % rows]
    chance = jnp.where(jnp.arange(rows)[:, None] == holders[None, :], 1 << 14, chance)
    merit = chance * amount + jnp.arange(amount)
    return lax.top_k(merit.astype(jnp.int32), top)[1].astype(jnp.int32)


def normal_values(own_key, dims, scale, bound, cuts=(), kind=jnp.bfloat16):
    entries = scale * jax.random.normal(own_key, dims, jnp.float32)
    if cuts:
        entries = entries * block_levels(own_key, dims, cuts, -0.22, 0.18)
    return jnp.clip(entries, -bound, bound).astype(kind)


def setup_inputs(seed: int = 0) -> dict:
    key_of = jax.random.split(jax.random.key(seed), 16)
    return {
        "tokens": normal_values(key_of[0], (TOKENS, D), 1.0, 6.0, ((0, 32),)),
        "w_query": normal_values(key_of[1], (D, H * HD), D ** -0.5, 0.15625, ((0, 32),)),
        "w_key": normal_values(key_of[2], (D, KVH * HD), D ** -0.5, 0.15625, ((0, 32),)),
        "w_value": normal_values(key_of[3], (D, KVH * HD), D ** -0.5, 0.15625, ((0, 32),)),
        "w_out": normal_values(key_of[4], (H * HD, D), (H * HD // 16) ** -0.5, 0.625, ((0, 32),)),
        "w_router": normal_values(key_of[5], (D, EXPERTS), (4 * D) ** -0.5, 0.078125, ((0, 32),)),
        "gain_attn": jnp.clip(1.0 + 0.18 * jax.random.normal(key_of[6], (D,), jnp.float32), 0.099609375, 1.8984375).astype(jnp.bfloat16),
        "gain_moe": jnp.clip(1.0 + 0.18 * jax.random.normal(key_of[7], (D,), jnp.float32), 0.099609375, 1.8984375).astype(jnp.bfloat16),
        "w_gate": normal_values(key_of[8], (EXPERTS, D, FF), D ** -0.5, 0.15625, ((0, 4),)),
        "w_up": normal_values(key_of[9], (EXPERTS, D, FF), D ** -0.5, 0.15625, ((0, 4),)),
        "w_down": normal_values(key_of[10], (EXPERTS, FF, D), (FF // 8) ** -0.5, 0.75, ((0, 4),)),
        "segments": draw_segments(jax.random.fold_in(key_of[15], 71), 0),
        "routes": choose_distinct(key_of[12], TOKENS, EXPERTS, TOPK, 1638),
        "priority": jax.vmap(lambda own: jax.random.permutation(own, TOPK))(jax.random.split(key_of[13], TOKENS)).reshape((TOKENS, TOPK)).astype(jnp.int32),
        "cotangent": normal_values(key_of[14], (TOKENS, D), 1.0, 6.0, ((0, 32),)),
    }


@jax.custom_vjp
def low(v):
    return lax.optimization_barrier(v.astype(jnp.bfloat16)).astype(jnp.float32)

@jax.custom_vjp
def low_back(v):
    return v

def low_keep(v):
    return (low(v), None)

def low_pass(kept, grad):
    return (grad,)

def back_keep(v):
    return (v, None)

def back_low(kept, grad):
    return (low(grad),)
low.defvjp(low_keep, low_pass)
low_back.defvjp(back_keep, back_low)
epsilon = 1e-06
rope_base = 10000.0
masked_score = -1e+30
precise = lax.Precision.HIGHEST

def norm_rows(values, gain_row):
    scaling = lax.rsqrt(lax.optimization_barrier(jnp.mean(values * values, axis=-1, keepdims=True)) + epsilon)
    return values * scaling * gain_row

def rope_tables(length):
    frequency = rope_base ** (-2.0 * jnp.arange(HD // 2, dtype=jnp.float32) / HD)
    angles = jnp.arange(length, dtype=jnp.float32)[:, None] * frequency[None, :]
    return (jnp.cos(angles), jnp.sin(angles))

def rotate(vectors, cosine, sine_part):
    halfway = vectors.shape[-1] // 2
    first_half = vectors[..., :halfway]
    second_half = vectors[..., halfway:]
    cos_rows = cosine[:, None, :]
    sin_rows = sine_part[:, None, :]
    return jnp.concatenate([first_half * cos_rows - second_half * sin_rows, second_half * cos_rows + first_half * sin_rows], axis=-1)

def slot_table(routes, priority, experts, capacity):
    top_count = routes.shape[1]
    count_rows = routes.shape[0]
    expert_hot = (routes[:, :, None] == jnp.arange(experts, dtype=jnp.int32)[None, None, :]).astype(jnp.int32)
    rank_hot = (priority[:, :, None] == jnp.arange(top_count, dtype=jnp.int32)[None, None, :]).astype(jnp.int32)
    per_rank = jnp.transpose(lax.optimization_barrier(jnp.sum(rank_hot[:, :, :, None] * expert_hot[:, :, None, :], axis=1)), (1, 0, 2)).astype(jnp.int32)
    flat_hot = per_rank.reshape(top_count * count_rows, experts)
    earlier = (jnp.cumsum(flat_hot, axis=0, dtype=jnp.int32) - flat_hot).reshape(per_rank.shape)
    token_ids = jnp.broadcast_to(jnp.arange(count_rows, dtype=jnp.int32)[:, None], routes.shape)
    slot_ids = earlier[priority, token_ids, routes].astype(jnp.int32)
    return (slot_ids, slot_ids < capacity)

def dispatch_table(routes, slot_ids, kept_pairs, experts, capacity):
    count_rows = routes.shape[0]
    token_ids = jnp.broadcast_to(jnp.arange(count_rows, dtype=jnp.int32)[:, None], routes.shape)
    target = jnp.where(kept_pairs, routes * capacity + slot_ids, experts * capacity).astype(jnp.int32)
    slot_owner = jnp.full((experts * capacity,), count_rows, dtype=jnp.int32)
    return slot_owner.at[target.reshape(-1)].set(token_ids.reshape(-1), mode='drop')

def take_rows(source, indices):
    return jnp.take(source, indices, axis=0)

def expert_block(rows, w_gate, w_up, w_down):
    gate_pre = low_back(jnp.einsum('nesd,edf->nesf', rows, w_gate, precision=precise))
    up_pre = low_back(jnp.einsum('nesd,edf->nesf', rows, w_up, precision=precise))
    hidden = low(jax.nn.silu(gate_pre) * up_pre)
    return low(low_back(jnp.einsum('nesf,efd->nesd', hidden, w_down, precision=precise)))

def sequence_layer(inputs, w_query, w_key, w_value, w_out, w_router, gain_attn, gain_moe, w_gate, w_up, w_down, seg_ids, route_rows, slot_owner, combine_index, kept_weight):
    length = inputs.shape[0]
    group_size = H // KVH
    cosine, sine_part = rope_tables(length)
    normed = low(norm_rows(inputs, gain_attn))
    query_pre = low_back(jnp.dot(normed, w_query, precision=precise)).reshape(length, H, HD)
    key_pre = low_back(jnp.dot(normed, w_key, precision=precise)).reshape(length, KVH, HD)
    value_rows = low(low_back(jnp.dot(normed, w_value, precision=precise))).reshape(length, KVH, HD)
    query_rot = low(rotate(query_pre, cosine, sine_part)).reshape(length, KVH, group_size, HD)
    key_rot = low(rotate(key_pre, cosine, sine_part))
    positions = jnp.arange(length, dtype=jnp.int32)
    allowed = (positions[None, :] <= positions[:, None]) & (seg_ids[None, :] == seg_ids[:, None])

    def attend(pieces):
        query_group, key_group, value_group = pieces
        scores = low_back(jnp.einsum('tgd,sd->gts', query_group, key_group, precision=precise) * HD ** (-0.5))
        softmax_rows = jax.nn.softmax(jnp.where(allowed[None], scores, masked_score), axis=-1)
        return jnp.einsum('gts,sd->tgd', low(softmax_rows), value_group, precision=precise)
    attended = lax.map(jax.checkpoint(attend), (jnp.transpose(query_rot, (1, 0, 2, 3)), jnp.transpose(key_rot, (1, 0, 2)), jnp.transpose(value_rows, (1, 0, 2))))
    mixed_heads = low(low_back(jnp.transpose(attended, (1, 0, 2, 3)).reshape(length, H * HD)))
    middle = inputs + low_back(jnp.dot(mixed_heads, w_out, precision=precise))
    normed_moe = low(norm_rows(middle, gain_moe))
    logits = low_back(jnp.dot(normed_moe, w_router, precision=precise))
    gate_probs = jax.nn.softmax(jnp.take_along_axis(logits, route_rows, axis=1), axis=-1)
    blocks = normed_moe.reshape(N_EXPERT, TOK_DEV, D)
    padded = jnp.concatenate([blocks, jnp.zeros((N_EXPERT, 1, D), jnp.float32)], axis=1)
    rows = low_back(jax.vmap(take_rows)(padded, slot_owner)).reshape(N_EXPERT, EXPERTS, CAP, D)
    results = expert_block(rows, w_gate, w_up, w_down).reshape(N_EXPERT, EXPERTS * CAP, D)
    picked = jax.vmap(take_rows)(results, combine_index).reshape(length, TOPK, D)
    branch = lax.optimization_barrier(jnp.sum((gate_probs * kept_weight)[:, :, None] * picked, axis=1))
    return middle + branch

def reference(tokens, w_query, w_key, w_value, w_out, w_router, gain_attn, gain_moe, w_gate, w_up, w_down, segments, routes, priority, cotangent):
    weights = tuple((weight_arg.astype(jnp.float32) for weight_arg in (w_query, w_key, w_value, w_out, w_router, gain_attn, gain_moe, w_gate, w_up, w_down)))
    sequence_count = TOKENS // LENGTH
    inputs = tokens.astype(jnp.float32).reshape(sequence_count, LENGTH, D)
    grads_given = cotangent.astype(jnp.float32).reshape(sequence_count, LENGTH, D)
    seg_all = segments.reshape(sequence_count, LENGTH)
    route_blocks = routes.reshape(sequence_count * N_EXPERT, TOK_DEV, TOPK)
    order_blocks = priority.reshape(sequence_count * N_EXPERT, TOK_DEV, TOPK)
    slot_ids, kept_pairs = jax.vmap(partial(slot_table, experts=EXPERTS, capacity=CAP))(route_blocks, order_blocks)
    owners = jax.vmap(partial(dispatch_table, experts=EXPERTS, capacity=CAP))(route_blocks, slot_ids, kept_pairs)
    owners = owners.reshape(sequence_count, N_EXPERT, EXPERTS * CAP)
    combine_index = (route_blocks * CAP + jnp.minimum(slot_ids, CAP - 1)).astype(jnp.int32).reshape(sequence_count, N_EXPERT, TOK_DEV * TOPK)
    kept_weight = kept_pairs.astype(jnp.float32).reshape(sequence_count, LENGTH, TOPK)
    route_seqs = routes.reshape(sequence_count, LENGTH, TOPK)

    def one_sequence(running, pieces):
        sequence_in, sequence_grad, sequence_segs, sequence_routes, sequence_owner, sequence_index, sequence_kept = pieces

        def layer(layer_input, *params):
            return sequence_layer(layer_input, *params, sequence_segs, sequence_routes, sequence_owner, sequence_index, sequence_kept)
        result, pull_back = jax.vjp(layer, sequence_in, *weights)
        gradients = pull_back(sequence_grad)
        running = tuple((acc_now + fresh_grad for acc_now, fresh_grad in zip(running, gradients[1:])))
        return (running, (result.astype(jnp.bfloat16), gradients[0]))
    start_sums = tuple((jnp.zeros_like(weight_arg) for weight_arg in weights))
    sums, (outputs, grad_inputs) = lax.scan(one_sequence, start_sums, (inputs, grads_given, seg_all, route_seqs, owners, combine_index, kept_weight))
    return (outputs.reshape(TOKENS, D), grad_inputs.reshape(TOKENS, D), sums[0], sums[1], sums[2], sums[3], sums[4], sums[5], sums[6], sums[7], sums[8], sums[9])
```

```python
import functools

import jax
import jax.numpy as jnp
from jax import lax
from jax.experimental import pallas as pl
from jax.experimental.pallas import tpu as pltpu
from jax.sharding import Mesh
from jax.sharding import PartitionSpec as P

HD = 64
QUAD = 4
F32 = jnp.float32
BF16 = jnp.bfloat16

epsilon = 1e-06
rope_base = 10000.0
masked_score = -1e30


def dot32(spec, a, b):
    return jnp.einsum(spec, a, b, preferred_element_type=F32)


def norm_parts(values, gain_row):
    scaling = lax.rsqrt(jnp.mean(values * values, axis=-1, keepdims=True) + epsilon)
    normed = values * scaling
    return (normed * gain_row, normed, scaling)


def norm_back(grad_rows, normed, scaling, gain_row):
    grad_normed = grad_rows * gain_row
    grad_gain = jnp.sum(grad_rows * normed, axis=0)
    inner_sum = jnp.mean(grad_normed * normed, axis=-1, keepdims=True)
    return (scaling * (grad_normed - normed * inner_sum), grad_gain)


def rope_tables(positions, head_size):
    frequency = rope_base ** (-2.0 * jnp.arange(head_size // 2, dtype=F32) / head_size)
    angles = positions.astype(F32)[:, None] * frequency[None, :]
    return (jnp.cos(angles), jnp.sin(angles))


def slot_dense(routes, priority, experts, capacity):
    rows, top_count = routes.shape
    hot = routes[:, :, None] == jnp.arange(experts, dtype=jnp.int32)
    rank = jnp.sum(jnp.where(hot, priority[:, :, None] + 1, 0), axis=1) - 1
    per_rank = rank[None] == jnp.arange(top_count, dtype=jnp.int32)[:, None, None]
    flat = jnp.transpose(per_rank.astype(BF16), (1, 0, 2)).reshape(rows, top_count * experts)
    index = jnp.arange(rows, dtype=jnp.int32)
    before = (index[None, :] < index[:, None]).astype(BF16)
    within = jnp.dot(before, flat, preferred_element_type=F32).reshape(rows, top_count, experts)
    totals = jnp.sum(per_rank.astype(F32), axis=1)
    base = jnp.cumsum(totals, axis=0) - totals
    slot = jnp.sum(
        jnp.where(jnp.transpose(per_rank, (1, 0, 2)), within + base[None], 0.0), axis=1
    )
    named = rank >= 0
    return named, jnp.where(named & (slot < capacity), slot, -1.0)


NT=(((1,),(1,)),((),()))
NN=(((1,),(0,)),((),()))
TN=(((0,),(0,)),((),()))

def mm(a,b,dims=NN):
    return lax.dot_general(a,b,dims,preferred_element_type=F32)

def swap_halves(x):
    lane=lax.broadcasted_iota(jnp.int32,(x.shape[0],128),1)
    low=(lane%HD)<HD//2
    parts=[]
    for c in range(x.shape[1]//128):
        g=x[:,c*128:(c+1)*128]
        parts.append(jnp.where(low,pltpu.roll(g,128-HD//2,1),pltpu.roll(g,HD//2,1)))
    return jnp.concatenate(parts,axis=1)

def bias_block(seg_row, keys, first):
    n=seg_row.shape[1]
    s=lax.broadcasted_iota(jnp.int32,(keys,n),0)
    t=lax.broadcasted_iota(jnp.int32,(keys,n),1)+first
    return jnp.where((s<=t)&(s>=seg_row),0.0,masked_score)

def forward_kernel(heads, kv_heads, block, x_ref, gain_ref, w_ref, cos_ref, sin_ref, seg_ref,
                   h1_ref, q_ref, k_ref, v_ref, o_ref, lse_ref, vt_ref):
    length=x_ref.shape[0]
    group=heads//kv_heads
    nq=heads*HD; nk=kv_heads*HD
    for i in range(length//block):
        rows=pl.ds(i*block,block)
        x=x_ref[rows,:].astype(F32)
        r=lax.rsqrt(jnp.mean(x*x,axis=1,keepdims=True)+epsilon)
        h1=(x*r*gain_ref[...]).astype(BF16)
        h1_ref[rows,:]=h1
        qkv=mm(h1,w_ref[...])
        qk=qkv[:,:nq+nk]
        c=jnp.concatenate([cos_ref[rows,:]]*((nq+nk)//128),axis=1)
        s=jnp.concatenate([sin_ref[rows,:]]*((nq+nk)//128),axis=1)
        qk=(qk*c+swap_halves(qk)*s).astype(BF16)
        v=qkv[:,nq+nk:].astype(BF16)
        for h in range(heads):
            q_ref[h,rows,:]=qk[:,h*HD:(h+1)*HD]
        vt=v.astype(F32).T.astype(BF16)
        for h in range(kv_heads):
            k_ref[h,rows,:]=qk[:,nq+h*HD:nq+(h+1)*HD]
            v_ref[h,rows,:]=v[:,h*HD:(h+1)*HD]
            vt_ref[h,:,rows]=vt[h*HD:(h+1)*HD,:]
        keys=(i+1)*block
        bias=bias_block(seg_ref[:,rows],keys,i*block)
        outs=[]
        for h in range(heads):
            g=h//group
            st=mm(k_ref[g,pl.ds(0,keys),:],q_ref[h,rows,:]*BF16(HD**-0.5),NT)+bias
            top=jnp.max(st,axis=0,keepdims=True)
            p=jnp.exp(st-top)
            total=jnp.sum(p,axis=0,keepdims=True)
            ot=mm(vt_ref[g,:,pl.ds(0,keys)],p.astype(BF16))
            outs.append(ot/total)
            lse_ref[pl.ds(h,1),rows]=top+jnp.log(total)
        o_ref[rows,:]=jnp.concatenate(outs,axis=0).T.astype(BF16)

def attention_forward(x_all,gain,w_qkv,cosine,sine,segments,heads,kv_heads,block=256):
    length,width=x_all.shape
    V=pl.BlockSpec(memory_space=pltpu.VMEM)
    nq=heads*HD
    pad=-(-heads//8)*8
    return pl.pallas_call(functools.partial(forward_kernel,heads,kv_heads,block),
        out_shape=(jax.ShapeDtypeStruct((length,width),BF16),
          jax.ShapeDtypeStruct((heads,length,HD),BF16),jax.ShapeDtypeStruct((kv_heads,length,HD),BF16),
          jax.ShapeDtypeStruct((kv_heads,length,HD),BF16),jax.ShapeDtypeStruct((length,nq),BF16),
          jax.ShapeDtypeStruct((pad,length),F32)),
        in_specs=[V]*6,out_specs=(V,)*6,
        scratch_shapes=[pltpu.VMEM((kv_heads,HD,length),BF16)],
        compiler_params=pltpu.CompilerParams(vmem_limit_bytes=56<<20),
        cost_estimate=pl.CostEstimate(flops=2*length*width*w_qkv.shape[1]+2*heads*length*length*256,bytes_accessed=14<<20,transcendentals=heads*length*length//2),
        name="attention_forward")(x_all,gain.reshape(1,-1),w_qkv,cosine,sine,segments.reshape(1,-1))

def backward_kernel(heads, kv_heads, block, q_ref, k_ref, v_ref, do_ref, lse_ref, cos_ref, sin_ref, seg_ref,
                    dqkv_ref, kt_ref, dk_ref, dv_ref):
    length=q_ref.shape[1]
    group=heads//kv_heads
    nq=heads*HD; nk=kv_heads*HD
    factor=HD**-0.5
    dk_ref[...]=jnp.zeros_like(dk_ref)
    dv_ref[...]=jnp.zeros_like(dv_ref)
    for g in range(kv_heads):
        kt_ref[g]=k_ref[g].astype(F32).T.astype(BF16)
    for i in range(length//block):
        rows=pl.ds(i*block,block)
        keys=(i+1)*block
        span=pl.ds(0,keys)
        bias=bias_block(seg_ref[:,rows],keys,i*block)
        dqs=[]
        for h in range(heads):
            g=h//group
            q=q_ref[h,rows,:]
            do=do_ref[rows,h*HD:(h+1)*HD]
            st=mm(k_ref[g,span,:],q*BF16(factor),NT)+bias
            p=jnp.exp(st-lse_ref[pl.ds(h,1),rows])
            dpt=mm(v_ref[g,span,:],do,NT)
            inner=jnp.sum(p*dpt,axis=0,keepdims=True)
            ds=(p*(dpt-inner)).astype(BF16)
            dv_ref[g,span,:]+=mm(p.astype(BF16),do)
            dk_ref[g,span,:]+=mm(ds,q)
            dqs.append(mm(kt_ref[g,:,span],ds))
        dq=jnp.concatenate(dqs,axis=0).T*factor
        c=jnp.concatenate([cos_ref[rows,:]]*(nq//128),axis=1)
        s=jnp.concatenate([sin_ref[rows,:]]*(nq//128),axis=1)
        dqkv_ref[rows,:nq]=(dq*c-swap_halves(dq)*s).astype(BF16)
    dk=jnp.concatenate([dk_ref[g] for g in range(kv_heads)],axis=1)*factor
    c=jnp.concatenate([cos_ref[...]]*(nk//128),axis=1)
    s=jnp.concatenate([sin_ref[...]]*(nk//128),axis=1)
    dqkv_ref[:,nq:nq+nk]=(dk*c-swap_halves(dk)*s).astype(BF16)
    dqkv_ref[:,nq+nk:]=jnp.concatenate([dv_ref[g] for g in range(kv_heads)],axis=1).astype(BF16)

def attention_backward(q,k,v,do,lse,cosine,sine,segments,block=256):
    heads,length,_=q.shape; kv_heads=k.shape[0]
    V=pl.BlockSpec(memory_space=pltpu.VMEM)
    return pl.pallas_call(functools.partial(backward_kernel,heads,kv_heads,block),
        out_shape=jax.ShapeDtypeStruct((length,(heads+2*kv_heads)*HD),BF16),
        in_specs=[V]*8,out_specs=V,
        scratch_shapes=[pltpu.VMEM((kv_heads,HD,length),BF16),pltpu.VMEM((kv_heads,length,HD),F32),pltpu.VMEM((kv_heads,length,HD),F32)],
        compiler_params=pltpu.CompilerParams(vmem_limit_bytes=56<<20),
        cost_estimate=pl.CostEstimate(flops=5*heads*length*length*256,bytes_accessed=10<<20,transcendentals=heads*length*length//2),
        name="attention_backward")(q,k,v,do,lse,cosine,sine,segments.reshape(1,-1))


ALL = ("q", "r", "expert")
DP = ("q", "r")
GROUP = ("r", "expert")


def shards(
    tokens, w_query, w_key, w_value, w_out, w_router, gain_attn, gain_moe,
    w_gate, w_up, w_down, segments, routes, priority, cotangent,
):
    rows_here, width = tokens.shape
    E = lax.axis_size("expert")
    R = lax.axis_size("r")
    Q = lax.axis_size("q")
    e = lax.axis_index("expert")
    r = lax.axis_index("r")
    shard_rows = w_query.shape[0]
    local = w_gate.shape[0]
    experts = local * E
    ffn = w_gate.shape[2]
    capacity = rows_here * routes.shape[1] // experts
    length = rows_here * E
    sources = R * E
    q_cols = w_query.shape[1] // E
    k_cols = w_key.shape[1] // E
    pieces = jnp.concatenate(
        [w.reshape(shard_rows, E, -1) for w in (w_query, w_key, w_value)], axis=2
    )
    mine = lax.all_to_all(pieces, "expert", split_axis=1, concat_axis=0, tiled=True)
    mine = mine.reshape(shard_rows * E, -1)
    w_qkv = lax.all_gather(mine, DP, axis=0, tiled=True)
    x_all = lax.all_gather(tokens, "expert", axis=0, tiled=True)
    small = jnp.concatenate([w_router, gain_attn[:, None], gain_moe[:, None]], axis=1)
    small = lax.all_gather(small, ALL, axis=0, tiled=True)
    router_full = small[:, :experts]
    attn_gain = small[:, experts].astype(F32)
    moe_gain = small[:, experts + 1].astype(F32)
    out_full = lax.all_gather(w_out, ALL, axis=0, tiled=True)
    dm_all = lax.all_gather(cotangent, GROUP, axis=0, tiled=True).reshape(
        sources, rows_here, width
    )
    named, slots = slot_dense(routes, priority, experts, capacity)

    positions = jnp.arange(length, dtype=jnp.int32)
    cosine, sine = rope_tables(positions, HD)
    cosine = jnp.tile(cosine, (1, 4))
    sine = jnp.tile(jnp.concatenate([-sine, sine], axis=1), (1, 2))
    kv_heads = k_cols // HD
    h1_all, query, key, value, mixed, log_total = attention_forward(
        x_all, attn_gain, w_qkv, cosine, sine, segments, q_cols // HD, kv_heads
    )
    mixed_own = lax.all_to_all(mixed, "expert", split_axis=0, concat_axis=1, tiled=True)
    inputs = tokens.astype(F32)
    middle = inputs + jnp.dot(mixed_own, out_full, preferred_element_type=F32)
    h2, unit_moe, scale_moe = norm_parts(middle, moe_gain)
    h2 = h2.astype(BF16)
    logits = jnp.dot(h2, router_full, preferred_element_type=F32)
    probs = jax.nn.softmax(jnp.where(named, logits, masked_score), axis=-1)
    probs = jnp.where(named, probs, 0.0)
    h2_all = lax.all_gather(h2, GROUP, axis=0, tiled=True).reshape(sources, rows_here, width)
    table = lax.all_gather(jnp.concatenate([slots, probs], axis=1), GROUP, axis=0, tiled=True)
    table = table.reshape(sources, rows_here, 2 * experts)
    slot_all, prob_all = table[..., :experts], table[..., experts:]

    count = -(-local // R)
    first = (r * local + R // 2) // R
    last = ((r + 1) * local + R // 2) // R
    y_part = jnp.zeros((sources, rows_here, width), F32)
    dr_part = jnp.zeros((sources, rows_here, width), F32)
    dg_part = jnp.zeros((sources, rows_here, experts), F32)
    gate_list, up_list, down_list = [], [], []
    for i in range(count):
        live = first + i < last
        place = jnp.minimum(first + i, local - 1)
        column = e * local + place
        wg = lax.dynamic_index_in_dim(w_gate, place, 0, False)
        wu = lax.dynamic_index_in_dim(w_up, place, 0, False)
        wd = lax.dynamic_index_in_dim(w_down, place, 0, False)
        slot_e = lax.dynamic_index_in_dim(slot_all, column, 2, False)
        prob_e = lax.dynamic_index_in_dim(prob_all, column, 2, False)
        hot = (slot_e[:, None, :] == jnp.arange(capacity, dtype=F32)[None, :, None]) & live
        hotb = hot.astype(BF16)
        weight = jnp.sum(jnp.where(hot, prob_e[:, None, :], 0.0), axis=-1).reshape(-1, 1)
        rows = dot32("sct,std->scd", hotb, h2_all).astype(BF16).reshape(-1, width)
        dm_rows = dot32("sct,std->scd", hotb, dm_all).astype(BF16).reshape(-1, width)
        ga = jnp.dot(rows, wg, preferred_element_type=F32)
        ua = jnp.dot(rows, wu, preferred_element_type=F32)
        sig = jax.nn.sigmoid(ga)
        silu = ga * sig
        m = silu * ua
        mg = (m * weight).astype(BF16)
        y_rows = jnp.dot(mg, wd, preferred_element_type=F32).astype(BF16)
        u = dot32("nd,fd->nf", dm_rows, wd)
        dg = jnp.sum(m * u, axis=-1)
        dmh = u * weight
        da = (dmh * ua * sig * (1.0 + ga * (1.0 - sig))).astype(BF16)
        du = (dmh * silu).astype(BF16)
        gate_list.append(dot32("nd,nf->df", rows, da).astype(BF16))
        up_list.append(dot32("nd,nf->df", rows, du).astype(BF16))
        down_list.append(dot32("nf,nd->fd", mg, dm_rows).astype(BF16))
        dr_rows = (dot32("nf,df->nd", da, wg) + dot32("nf,df->nd", du, wu)).astype(BF16)
        shape = (sources, capacity, width)
        y_part = y_part + dot32("sct,scd->std", hotb, y_rows.reshape(shape))
        dr_part = dr_part + dot32("sct,scd->std", hotb, dr_rows.reshape(shape))
        back = jnp.sum(jnp.where(hot, dg.reshape(sources, capacity, 1), 0.0), axis=1)
        dg_part = dg_part + back[:, :, None] * (
            jnp.arange(experts, dtype=jnp.int32) == column
        ).astype(F32)
    dr_sum = lax.psum_scatter(
        dr_part.astype(BF16).reshape(-1, width), GROUP, scatter_dimension=0, tiled=True
    ).astype(F32)
    dg = lax.psum_scatter(dg_part.reshape(-1, experts), GROUP, scatter_dimension=0, tiled=True)
    y_sum = lax.psum_scatter(
        y_part.astype(BF16).reshape(-1, width), GROUP, scatter_dimension=0, tiled=True
    ).astype(F32)
    outputs = (middle + y_sum).astype(BF16)

    dp = Q * R
    share_d, share_f = width // dp, ffn // dp

    def spread(parts, rows):
        stack = jnp.stack(parts).reshape(count, dp, rows, -1)
        stack = jnp.transpose(stack, (1, 0, 2, 3))
        got = lax.all_to_all(stack, DP, split_axis=0, concat_axis=0, tiled=True)
        got = jnp.sum(got.reshape((Q, R) + got.shape[1:]).astype(F32), axis=0)
        keep = []
        for place in range(R):
            lo = (place * local + R // 2) // R
            hi = ((place + 1) * local + R // 2) // R
            keep.append(got[place, : hi - lo])
        return jnp.concatenate(keep, axis=0)

    gate_share = spread(gate_list, share_d)
    up_share = spread(up_list, share_d)
    down_share = spread(down_list, share_f)

    inner = jnp.sum(probs * dg, axis=-1, keepdims=True)
    dz = (probs * (dg - inner)).astype(BF16)
    grad_router = dot32("td,te->de", h2, dz)
    dh2 = dr_sum + dot32("te,de->td", dz, router_full)
    add, grad_moe_gain = norm_back(dh2, unit_moe, scale_moe, moe_gain)
    dx1 = cotangent.astype(F32) + add
    dat = dx1.astype(BF16)
    dat_all = lax.all_gather(dat, "expert", axis=0, tiled=True)
    do_own = dot32("td,cd->tc", dat, out_full).astype(BF16)
    do = lax.all_to_all(do_own, "expert", split_axis=1, concat_axis=0, tiled=True)
    grad_out = dot32("tc,td->cd", mixed, dat_all)
    dqkv = attention_backward(query, key, value, do, log_total, cosine, sine, segments)
    grad_qkv = dot32("tc,tq->cq", h1_all, dqkv)
    dh1 = lax.psum_scatter(
        dot32("tq,cq->tc", dqkv, w_qkv).astype(BF16), "expert", scatter_dimension=0, tiled=True
    ).astype(F32)
    _, unit_attn, scale_attn = norm_parts(inputs, attn_gain)
    add, grad_attn_gain = norm_back(dh1, unit_attn, scale_attn, attn_gain)
    grad_tokens = dx1 + add

    qkv_sum = lax.psum_scatter(grad_qkv.astype(BF16), DP, scatter_dimension=0, tiled=True)
    qkv_own = lax.all_to_all(
        qkv_sum.reshape(E, shard_rows, -1), "expert", split_axis=0, concat_axis=0, tiled=True
    )
    qkv_own = jnp.transpose(qkv_own, (1, 0, 2)).astype(F32)
    grad_query = qkv_own[:, :, :q_cols].reshape(shard_rows, -1)
    grad_key = qkv_own[:, :, q_cols : q_cols + k_cols].reshape(shard_rows, -1)
    grad_value = qkv_own[:, :, q_cols + k_cols :].reshape(shard_rows, -1)
    out_sum = lax.psum_scatter(grad_out.astype(BF16), DP, scatter_dimension=0, tiled=True)
    perm = [(p * E + x, dp * x + p) for p in range(dp) for x in range(E)]
    out_own = lax.ppermute(out_sum, ALL, perm).astype(F32)
    small_grad = jnp.concatenate(
        [grad_router, grad_attn_gain[:, None], grad_moe_gain[:, None]], axis=1
    )
    small_own = lax.psum_scatter(small_grad, ALL, scatter_dimension=0, tiled=True)
    return (
        outputs,
        grad_tokens,
        grad_query,
        grad_key,
        grad_value,
        out_own,
        small_own[:, :experts],
        small_own[:, experts],
        small_own[:, experts + 1],
        gate_share,
        up_share,
        down_share,
    )


def solution(mesh):
    dp, ex = mesh.devices.shape
    fine = Mesh(mesh.devices.reshape(dp // QUAD, QUAD, ex), ALL)
    row, flat = P(ALL, None), P(ALL)
    bank = P("expert", None, None)
    spread = P("expert", DP, None)
    return jax.shard_map(
        shards,
        mesh=fine,
        in_specs=(row,) * 6 + (flat,) * 2 + (bank,) * 3 + (P(DP),) + (row,) * 3,
        out_specs=(row,) * 7 + (flat,) * 2 + (spread,) * 3,
        check_vma=False,
    )
```

```python
import functools

import jax
import jax.numpy as jnp
from jax import lax
from jax.experimental import pallas as pl
from jax.experimental.pallas import tpu as pltpu
from jax.sharding import Mesh
from jax.sharding import PartitionSpec as P

HD = 64
QUAD = 4
F32 = jnp.float32
BF16 = jnp.bfloat16

epsilon = 1e-06
rope_base = 10000.0
masked_score = -1e30


def dot32(spec, a, b):
    return jnp.einsum(spec, a, b, preferred_element_type=F32)


def norm_parts(values, gain_row):
    scaling = lax.rsqrt(jnp.mean(values * values, axis=-1, keepdims=True) + epsilon)
    normed = values * scaling
    return (normed * gain_row, normed, scaling)


def norm_back(grad_rows, normed, scaling, gain_row):
    grad_normed = grad_rows * gain_row
    grad_gain = jnp.sum(grad_rows * normed, axis=0)
    inner_sum = jnp.mean(grad_normed * normed, axis=-1, keepdims=True)
    return (scaling * (grad_normed - normed * inner_sum), grad_gain)


def rope_tables(positions, head_size):
    frequency = rope_base ** (-2.0 * jnp.arange(head_size // 2, dtype=F32) / head_size)
    angles = positions.astype(F32)[:, None] * frequency[None, :]
    return (jnp.cos(angles), jnp.sin(angles))


def slot_dense(routes, priority, experts, capacity):
    rows, top_count = routes.shape
    hot = routes[:, :, None] == jnp.arange(experts, dtype=jnp.int32)
    rank = jnp.sum(jnp.where(hot, priority[:, :, None] + 1, 0), axis=1) - 1
    per_rank = rank[None] == jnp.arange(top_count, dtype=jnp.int32)[:, None, None]
    flat = jnp.transpose(per_rank.astype(BF16), (1, 0, 2)).reshape(rows, top_count * experts)
    index = jnp.arange(rows, dtype=jnp.int32)
    before = (index[None, :] < index[:, None]).astype(BF16)
    within = jnp.dot(before, flat, preferred_element_type=F32).reshape(rows, top_count, experts)
    totals = jnp.sum(per_rank.astype(F32), axis=1)
    base = jnp.cumsum(totals, axis=0) - totals
    slot = jnp.sum(
        jnp.where(jnp.transpose(per_rank, (1, 0, 2)), within + base[None], 0.0), axis=1
    )
    named = rank >= 0
    return named, jnp.where(named & (slot < capacity), slot, -1.0)


NT=(((1,),(1,)),((),()))
NN=(((1,),(0,)),((),()))
TN=(((0,),(0,)),((),()))

def mm(a,b,dims=NN):
    return lax.dot_general(a,b,dims,preferred_element_type=F32)

def swap_halves(x):
    lane=lax.broadcasted_iota(jnp.int32,(x.shape[0],128),1)
    low=(lane%HD)<HD//2
    parts=[]
    for c in range(x.shape[1]//128):
        g=x[:,c*128:(c+1)*128]
        parts.append(jnp.where(low,pltpu.roll(g,128-HD//2,1),pltpu.roll(g,HD//2,1)))
    return jnp.concatenate(parts,axis=1)

def bias_block(seg_row, keys, first):
    n=seg_row.shape[1]
    s=lax.broadcasted_iota(jnp.int32,(keys,n),0)
    t=lax.broadcasted_iota(jnp.int32,(keys,n),1)+first
    return jnp.where((s<=t)&(s>=seg_row),0.0,masked_score)

def forward_kernel(heads, kv_heads, block, x_ref, gain_ref, w_ref, cos_ref, sin_ref, seg_ref,
                   h1_ref, q_ref, k_ref, v_ref, o_ref, lse_ref, vt_ref):
    length=x_ref.shape[0]
    group=heads//kv_heads
    nq=heads*HD; nk=kv_heads*HD
    for i in range(length//block):
        rows=pl.ds(i*block,block)
        x=x_ref[rows,:].astype(F32)
        r=lax.rsqrt(jnp.mean(x*x,axis=1,keepdims=True)+epsilon)
        h1=(x*r*gain_ref[...]).astype(BF16)
        h1_ref[rows,:]=h1
        qkv=mm(h1,w_ref[...])
        qk=qkv[:,:nq+nk]
        c=jnp.concatenate([cos_ref[rows,:]]*((nq+nk)//128),axis=1)
        s=jnp.concatenate([sin_ref[rows,:]]*((nq+nk)//128),axis=1)
        qk=(qk*c+swap_halves(qk)*s).astype(BF16)
        v=qkv[:,nq+nk:].astype(BF16)
        for h in range(heads):
            q_ref[h,rows,:]=qk[:,h*HD:(h+1)*HD]
        vt=v.astype(F32).T.astype(BF16)
        for h in range(kv_heads):
            k_ref[h,rows,:]=qk[:,nq+h*HD:nq+(h+1)*HD]
            v_ref[h,rows,:]=v[:,h*HD:(h+1)*HD]
            vt_ref[h,:,rows]=vt[h*HD:(h+1)*HD,:]
        keys=(i+1)*block
        bias=bias_block(seg_ref[:,rows],keys,i*block)
        outs=[]
        for h in range(heads):
            g=h//group
            st=mm(k_ref[g,pl.ds(0,keys),:],q_ref[h,rows,:]*BF16(HD**-0.5),NT)+bias
            top=jnp.max(st,axis=0,keepdims=True)
            p=jnp.exp(st-top)
            total=jnp.sum(p,axis=0,keepdims=True)
            ot=mm(vt_ref[g,:,pl.ds(0,keys)],p.astype(BF16))
            outs.append(ot/total)
            lse_ref[pl.ds(h,1),rows]=top+jnp.log(total)
        o_ref[rows,:]=jnp.concatenate(outs,axis=0).T.astype(BF16)

def attention_forward(x_all,gain,w_qkv,cosine,sine,segments,heads,kv_heads,block=256):
    length,width=x_all.shape
    V=pl.BlockSpec(memory_space=pltpu.VMEM)
    nq=heads*HD
    pad=-(-heads//8)*8
    return pl.pallas_call(functools.partial(forward_kernel,heads,kv_heads,block),
        out_shape=(jax.ShapeDtypeStruct((length,width),BF16),
          jax.ShapeDtypeStruct((heads,length,HD),BF16),jax.ShapeDtypeStruct((kv_heads,length,HD),BF16),
          jax.ShapeDtypeStruct((kv_heads,length,HD),BF16),jax.ShapeDtypeStruct((length,nq),BF16),
          jax.ShapeDtypeStruct((pad,length),F32)),
        in_specs=[V]*6,out_specs=(V,)*6,
        scratch_shapes=[pltpu.VMEM((kv_heads,HD,length),BF16)],
        compiler_params=pltpu.CompilerParams(vmem_limit_bytes=56<<20),
        cost_estimate=pl.CostEstimate(flops=2*length*width*w_qkv.shape[1]+2*heads*length*length*256,bytes_accessed=14<<20,transcendentals=heads*length*length//2),
        name="attention_forward")(x_all,gain.reshape(1,-1),w_qkv,cosine,sine,segments.reshape(1,-1))

def backward_kernel(heads, kv_heads, block, q_ref, k_ref, v_ref, do_ref, lse_ref, cos_ref, sin_ref, seg_ref,
                    dqkv_ref, kt_ref, dk_ref, dv_ref):
    length=q_ref.shape[1]
    group=heads//kv_heads
    nq=heads*HD; nk=kv_heads*HD
    factor=HD**-0.5
    dk_ref[...]=jnp.zeros_like(dk_ref)
    dv_ref[...]=jnp.zeros_like(dv_ref)
    for g in range(kv_heads):
        kt_ref[g]=k_ref[g].astype(F32).T.astype(BF16)
    for i in range(length//block):
        rows=pl.ds(i*block,block)
        keys=(i+1)*block
        span=pl.ds(0,keys)
        bias=bias_block(seg_ref[:,rows],keys,i*block)
        dqs=[]
        for h in range(heads):
            g=h//group
            q=q_ref[h,rows,:]
            do=do_ref[rows,h*HD:(h+1)*HD]
            st=mm(k_ref[g,span,:],q*BF16(factor),NT)+bias
            p=jnp.exp(st-lse_ref[pl.ds(h,1),rows])
            dpt=mm(v_ref[g,span,:],do,NT)
            inner=jnp.sum(p*dpt,axis=0,keepdims=True)
            ds=(p*(dpt-inner)).astype(BF16)
            dv_ref[g,span,:]+=mm(p.astype(BF16),do)
            dk_ref[g,span,:]+=mm(ds,q)
            dqs.append(mm(kt_ref[g,:,span],ds))
        dq=jnp.concatenate(dqs,axis=0).T*factor
        c=jnp.concatenate([cos_ref[rows,:]]*(nq//128),axis=1)
        s=jnp.concatenate([sin_ref[rows,:]]*(nq//128),axis=1)
        dqkv_ref[rows,:nq]=(dq*c-swap_halves(dq)*s).astype(BF16)
    dk=jnp.concatenate([dk_ref[g] for g in range(kv_heads)],axis=1)*factor
    c=jnp.concatenate([cos_ref[...]]*(nk//128),axis=1)
    s=jnp.concatenate([sin_ref[...]]*(nk//128),axis=1)
    dqkv_ref[:,nq:nq+nk]=(dk*c-swap_halves(dk)*s).astype(BF16)
    dqkv_ref[:,nq+nk:]=jnp.concatenate([dv_ref[g] for g in range(kv_heads)],axis=1).astype(BF16)

def attention_backward(q,k,v,do,lse,cosine,sine,segments,block=256):
    heads,length,_=q.shape; kv_heads=k.shape[0]
    V=pl.BlockSpec(memory_space=pltpu.VMEM)
    return pl.pallas_call(functools.partial(backward_kernel,heads,kv_heads,block),
        out_shape=jax.ShapeDtypeStruct((length,(heads+2*kv_heads)*HD),BF16),
        in_specs=[V]*8,out_specs=V,
        scratch_shapes=[pltpu.VMEM((kv_heads,HD,length),BF16),pltpu.VMEM((kv_heads,length,HD),F32),pltpu.VMEM((kv_heads,length,HD),F32)],
        compiler_params=pltpu.CompilerParams(vmem_limit_bytes=56<<20),
        cost_estimate=pl.CostEstimate(flops=5*heads*length*length*256,bytes_accessed=10<<20,transcendentals=heads*length*length//2),
        name="attention_backward")(q,k,v,do,lse,cosine,sine,segments.reshape(1,-1))


MESH=pl.DeviceIdType.MESH
CORE=1
ORDERS=((2,4,8),(4,8,2),(8,2,4))

def flip(value, mask):
    low, high = value % 2, value // 2
    if mask & 1:
        low = 1 - low
    if mask & 2:
        high = 1 - high
    return high * 2 + low

def group_device(mask):
    q, r, e = lax.axis_index("q"), lax.axis_index("r"), lax.axis_index("expert")
    return (q, flip(r, mask >> 2), flip(e, mask & 3))

def group_member(mask):
    return flip(lax.axis_index("r"), mask >> 2) * 4 + flip(lax.axis_index("expert"), mask & 3)

def greet(masks):
    barrier = pltpu.get_barrier_semaphore()
    for mask in masks:
        pl.semaphore_signal(barrier, inc=1, device_id=group_device(mask), device_id_type=MESH)
    pl.semaphore_wait(barrier, len(masks))

def last_hop(part, mask):
    if mask & CORE:
        return CORE
    return [bit for bit in ORDERS[part] if mask & bit][-1]

def gather_order():
    free = {2: 0.0, 4: 0.0, 8: 0.0}
    arrived, todo = {(p, 0): 0.0 for p in range(3)}, [(p, m) for p in range(3) for m in range(2, 16, 2)]
    order = []
    while todo:
        best = None
        for p, m in todo:
            hop = last_hop(p, m)
            if (p, m ^ hop) in arrived:
                key = (max(free[hop], arrived[p, m ^ hop]), ORDERS[p].index(hop), p, m)
                if best is None or key < best:
                    best = key
        start, _, p, m = best
        hop = last_hop(p, m)
        free[hop] = start + 1
        arrived[p, m] = start + 1
        todo.remove((p, m))
        order.append((start + 1, p, m))
    return [(p, m) for _, p, m in sorted(order)]

def one_hot(table, capacity, slots):
    place = lax.broadcasted_iota(jnp.int32, (capacity, table.shape[1]), 0).astype(F32)
    return [table[k:k + 1, :] == place for k in range(slots)]

def gather_kernel(slots, capacity, h2_ref, table_ref, dm_ref, rows_ref, dm_rows_ref, weight_ref, tables_ref,
                  held, arrived, dm_held, send, recv, table_send, table_recv, dm_sem):
    width = h2_ref.shape[1]
    part_width = width // 3
    greet(range(1, 16))
    tables = []
    for mask in range(1, 16):
        copy = pltpu.make_async_remote_copy(table_ref.at[group_member(mask)], arrived.at[mask],
            table_send.at[mask], table_recv.at[mask], device_id=group_device(mask), device_id_type=MESH)
        copy.start()
        tables.append(copy)
    arrived[0] = table_ref[group_member(0)]
    copies = {}
    for p in range(3):
        for mask in range(1, 16):
            hop = last_hop(p, mask)
            source = mask ^ hop
            src = h2_ref.at[:, pl.ds(p * part_width, part_width)] if source == 0 else held.at[p, source]
            copies[p, mask] = pltpu.make_async_remote_copy(src, held.at[p, mask], send.at[p, mask], recv.at[p, mask],
                device_id=group_device(hop), device_id_type=MESH)
    order = gather_order()
    for p, mask in order + [(p, CORE) for p in range(3)]:
        if mask ^ last_hop(p, mask) == 0:
            copies[p, mask].start()
    def dm_copy(mask):
        return pltpu.make_async_copy(dm_ref.at[group_member(mask)], dm_held.at[mask % 2], dm_sem.at[mask % 2])
    dm_copy(0).start()
    for copy in tables:
        copy.wait_recv()
    def hots(mask):
        return one_hot(arrived[mask], capacity, slots)
    def place(target, mask, hot, block, columns):
        got = mm(jnp.concatenate([h.astype(BF16) for h in hot], axis=0), block).astype(BF16)
        for k in range(slots):
            target[k, pl.ds(mask * capacity, capacity), columns] = got[k * capacity:(k + 1) * capacity]
    def dm_step(mask):
        if mask + 1 < 16:
            dm_copy(mask + 1).start()
        dm_copy(mask).wait()
        hot = hots(mask)
        place(dm_rows_ref, mask, hot, dm_held[mask % 2], slice(None))
        if mask == 0:
            place(rows_ref, 0, hot, h2_ref[...], slice(None))
        table = arrived[mask]
        for k in range(slots):
            weight_ref[k, pl.ds(mask * capacity, capacity), :] = jnp.sum(
                jnp.where(hot[k], table[4 + k:5 + k, :], 0.0), axis=1, keepdims=True)
        tables_ref[mask] = table
    todo = list(range(16))
    dm_step(todo.pop(0))
    dm_step(todo.pop(0))
    def arrive(p, mask):
        copies[p, mask].wait_recv()
        for nxt in range(1, 16):
            if nxt != mask and (nxt ^ last_hop(p, nxt)) == mask:
                copies[p, nxt].start()
        place(rows_ref, mask, hots(mask), held[p, mask], pl.ds(p * part_width, part_width))
    for step, (p, mask) in enumerate(order):
        arrive(p, mask)
        if todo:
            dm_step(todo.pop(0))
    for p in range(3):
        arrive(p, CORE)
    for p, mask in order:
        arrive(p, mask | CORE)
    for copy in tables:
        copy.wait_send()
    for key in copies:
        copies[key].wait_send()

def gather_rows(h2, table, dm_all, slots, capacity, collective_id):
    tokens, width = h2.shape
    V = pl.BlockSpec(memory_space=pltpu.VMEM)
    rows = jax.ShapeDtypeStruct((slots, 16 * capacity, width), BF16)
    return pl.pallas_call(functools.partial(gather_kernel, slots, capacity),
        out_shape=(rows, rows, jax.ShapeDtypeStruct((slots, 16 * capacity, 1), F32), jax.ShapeDtypeStruct(table.shape, F32)),
        in_specs=[V, V, pl.BlockSpec(memory_space=pl.ANY)], out_specs=(V,) * 4,
        scratch_shapes=[pltpu.VMEM((3, 16, tokens, width // 3), BF16), pltpu.VMEM(table.shape, F32),
            pltpu.VMEM((2, tokens, width), BF16), pltpu.SemaphoreType.DMA((3, 16)), pltpu.SemaphoreType.DMA((3, 16)),
            pltpu.SemaphoreType.DMA((16,)), pltpu.SemaphoreType.DMA((16,)), pltpu.SemaphoreType.DMA((2,))],
        compiler_params=pltpu.CompilerParams(vmem_limit_bytes=58 << 20, collective_id=collective_id, has_side_effects=True),
        cost_estimate=pl.CostEstimate(flops=4 * 16 * slots * capacity * tokens * width, bytes_accessed=60 << 20, transcendentals=0),
        name="gather_rows")(h2, table, dm_all)

def expert_kernel(chunks, dp, place_ref, x_ref, dm_ref, weight_ref, wg_ref, wu_ref, wd_ref,
                  y_ref, dr_ref, dg_ref, gu_ref, down_ref, xs, dms, mgs, das):
    i = pl.program_id(0)
    ff = wg_ref.shape[2]
    block = x_ref.shape[1]
    @pl.when(i < chunks)
    def _():
        x, dmr, w = x_ref[0], dm_ref[0], weight_ref[0]
        rows = pl.ds(pl.multiple_of(i * block, block), block)
        xs[rows, :] = x
        dms[rows, :] = dmr
        ga = mm(x, wg_ref[0])
        ua = mm(x, wu_ref[0])
        u = mm(dmr, wd_ref[0], NT)
        sig = 1.0 / (1.0 + jnp.exp(-ga))
        silu = ga * sig
        m = silu * ua
        mg = (m * w).astype(BF16)
        dg_ref[...] = jnp.sum(m * u, axis=1, keepdims=True)
        dmh = u * w
        da = (dmh * ua * (sig * (1.0 + ga * (1.0 - sig)))).astype(BF16)
        du = (dmh * silu).astype(BF16)
        mgs[rows, :] = mg
        das[rows, :ff] = da
        das[rows, ff:] = du
        y_ref[...] = mm(mg, wd_ref[0]).astype(BF16)
        dr_ref[...] = (mm(da, wg_ref[0], NT) + mm(du, wu_ref[0], NT)).astype(BF16)
    @pl.when(i == chunks)
    def _():
        share = gu_ref.shape[1] // 2
        for half in range(2):
            grad = mm(xs[...], das[:, half * ff:(half + 1) * ff], TN).astype(BF16)
            for d in range(dp):
                gu_ref[d, half * share:(half + 1) * share, :] = grad[d * share:(d + 1) * share]
        down_ref[...] = mm(mgs[...], dms[...], TN).astype(BF16)

def expert_call(rows, dm_rows, weight, slot, w_gate, w_up, w_down, place, dp, block=512):
    _, total, width = rows.shape
    ff = w_gate.shape[2]
    chunks = total // block
    row_spec = pl.BlockSpec((1, block, width), lambda i, s: (slot, jnp.minimum(i, chunks - 1), 0))
    out_row = pl.BlockSpec((block, width), lambda i, s: (jnp.minimum(i, chunks - 1), 0))
    bank = lambda a: pl.BlockSpec((1,) + a.shape[1:], lambda i, s: (s[0], 0, 0))
    share = width // dp
    return pl.pallas_call(functools.partial(expert_kernel, chunks, dp),
        grid_spec=pltpu.PrefetchScalarGridSpec(num_scalar_prefetch=1, grid=(chunks + 1,),
            in_specs=[row_spec, row_spec, pl.BlockSpec((1, block, 1), lambda i, s: (slot, jnp.minimum(i, chunks - 1), 0)),
                bank(w_gate), bank(w_up), bank(w_down)],
            out_specs=(out_row, out_row, pl.BlockSpec((block, 1), lambda i, s: (jnp.minimum(i, chunks - 1), 0)),
                pl.BlockSpec((dp, 2 * share, ff), lambda i, s: (0, 0, 0)), pl.BlockSpec((ff, width), lambda i, s: (0, 0))),
            scratch_shapes=[pltpu.VMEM((total, width), BF16), pltpu.VMEM((total, width), BF16),
                pltpu.VMEM((total, ff), BF16), pltpu.VMEM((total, 2 * ff), BF16)]),
        out_shape=(jax.ShapeDtypeStruct((total, width), BF16), jax.ShapeDtypeStruct((total, width), BF16),
            jax.ShapeDtypeStruct((total, 1), F32), jax.ShapeDtypeStruct((dp, 2 * share, ff), BF16),
            jax.ShapeDtypeStruct((ff, width), BF16)),
        compiler_params=pltpu.CompilerParams(vmem_limit_bytes=58 << 20, dimension_semantics=("arbitrary",)),
        cost_estimate=pl.CostEstimate(flops=18 * total * width * ff, bytes_accessed=24 << 20, transcendentals=total * ff),
        name="expert")(place.reshape(1), rows, dm_rows, weight, w_gate, w_up, w_down)

def first_hop(part, mask):
    return [bit for bit in ORDERS[part] if mask & bit][0]

def combine_kernel(slots, capacity, with_dg, *refs):
    rows = refs[:slots]
    refs = refs[slots:]
    tables_ref = refs[0]
    refs = refs[1:]
    if with_dg:
        dg_refs, refs = refs[:slots], refs[slots:]
        out_ref, dg_out = refs[:2]
        refs = refs[2:]
    else:
        out_ref, refs = refs[0], refs[1:]
    core_out, core_in, held, got, core_send, core_recv, send, recv = refs[:8]
    if with_dg:
        dg_hold, dg_in, dg_send, dg_recv = refs[8:]
    width = out_ref.shape[1]
    part_width = width // 3
    greet(range(1, 16) if with_dg else (1, 2, 4, 8))
    def hots(mask):
        return one_hot(tables_ref[mask], capacity, slots)
    def block_sum(mask, hot):
        return mm(jnp.concatenate([h.astype(BF16) for h in hot], axis=0),
            jnp.concatenate([rows[k][pl.ds(mask * capacity, capacity), :] for k in range(slots)], axis=0), TN)
    dg_copies = []
    def dg_step(mask, hot):
        if not with_dg:
            return
        for k in range(slots):
            col = dg_refs[k][pl.ds(mask * capacity, capacity), :]
            dg_hold[mask, k:k + 1, :] = jnp.sum(jnp.where(hot[k], col, 0.0), axis=0, keepdims=True)
        if mask == 0:
            return
        copy = pltpu.make_async_remote_copy(dg_hold.at[mask], dg_in.at[mask], dg_send.at[mask], dg_recv.at[mask],
            device_id=group_device(mask), device_id_type=MESH)
        copy.start()
        dg_copies.append(copy)
    listed = sorted(range(0, 16, 2), key=lambda m: (-bin(m).count("1"), m))
    if with_dg:
        dg_hold[...] = jnp.zeros_like(dg_hold)
    core = {}
    for mask in listed:
        hot = hots(mask | CORE)
        core_out[mask // 2] = block_sum(mask | CORE, hot).astype(BF16)
        core[mask] = pltpu.make_async_remote_copy(core_out.at[mask // 2], core_in.at[mask // 2], core_send.at[mask // 2],
            core_recv.at[mask // 2], device_id=group_device(CORE), device_id_type=MESH)
        core[mask].start()
        dg_step(mask | CORE, hot)
    copies = {}
    for p in range(3):
        for mask in range(2, 16, 2):
            copies[p, mask] = pltpu.make_async_remote_copy(held.at[p, mask // 2], got.at[p, mask // 2], send.at[p, mask // 2],
                recv.at[p, mask // 2], device_id=group_device(first_hop(p, mask)), device_id_type=MESH)
    for mask in listed:
        hot = hots(mask)
        own = block_sum(mask, hot)
        core[mask].wait_recv()
        own = (own + core_in[mask // 2].astype(F32)).astype(BF16)
        for p in range(3):
            held[p, mask // 2] = own[:, p * part_width:(p + 1) * part_width]
            if mask & ORDERS[p][0]:
                copies[p, mask].start()
        dg_step(mask, hot)
    def add(p, target, sources):
        total = held[p, target // 2].astype(F32)
        for source in sources:
            copies[p, source].wait_recv()
            total = total + got[p, source // 2].astype(F32)
        return total
    def forward(p, target, sources):
        held[p, target // 2] = add(p, target, sources).astype(BF16)
        copies[p, target].start()
    for both in (True, False):
        for p in range(3):
            a, b, c = ORDERS[p]
            target = b | c if both else b
            forward(p, target, [target | a])
    for p in range(3):
        a, b, c = ORDERS[p]
        forward(p, c, [c | a, c | b])
    for p in range(3):
        a, b, c = ORDERS[p]
        out_ref[:, p * part_width:(p + 1) * part_width] = add(p, 0, [a, b, c])
    if with_dg:
        dg_out[0] = dg_hold[0]
        for copy in dg_copies:
            copy.wait_recv()
        for mask in range(1, 16):
            dg_out[mask] = dg_in[mask]
        for copy in dg_copies:
            copy.wait_send()
    for mask in listed:
        core[mask].wait_send()
    for key in copies:
        copies[key].wait_send()

def combine_rows(rows, tables, dgs, capacity, collective_id):
    slots = len(rows)
    tokens, width = tables.shape[2], rows[0].shape[1]
    V = pl.BlockSpec(memory_space=pltpu.VMEM)
    with_dg = dgs is not None
    out = jax.ShapeDtypeStruct((tokens, width), F32)
    table = pltpu.VMEM(tables.shape, F32)
    sem = pltpu.SemaphoreType.DMA
    return pl.pallas_call(functools.partial(combine_kernel, slots, capacity, with_dg),
        out_shape=(out, jax.ShapeDtypeStruct(tables.shape, F32)) if with_dg else out,
        in_specs=[V] * (slots + 1 + (slots if with_dg else 0)), out_specs=(V, V) if with_dg else V,
        scratch_shapes=[pltpu.VMEM((8, tokens, width), BF16), pltpu.VMEM((8, tokens, width), BF16),
            pltpu.VMEM((3, 8, tokens, width // 3), BF16), pltpu.VMEM((3, 8, tokens, width // 3), BF16),
            sem((8,)), sem((8,)), sem((3, 8)), sem((3, 8))] + ([table, table, sem((16,)), sem((16,))] if with_dg else []),
        compiler_params=pltpu.CompilerParams(vmem_limit_bytes=58 << 20, collective_id=collective_id, has_side_effects=True),
        cost_estimate=pl.CostEstimate(flops=2 * 16 * slots * capacity * tokens * width, bytes_accessed=40 << 20, transcendentals=0),
        name="combine_with_dg" if with_dg else "combine_rows")(*rows, tables, *(dgs if with_dg else ()))


ALL = ("q", "r", "expert")
DP = ("q", "r")
GROUP = ("r", "expert")


def shards(
    tokens, w_query, w_key, w_value, w_out, w_router, gain_attn, gain_moe,
    w_gate, w_up, w_down, segments, routes, priority, cotangent,
):
    rows_here, width = tokens.shape
    E = lax.axis_size("expert")
    R = lax.axis_size("r")
    Q = lax.axis_size("q")
    e = lax.axis_index("expert")
    r = lax.axis_index("r")
    shard_rows = w_query.shape[0]
    local = w_gate.shape[0]
    experts = local * E
    ffn = w_gate.shape[2]
    capacity = rows_here * routes.shape[1] // experts
    length = rows_here * E
    sources = R * E
    q_cols = w_query.shape[1] // E
    k_cols = w_key.shape[1] // E
    pieces = jnp.concatenate(
        [w.reshape(shard_rows, E, -1) for w in (w_query, w_key, w_value)], axis=2
    )
    mine = lax.all_to_all(pieces, "expert", split_axis=1, concat_axis=0, tiled=True)
    mine = mine.reshape(shard_rows * E, -1)
    w_qkv = lax.all_gather(mine, DP, axis=0, tiled=True)
    x_all = lax.all_gather(tokens, "expert", axis=0, tiled=True)
    small = jnp.concatenate([w_router, gain_attn[:, None], gain_moe[:, None]], axis=1)
    small = lax.all_gather(small, ALL, axis=0, tiled=True)
    router_full = small[:, :experts]
    attn_gain = small[:, experts].astype(F32)
    moe_gain = small[:, experts + 1].astype(F32)
    out_full = lax.all_gather(w_out, ALL, axis=0, tiled=True)
    dm_all = lax.all_gather(cotangent, GROUP, axis=0, tiled=True).reshape(
        sources, rows_here, width
    )
    named, slots_dense = slot_dense(routes, priority, experts, capacity)

    pick_columns = None
    shared_banks = None
    if local % R:
        ways = R // (local % R)
        part = ffn // (Q * R * ways)
        at = jnp.arange(ffn // ways, dtype=jnp.int32)
        at = (at // part * ways)[None] * part + at % part + jnp.arange(ways, dtype=jnp.int32)[:, None] * part
        pick_columns = (jnp.arange(ffn, dtype=jnp.int32)[None, :, None] == at[:, None, :]).astype(BF16)
        mine = lax.dynamic_index_in_dim(pick_columns, r % ways, 0, False)
        place = (local // R) * R + r // ways
        shared = [lax.dynamic_index_in_dim(w, place, 0, False) for w in (w_gate, w_up, w_down)]
        shared_banks = (
            dot32("df,fc->dc", shared[0], mine).astype(BF16)[None],
            dot32("df,fc->dc", shared[1], mine).astype(BF16)[None],
            dot32("fd,fc->cd", shared[2], mine).astype(BF16)[None],
        )
    positions = jnp.arange(length, dtype=jnp.int32)
    cosine, sine = rope_tables(positions, HD)
    cosine = jnp.tile(cosine, (1, 4))
    sine = jnp.tile(jnp.concatenate([-sine, sine], axis=1), (1, 2))
    kv_heads = k_cols // HD
    h1_all, query, key, value, mixed, log_total = attention_forward(
        x_all, attn_gain, w_qkv, cosine, sine, segments, q_cols // HD, kv_heads
    )
    mixed_own = lax.all_to_all(mixed, "expert", split_axis=0, concat_axis=1, tiled=True)
    inputs = tokens.astype(F32)
    middle = inputs + jnp.dot(mixed_own, out_full, preferred_element_type=F32)
    h2, unit_moe, scale_moe = norm_parts(middle, moe_gain)
    h2 = h2.astype(BF16)
    logits = jnp.dot(h2, router_full, preferred_element_type=F32)
    probs = jax.nn.softmax(jnp.where(named, logits, masked_score), axis=-1)
    probs = jnp.where(named, probs, 0.0)
    dp = Q * R
    whole = local // R
    rest = local - whole * R
    ways = R // rest if rest else 1
    slots = whole + (1 if rest else 0)

    def by_device(table):
        table = table.T.reshape(E, local, rows_here)
        picks = [
            table[:, [r * whole + s for s in range(whole)] + ([R * whole + r // ways] if rest else [])]
            for r in range(R)
        ]
        return jnp.stack(picks).reshape(sources, slots, rows_here)

    table = jnp.concatenate(
        [
            by_device(slots_dense),
            jnp.zeros((sources, 4 - slots, rows_here), F32),
            by_device(probs),
            jnp.zeros((sources, 4 - slots, rows_here), F32),
        ],
        axis=1,
    )
    rows, dm_rows, weight, tables = gather_rows(h2, table, dm_all, slots, capacity, 1)
    y_rows, dr_rows, dg_rows, spread_in = [], [], [], []
    for s in range(slots):
        if s < whole:
            banks, place = (w_gate, w_up, w_down), r * whole + s
        else:
            banks, place = shared_banks, jnp.int32(0)
        y, dr, dg, grad_gu, grad_down = expert_call(
            rows, dm_rows, weight, s, *banks, place.astype(jnp.int32), dp
        )
        y_rows.append(y)
        dr_rows.append(dr)
        dg_rows.append(dg)
        spread_in.append((grad_gu, grad_down.reshape(dp, -1, width)))
    moved = [
        tuple(lax.all_to_all(a, DP, split_axis=0, concat_axis=0, tiled=True) for a in pair)
        for pair in spread_in
    ]
    dr_sum, dg_back = combine_rows(dr_rows, tables, dg_rows, capacity, 2)
    y_sum = combine_rows(y_rows, tables, None, capacity, 3)
    outputs = (middle + y_sum).astype(BF16)
    me = r * E + e
    dg_back = jnp.take(dg_back, me ^ jnp.arange(sources), axis=0)[:, :slots]
    dg_back = dg_back.reshape(R, E, slots, rows_here)
    pieces = [jnp.transpose(dg_back[:, :, :whole], (1, 0, 2, 3)).reshape(E, R * whole, rows_here)]
    if rest:
        pieces.append(
            jnp.transpose(jnp.sum(dg_back[:, :, whole].reshape(rest, ways, E, rows_here), axis=1), (1, 0, 2))
        )
    dg = jnp.concatenate(pieces, axis=1).reshape(experts, rows_here).T

    share_d, share_f = width // dp, ffn // dp
    sums = []
    for s in range(whole):
        gu, down = moved[s]
        sums.append(
            (
                jnp.sum(gu.reshape(Q, R, 2, share_d, ffn).astype(F32), axis=0),
                jnp.sum(down.reshape(Q, R, share_f, width).astype(F32), axis=0),
            )
        )
    gate_share = jnp.stack([a[:, 0] for a, _ in sums], axis=1).reshape(-1, share_d, ffn)
    up_share = jnp.stack([a[:, 1] for a, _ in sums], axis=1).reshape(-1, share_d, ffn)
    down_share = jnp.stack([a for _, a in sums], axis=1).reshape(-1, share_f, width)
    if rest:
        gu, down = moved[whole]
        gu = gu.reshape(Q, rest, ways, 2, share_d, ffn // ways)
        gu = dot32("qxhgdc,hfc->xgdf", gu, pick_columns)
        gate_share = jnp.concatenate([gate_share, gu[:, 0]], axis=0)
        up_share = jnp.concatenate([up_share, gu[:, 1]], axis=0)
        down = jnp.sum(down.reshape(Q, rest, share_f, width).astype(F32), axis=0)
        down_share = jnp.concatenate([down_share, down], axis=0)

    inner = jnp.sum(probs * dg, axis=-1, keepdims=True)
    dz = (probs * (dg - inner)).astype(BF16)
    grad_router = dot32("td,te->de", h2, dz)
    dh2 = dr_sum + dot32("te,de->td", dz, router_full)
    add, grad_moe_gain = norm_back(dh2, unit_moe, scale_moe, moe_gain)
    dx1 = cotangent.astype(F32) + add
    dat = dx1.astype(BF16)
    dat_all = lax.all_gather(dat, "expert", axis=0, tiled=True)
    do_own = dot32("td,cd->tc", dat, out_full).astype(BF16)
    do = lax.all_to_all(do_own, "expert", split_axis=1, concat_axis=0, tiled=True)
    grad_out = dot32("tc,td->cd", mixed, dat_all)
    dqkv = attention_backward(query, key, value, do, log_total, cosine, sine, segments)
    grad_qkv = dot32("tc,tq->cq", h1_all, dqkv)
    dh1_part = dot32("tq,cq->tc", dqkv, w_qkv)
    unit_all = norm_parts(x_all.astype(F32), attn_gain)[1]
    grad_attn_gain = jnp.sum(dh1_part * unit_all, axis=0)
    dh1 = lax.psum_scatter(
        dh1_part.astype(BF16), "expert", scatter_dimension=0, tiled=True
    ).astype(F32)
    _, unit_attn, scale_attn = norm_parts(inputs, attn_gain)
    add, _ = norm_back(dh1, unit_attn, scale_attn, attn_gain)
    grad_tokens = dx1 + add

    small_grad = jnp.concatenate(
        [grad_router, grad_attn_gain[:, None], grad_moe_gain[:, None]], axis=1
    )
    small_grad = jnp.pad(small_grad, ((0, 0), (0, 128 - small_grad.shape[1])))
    grad_all = jnp.concatenate([grad_qkv, small_grad], axis=1).astype(BF16)
    qkv_sum = lax.psum_scatter(grad_all, DP, scatter_dimension=0, tiled=True)
    qkv_own = lax.all_to_all(
        qkv_sum.reshape(E, shard_rows, -1), "expert", split_axis=0, concat_axis=0, tiled=True
    )
    qkv_own = jnp.transpose(qkv_own, (1, 0, 2)).astype(F32)
    small_own = jnp.sum(qkv_own[:, :, q_cols + 2 * k_cols :], axis=1)
    grad_query = qkv_own[:, :, :q_cols].reshape(shard_rows, -1)
    grad_key = qkv_own[:, :, q_cols : q_cols + k_cols].reshape(shard_rows, -1)
    grad_value = qkv_own[:, :, q_cols + k_cols : q_cols + 2 * k_cols].reshape(shard_rows, -1)
    out_sum = lax.psum_scatter(grad_out.astype(BF16), DP, scatter_dimension=0, tiled=True)
    perm = [(p * E + x, dp * x + p) for p in range(dp) for x in range(E)]
    out_own = lax.ppermute(out_sum, ALL, perm).astype(F32)
    return (
        outputs,
        grad_tokens,
        grad_query,
        grad_key,
        grad_value,
        out_own,
        small_own[:, :experts],
        small_own[:, experts],
        small_own[:, experts + 1],
        gate_share,
        up_share,
        down_share,
    )


def solution(mesh):
    dp, ex = mesh.devices.shape
    fine = Mesh(mesh.devices.reshape(dp // QUAD, QUAD, ex), ALL)
    row, flat = P(ALL, None), P(ALL)
    bank = P("expert", None, None)
    spread = P("expert", DP, None)
    return jax.shard_map(
        shards,
        mesh=fine,
        in_specs=(row,) * 6 + (flat,) * 2 + (bank,) * 3 + (P(DP),) + (row,) * 3,
        out_specs=(row,) * 7 + (flat,) * 2 + (spread,) * 3,
        check_vma=False,
    )
```

```python
import functools

import jax
import jax.numpy as jnp
from jax import lax
from jax.experimental import pallas as pl
from jax.experimental.pallas import tpu as pltpu
from jax.sharding import Mesh
from jax.sharding import PartitionSpec as P

HD = 64
QUAD = 4
F32 = jnp.float32
BF16 = jnp.bfloat16

CHEAP = pl.CostEstimate(flops=1 << 20, bytes_accessed=1 << 16, transcendentals=0)

epsilon = 1e-06
rope_base = 10000.0
masked_score = -1e30


def dot32(spec, a, b):
    return jnp.einsum(spec, a, b, preferred_element_type=F32)


def norm_parts(values, gain_row):
    scaling = lax.rsqrt(jnp.mean(values * values, axis=-1, keepdims=True) + epsilon)
    normed = values * scaling
    return (normed * gain_row, normed, scaling)


def norm_back(grad_rows, normed, scaling, gain_row):
    grad_normed = grad_rows * gain_row
    grad_gain = jnp.sum(grad_rows * normed, axis=0)
    inner_sum = jnp.mean(grad_normed * normed, axis=-1, keepdims=True)
    return (scaling * (grad_normed - normed * inner_sum), grad_gain)


def rope_tables(positions, head_size):
    frequency = rope_base ** (-2.0 * jnp.arange(head_size // 2, dtype=F32) / head_size)
    angles = positions.astype(F32)[:, None] * frequency[None, :]
    return (jnp.cos(angles), jnp.sin(angles))


def slot_dense(routes, priority, experts, capacity):
    rows, top_count = routes.shape
    hot = routes[:, :, None] == jnp.arange(experts, dtype=jnp.int32)
    rank = jnp.sum(jnp.where(hot, priority[:, :, None] + 1, 0), axis=1) - 1
    per_rank = rank[None] == jnp.arange(top_count, dtype=jnp.int32)[:, None, None]
    flat = jnp.transpose(per_rank.astype(BF16), (1, 0, 2)).reshape(rows, top_count * experts)
    index = jnp.arange(rows, dtype=jnp.int32)
    before = (index[None, :] < index[:, None]).astype(BF16)
    within = jnp.dot(before, flat, preferred_element_type=F32).reshape(rows, top_count, experts)
    totals = jnp.sum(per_rank.astype(F32), axis=1)
    base = jnp.cumsum(totals, axis=0) - totals
    slot = jnp.sum(
        jnp.where(jnp.transpose(per_rank, (1, 0, 2)), within + base[None], 0.0), axis=1
    )
    named = rank >= 0
    return named, jnp.where(named & (slot < capacity), slot, -1.0)


NT=(((1,),(1,)),((),()))
NN=(((1,),(0,)),((),()))
TN=(((0,),(0,)),((),()))

def mm(a,b,dims=NN):
    return lax.dot_general(a,b,dims,preferred_element_type=F32)

def swap_halves(x):
    lane=lax.broadcasted_iota(jnp.int32,(x.shape[0],128),1)
    low=(lane%HD)<HD//2
    parts=[]
    for c in range(x.shape[1]//128):
        g=x[:,c*128:(c+1)*128]
        parts.append(jnp.where(low,pltpu.roll(g,128-HD//2,1),pltpu.roll(g,HD//2,1)))
    return jnp.concatenate(parts,axis=1)

def bias_block(seg_row, keys, first):
    n=seg_row.shape[1]
    s=lax.broadcasted_iota(jnp.int32,(keys,n),0)
    t=lax.broadcasted_iota(jnp.int32,(keys,n),1)+first
    return jnp.where((s<=t)&(s>=seg_row),0.0,masked_score)

MESH=pl.DeviceIdType.MESH
CORE = 1
GATHER_ORDERS = ((2, 4, 8), (4, 8, 2), (8, 2, 4))
SUM_ORDERS = ((4, 2, 8), (2, 4, 8))

def member_r():
    return lax.axis_index("rh") * 2 + lax.axis_index("rl")

def device_at(q, r, e):
    return (q, r // 2, r % 2, e)

def place_at(q, r):
    return q * QUAD + r

def flip(value, mask):
    low, high = value % 2, value // 2
    if mask & 1:
        low = 1 - low
    if mask & 2:
        high = 1 - high
    return high * 2 + low

def group_device(mask):
    return device_at(lax.axis_index("q"), flip(member_r(), mask >> 2), flip(lax.axis_index("expert"), mask & 3))

def group_member(mask):
    return flip(member_r(), mask >> 2) * 4 + flip(lax.axis_index("expert"), mask & 3)

def greet(masks):
    barrier = pltpu.get_barrier_semaphore()
    for mask in masks:
        pl.semaphore_signal(barrier, inc=1, device_id=group_device(mask), device_id_type=MESH)
    pl.semaphore_wait(barrier, len(masks))

def last_hop(part, mask):
    if mask & CORE:
        return CORE
    return [bit for bit in GATHER_ORDERS[part] if mask & bit][-1]

def gather_order():
    free = {2: 0.0, 4: 0.0, 8: 0.0}
    arrived, todo = {(p, 0): 0.0 for p in range(len(GATHER_ORDERS))}, [(p, m) for p in range(len(GATHER_ORDERS)) for m in range(2, 16, 2)]
    order = []
    while todo:
        best = None
        for p, m in todo:
            hop = last_hop(p, m)
            if (p, m ^ hop) in arrived:
                key = (max(free[hop], arrived[p, m ^ hop]), GATHER_ORDERS[p].index(hop), p, m)
                if best is None or key < best:
                    best = key
        start, _, p, m = best
        hop = last_hop(p, m)
        free[hop] = start + 1
        arrived[p, m] = start + 1
        todo.remove((p, m))
        order.append((start + 1, p, m))
    return [(p, m) for _, p, m in sorted(order)]

def one_hot(table, capacity, slots):
    place = lax.broadcasted_iota(jnp.int32, (capacity, table.shape[1]), 0).astype(F32)
    return [table[k:k + 1, :] == place for k in range(slots)]

def gather_kernel(slots, capacity, h2_ref, table_ref, dm_ref, rows_ref, dm_rows_ref, weight_ref, tables_ref,
                  held, arrived, dm_held, send, recv, table_send, table_recv, dm_sem):
    width = h2_ref.shape[1]
    part_width = width // len(GATHER_ORDERS)
    greet(range(1, 16))
    tables = []
    for mask in range(1, 16):
        copy = pltpu.make_async_remote_copy(table_ref.at[group_member(mask)], arrived.at[mask],
            table_send.at[mask], table_recv.at[mask], device_id=group_device(mask), device_id_type=MESH)
        copy.start()
        tables.append(copy)
    arrived[0] = table_ref[group_member(0)]
    copies = {}
    for p in range(len(GATHER_ORDERS)):
        for mask in range(1, 16):
            hop = last_hop(p, mask)
            source = mask ^ hop
            src = h2_ref.at[:, pl.ds(p * part_width, part_width)] if source == 0 else held.at[p, source]
            copies[p, mask] = pltpu.make_async_remote_copy(src, held.at[p, mask], send.at[p, mask], recv.at[p, mask],
                device_id=group_device(hop), device_id_type=MESH)
    order = gather_order()
    for p, mask in order + [(p, CORE) for p in range(len(GATHER_ORDERS))]:
        if mask ^ last_hop(p, mask) == 0:
            copies[p, mask].start()
    def dm_copy(mask):
        return pltpu.make_async_copy(dm_ref.at[group_member(mask)], dm_held.at[mask % 2], dm_sem.at[mask % 2])
    dm_copy(0).start()
    for copy in tables:
        copy.wait_recv()
    def hots(mask):
        return one_hot(arrived[mask], capacity, slots)
    def place(target, mask, hot, block, columns):
        got = mm(jnp.concatenate([h.astype(BF16) for h in hot], axis=0), block).astype(BF16)
        for k in range(slots):
            target[k, pl.ds(mask * capacity, capacity), columns] = got[k * capacity:(k + 1) * capacity]
    def dm_step(mask):
        if mask + 1 < 16:
            dm_copy(mask + 1).start()
        dm_copy(mask).wait()
        hot = hots(mask)
        place(dm_rows_ref, mask, hot, dm_held[mask % 2], slice(None))
        if mask == 0:
            place(rows_ref, 0, hot, h2_ref[...], slice(None))
        table = arrived[mask]
        for k in range(slots):
            weight_ref[k, pl.ds(mask * capacity, capacity), :] = jnp.sum(
                jnp.where(hot[k], table[4 + k:5 + k, :], 0.0), axis=1, keepdims=True)
        tables_ref[mask] = table
    todo = list(range(16))
    dm_step(todo.pop(0))
    dm_step(todo.pop(0))
    def arrive(p, mask):
        copies[p, mask].wait_recv()
        for nxt in range(1, 16):
            if nxt != mask and (nxt ^ last_hop(p, nxt)) == mask:
                copies[p, nxt].start()
        place(rows_ref, mask, hots(mask), held[p, mask], pl.ds(p * part_width, part_width))
    for step, (p, mask) in enumerate(order):
        arrive(p, mask)
        if todo:
            dm_step(todo.pop(0))
    for p in range(len(GATHER_ORDERS)):
        arrive(p, CORE)
    for p, mask in order:
        arrive(p, mask | CORE)
    for copy in tables:
        copy.wait_send()
    for key in copies:
        copies[key].wait_send()

def gather_rows(h2, table, dm_all, slots, capacity, collective_id):
    tokens, width = h2.shape
    V = pl.BlockSpec(memory_space=pltpu.VMEM)
    rows = jax.ShapeDtypeStruct((slots, 16 * capacity, width), BF16)
    return pl.pallas_call(functools.partial(gather_kernel, slots, capacity),
        out_shape=(rows, rows, jax.ShapeDtypeStruct((slots, 16 * capacity, 1), F32), jax.ShapeDtypeStruct(table.shape, F32)),
        in_specs=[V, V, pl.BlockSpec(memory_space=pl.ANY)], out_specs=(V,) * 4,
        scratch_shapes=[pltpu.VMEM((len(GATHER_ORDERS), 16, tokens, width // len(GATHER_ORDERS)), BF16), pltpu.VMEM(table.shape, F32),
            pltpu.VMEM((2, tokens, width), BF16), pltpu.SemaphoreType.DMA((len(GATHER_ORDERS), 16)), pltpu.SemaphoreType.DMA((len(GATHER_ORDERS), 16)),
            pltpu.SemaphoreType.DMA((16,)), pltpu.SemaphoreType.DMA((16,)), pltpu.SemaphoreType.DMA((2,))],
        compiler_params=pltpu.CompilerParams(vmem_limit_bytes=58 << 20, collective_id=collective_id, has_side_effects=True),
        cost_estimate=CHEAP,
        name="gather_rows")(h2, table, dm_all)

def expert_kernel(chunks, dp, ways, s_ref, x_ref, dm_ref, weight_ref, wg_ref, wu_ref, wd_ref,
                  y_ref, dr_ref, dg_ref, grads, xs, dms, mgs, das, *banks):
    i = pl.program_id(1)
    block = x_ref.shape[1]
    if ways > 1:
        wg, wu, wd = banks
        ff = wg.shape[1]
        part = ff // dp
        @pl.when(i == 0)
        def _():
            shape = (ff * ways, ff)
            row, col = lax.broadcasted_iota(jnp.int32, shape, 0), lax.broadcasted_iota(jnp.int32, shape, 1)
            pick = (row == (col // part * ways + s_ref[s_ref.shape[0] - 1]) * part + col % part).astype(F32).astype(BF16)
            wg[...] = mm(wg_ref[0], pick).astype(BF16)
            wu[...] = mm(wu_ref[0], pick).astype(BF16)
            wd[...] = mm(pick, wd_ref[0], TN).astype(BF16)
    else:
        wg, wu, wd = wg_ref.at[0], wu_ref.at[0], wd_ref.at[0]
        ff = wg.shape[1]
    @pl.when(i < chunks)
    def _():
        x, dmr, w = x_ref[0], dm_ref[0], weight_ref[0]
        rows = pl.ds(pl.multiple_of(i * block, block), block)
        xs[rows, :] = x
        dms[rows, :] = dmr
        ga = mm(x, wg[...])
        ua = mm(x, wu[...])
        u = mm(dmr, wd[...], NT)
        sig = 1.0 / (1.0 + jnp.exp(-ga))
        silu = ga * sig
        m = silu * ua
        mg = (m * w).astype(BF16)
        dg_ref[0] = jnp.sum(m * u, axis=1, keepdims=True)
        dmh = u * w
        da = (dmh * ua * (sig * (1.0 + ga * (1.0 - sig)))).astype(BF16)
        du = (dmh * silu).astype(BF16)
        mgs[rows, :] = mg
        das[rows, :ff] = da
        das[rows, ff:] = du
        y_ref[0] = mm(mg, wd[...]).astype(BF16)
        dr_ref[0] = (mm(da, wg[...], NT) + mm(du, wu[...], NT)).astype(BF16)
    @pl.when(i == chunks)
    def _():
        width = xs.shape[1]
        share, down_share = width // dp, ff // dp
        for half in range(2):
            grad = mm(xs[...], das[:, half * ff:(half + 1) * ff], TN).astype(BF16)
            for d in range(dp):
                grads[d, 0, half * share:(half + 1) * share, :] = grad[d * share:(d + 1) * share]
        down = mm(mgs[...], dms[...], TN).astype(BF16)
        for d in range(dp):
            for c in range(width // ff):
                first = 2 * share + c * down_share
                grads[d, 0, first:first + down_share, :] = down[d * down_share:(d + 1) * down_share, c * ff:(c + 1) * ff]

def expert_call(rows, dm_rows, weight, first, count, w_gate, w_up, w_down, scalars, dp, ways, block=512):
    _, total, width = rows.shape
    ff = w_gate.shape[2] // ways
    chunks = total // block
    row = lambda n, i, s: (first + n, jnp.minimum(i, chunks - 1), 0)
    out = lambda n, i, s: (n, jnp.minimum(i, chunks - 1), 0)
    bank = lambda a: pl.BlockSpec((1,) + a.shape[1:], lambda n, i, s: (s[n], 0, 0))
    share = width // dp
    S, M = jax.ShapeDtypeStruct, pltpu.VMEM
    return pl.pallas_call(functools.partial(expert_kernel, chunks, dp, ways),
        grid_spec=pltpu.PrefetchScalarGridSpec(num_scalar_prefetch=1, grid=(count, chunks + 1),
            in_specs=[pl.BlockSpec((1, block, width), row), pl.BlockSpec((1, block, width), row), pl.BlockSpec((1, block, 1), row),
                bank(w_gate), bank(w_up), bank(w_down)],
            out_specs=(pl.BlockSpec((1, block, width), out), pl.BlockSpec((1, block, width), out), pl.BlockSpec((1, block, 1), out),
                pl.BlockSpec((dp, 1, 3 * share, ff), lambda n, i, s: (0, n, 0, 0))),
            scratch_shapes=[M((total, width), BF16), M((total, width), BF16), M((total, ff), BF16), M((total, 2 * ff), BF16)]
                + ([M((width, ff), BF16), M((width, ff), BF16), M((ff, width), BF16)] if ways > 1 else [])),
        out_shape=(S((count, total, width), BF16), S((count, total, width), BF16), S((count, total, 1), F32),
            S((dp, count, 3 * share, ff), BF16)),
        compiler_params=pltpu.CompilerParams(vmem_limit_bytes=58 << 20, dimension_semantics=("arbitrary", "arbitrary")),
        cost_estimate=CHEAP,
        name="expert_part" if ways > 1 else "experts")(scalars, rows, dm_rows, weight, w_gate, w_up, w_down)

def place_kernel(whole, rest, ways, *refs):
    moved, (gate_ref, up_ref, down_ref) = refs[:-3], refs[-3:]
    i = pl.program_id(0)
    share, down_share = gate_ref.shape[1], down_ref.shape[1]
    width, ff = down_ref.shape[2], gate_ref.shape[2]
    quads = moved[0].shape[0]
    @pl.when(i < QUAD)
    def _():
        for s in range(whole):
            block = sum(moved[0][k, 0, s].astype(F32) for k in range(quads))
            gate_ref[s] = block[:share]
            up_ref[s] = block[share:2 * share]
            for c in range(width // ff):
                first = 2 * share + c * down_share
                down_ref[s, :, c * ff:(c + 1) * ff] = block[first:first + down_share]
    if rest:
        @pl.when(i == QUAD)
        def _():
            cols = ff // ways
            part = down_share // ways
            for x in range(rest):
                gate = jnp.zeros((2 * share, ff), F32)
                for h in range(ways):
                    col = lax.broadcasted_iota(jnp.int32, (cols, ff), 0)
                    spot = (col // part * ways + h) * part + col % part
                    pick = (lax.broadcasted_iota(jnp.int32, (cols, ff), 1) == spot).astype(F32).astype(BF16)
                    down = jnp.zeros((share, cols), F32)
                    for k in range(quads):
                        block = moved[1][k, x * ways + h, 0]
                        gate = gate + mm(block[:2 * share], pick)
                        down = down + block[2 * share:].astype(F32)
                    for c in range(width // cols):
                        down_ref[x, h * part:(h + 1) * part, c * cols:(c + 1) * cols] = down[c * part:(c + 1) * part]
                gate_ref[x] = gate[:share]
                up_ref[x] = gate[share:]

def place_call(moved, local, ffn, width):
    whole = local // QUAD
    rest = local - whole * QUAD
    ways = QUAD // rest if rest else 1
    share = moved[0].shape[2] // 3
    down_share = ffn * share // width
    quads = moved[0].shape[0] // QUAD
    steps = QUAD + (1 if rest else 0)
    moved = [a.reshape((quads, QUAD) + a.shape[1:]) for a in moved]
    one = lambda a: pl.BlockSpec((quads, 1) + a.shape[2:], lambda i: (0, jnp.minimum(i, QUAD - 1), 0, 0, 0))
    full = lambda a: pl.BlockSpec(a.shape, lambda i: (0, 0, 0, 0, 0))
    out = lambda a, b: pl.BlockSpec((whole, a, b), lambda i: (i, 0, 0))
    S = jax.ShapeDtypeStruct
    return pl.pallas_call(functools.partial(place_kernel, whole, rest, ways), grid=(steps,),
        in_specs=[one(moved[0])] + [full(a) for a in moved[1:]],
        out_specs=(out(share, ffn), out(share, ffn), out(down_share, width)),
        out_shape=(S((local, share, ffn), F32), S((local, share, ffn), F32), S((local, down_share, width), F32)),
        compiler_params=pltpu.CompilerParams(vmem_limit_bytes=58 << 20, dimension_semantics=("arbitrary",)),
        cost_estimate=CHEAP, name="place_gradients")(*moved)

def first_hop(part, mask):
    return [bit for bit in SUM_ORDERS[part] if mask & bit][0]

def combine_kernel(banks, slots, capacity, with_dg, *refs):
    rows = refs[:banks]
    refs = refs[banks:]
    tables_ref = refs[0]
    refs = refs[1:]
    if with_dg:
        dg_refs, refs = refs[:banks], refs[banks:]
        out_ref, dg_out = refs[:2]
        refs = refs[2:]
    else:
        out_ref, refs = refs[0], refs[1:]
    core_out, core_in, held, got, core_send, core_recv, send, recv = refs[:8]
    if with_dg:
        dg_hold, dg_in, dg_send, dg_recv = refs[8:]
    width = out_ref.shape[1]
    part_width = width // len(SUM_ORDERS)
    greet(range(1, 16) if with_dg else (1, 2, 4, 8))
    def hots(mask):
        return one_hot(tables_ref[mask], capacity, slots)
    def block_sum(mask, hot):
        return mm(jnp.concatenate([h.astype(BF16) for h in hot], axis=0),
            jnp.concatenate([a[n, pl.ds(mask * capacity, capacity), :] for a in rows for n in range(a.shape[0])], axis=0), TN)
    dg_copies = []
    def dg_step(mask, hot):
        if not with_dg:
            return
        for k in range(slots):
            col = [(a, n) for a in dg_refs for n in range(a.shape[0])][k]
            col = col[0][col[1], pl.ds(mask * capacity, capacity), :]
            dg_hold[mask, k:k + 1, :] = jnp.sum(jnp.where(hot[k], col, 0.0), axis=0, keepdims=True)
        if mask == 0:
            return
        copy = pltpu.make_async_remote_copy(dg_hold.at[mask], dg_in.at[mask], dg_send.at[mask], dg_recv.at[mask],
            device_id=group_device(mask), device_id_type=MESH)
        copy.start()
        dg_copies.append(copy)
    listed = sorted(range(0, 16, 2), key=lambda m: (-bin(m).count("1"), m))
    if with_dg:
        dg_hold[...] = jnp.zeros_like(dg_hold)
    core = {}
    for mask in listed:
        hot = hots(mask | CORE)
        core_out[mask // 2] = block_sum(mask | CORE, hot).astype(BF16)
        core[mask] = pltpu.make_async_remote_copy(core_out.at[mask // 2], core_in.at[mask // 2], core_send.at[mask // 2],
            core_recv.at[mask // 2], device_id=group_device(CORE), device_id_type=MESH)
        core[mask].start()
        dg_step(mask | CORE, hot)
    copies = {}
    for p in range(len(SUM_ORDERS)):
        for mask in range(2, 16, 2):
            copies[p, mask] = pltpu.make_async_remote_copy(held.at[p, mask // 2], got.at[p, mask // 2], send.at[p, mask // 2],
                recv.at[p, mask // 2], device_id=group_device(first_hop(p, mask)), device_id_type=MESH)
    for mask in listed:
        hot = hots(mask)
        own = block_sum(mask, hot)
        core[mask].wait_recv()
        own = (own + core_in[mask // 2].astype(F32)).astype(BF16)
        for p in range(len(SUM_ORDERS)):
            held[p, mask // 2] = own[:, p * part_width:(p + 1) * part_width]
            if mask & SUM_ORDERS[p][0]:
                copies[p, mask].start()
        dg_step(mask, hot)
    def add(p, target, sources):
        total = held[p, target // 2].astype(F32)
        for source in sources:
            copies[p, source].wait_recv()
            total = total + got[p, source // 2].astype(F32)
        return total
    def forward(p, target, sources):
        held[p, target // 2] = add(p, target, sources).astype(BF16)
        copies[p, target].start()
    for both in (True, False):
        for p in range(len(SUM_ORDERS)):
            a, b, c = SUM_ORDERS[p]
            target = b | c if both else b
            forward(p, target, [target | a])
    for p in range(len(SUM_ORDERS)):
        a, b, c = SUM_ORDERS[p]
        forward(p, c, [c | a, c | b])
    for p in range(len(SUM_ORDERS)):
        a, b, c = SUM_ORDERS[p]
        out_ref[:, p * part_width:(p + 1) * part_width] = add(p, 0, [a, b, c])
    if with_dg:
        dg_out[0] = dg_hold[0]
        for copy in dg_copies:
            copy.wait_recv()
        for mask in range(1, 16):
            dg_out[mask] = dg_in[mask]
        for copy in dg_copies:
            copy.wait_send()
    for mask in listed:
        core[mask].wait_send()
    for key in copies:
        copies[key].wait_send()

def combine_rows(rows, tables, dgs, capacity, collective_id):
    banks, slots = len(rows), sum(a.shape[0] for a in rows)
    tokens, width = tables.shape[2], rows[0].shape[2]
    V = pl.BlockSpec(memory_space=pltpu.VMEM)
    with_dg = dgs is not None
    out = jax.ShapeDtypeStruct((tokens, width), F32)
    table = pltpu.VMEM(tables.shape, F32)
    sem = pltpu.SemaphoreType.DMA
    return pl.pallas_call(functools.partial(combine_kernel, banks, slots, capacity, with_dg),
        out_shape=(out, jax.ShapeDtypeStruct(tables.shape, F32)) if with_dg else out,
        in_specs=[V] * (banks + 1 + (banks if with_dg else 0)), out_specs=(V, V) if with_dg else V,
        scratch_shapes=[pltpu.VMEM((8, tokens, width), BF16), pltpu.VMEM((8, tokens, width), BF16),
            pltpu.VMEM((len(SUM_ORDERS), 8, tokens, width // len(SUM_ORDERS)), BF16), pltpu.VMEM((len(SUM_ORDERS), 8, tokens, width // len(SUM_ORDERS)), BF16),
            sem((8,)), sem((8,)), sem((len(SUM_ORDERS), 8)), sem((len(SUM_ORDERS), 8))] + ([table, table, sem((16,)), sem((16,))] if with_dg else []),
        compiler_params=pltpu.CompilerParams(vmem_limit_bytes=58 << 20, collective_id=collective_id, has_side_effects=True),
        cost_estimate=CHEAP,
        name="combine_with_dg" if with_dg else "combine_rows")(*rows, tables, *(dgs if with_dg else ()))


DP_ORDERS = (("q", 1, 2), ("q", 2, 1), ("q", 2, 1))


def device_experts(local, r):
    whole = local // QUAD
    rest = local - whole * QUAD
    return [r * whole + s for s in range(whole)] + ([QUAD * whole + r // (QUAD // rest)] if rest else [])


def dp_last(part, k, m):
    return [dim for dim in DP_ORDERS[part] if (k if dim == "q" else m & dim)][-1]

def dp_source(part, k, m):
    dim = dp_last(part, k, m)
    return (0, m) if dim == "q" else (k, m ^ dim)

def dp_origin(k, m):
    return place_at((lax.axis_index("q") + k) % lax.axis_size("q"), flip(member_r(), m))

def dp_copies(ref, rows, first, part_width, send, recv):
    quads = lax.axis_size("q")
    copies = {}
    for p in range(3):
        columns = pl.ds(p * part_width, part_width)
        for k in range(quads):
            for m in range(QUAD):
                if (k, m) == (0, 0):
                    continue
                dim = dp_last(p, k, m)
                block = ref.at[pl.ds(first(dp_origin(*dp_source(p, k, m))), rows), columns]
                q, r, e = lax.axis_index("q"), member_r(), lax.axis_index("expert")
                device = device_at((q + quads - k) % quads, r, e) if dim == "q" else device_at(q, flip(r, dim), e)
                copies[p, k, m] = pltpu.make_async_remote_copy(block, block, send.at[p, k, m], recv.at[p, k, m],
                    device_id=device, device_id_type=MESH)
    return copies

def dp_order(copies):
    def hops(key):
        p, k, m = key
        return (1 if k else 0) + bin(m).count("1")
    return sorted(copies, key=lambda key: (hops(key), DP_ORDERS[key[0]].index(dp_last(*key)), key[0], key))

def dp_start(copies, arrived):
    for key in dp_order(copies):
        if arrived[0] == key[0] and dp_source(*key) == arrived[1:]:
            copies[key].start()

def start_kernel(dims, exchange, *refs):
    (experts, capacity, top_count, q_cols, k_cols, rows_here, shard_rows) = dims
    (tokens_ref, pieces_ref, wout_ref, routes_ref, priority_ref, seg_ref, cos_ref, sin_ref,
     x_out, w_out, wout_out, h1_ref, q_ref, k_ref, v_ref, o_ref, lse_ref, middle_ref, h2_ref, table_ref, probs_ref, gains_ref,
     xs, ws, wouts, vt_ref, h1s, os, own_sem,
     x_send, x_recv, p_send, p_recv, w_send, w_recv, o_send, o_recv, wo_send, wo_recv, wx_send, wx_recv) = refs
    E = lax.axis_size("expert")
    quads = lax.axis_size("q")
    dp = quads * QUAD
    q, r, e = lax.axis_index("q"), member_r(), lax.axis_index("expert")
    place = place_at(q, r)
    length, width = xs.shape
    total = ws.shape[1]
    block_rows = ws.shape[0] // dp
    heads, kv_heads = q_cols // HD, k_cols // HD
    group = heads // kv_heads
    block = 256

    barrier = pltpu.get_barrier_semaphore()
    friends = [device_at(q, r, flip(e, j)) for j in (1, 2, 3)] + [device_at(q, flip(r, m), e) for m in (1, 2)]
    friends += [device_at((q + k) % quads, r, e) for k in range(1, quads)]
    for friend in friends:
        pl.semaphore_signal(barrier, inc=1, device_id=friend, device_id_type=MESH)
    pl.semaphore_wait(barrier, len(friends))

    def token_rows(who):
        return pl.ds(pl.multiple_of(who * rows_here, 16), rows_here)

    x_copies = {}
    for j in (1, 2, 3):
        source = tokens_ref if j < 3 else xs.at[token_rows(flip(e, 2))]
        target = e if j < 3 else flip(e, 2)
        x_copies[j] = pltpu.make_async_remote_copy(source, xs.at[token_rows(target)], x_send.at[j], x_recv.at[j],
            device_id=device_at(q, r, flip(e, j if j < 3 else 1)), device_id_type=MESH)
    p_copies = []
    mine = pl.multiple_of(place * block_rows, 16)
    if exchange:
        for j in (1, 2, 3):
            rows = pl.ds(pl.multiple_of(place * block_rows + e * shard_rows, 16), shard_rows)
            copy = pltpu.make_async_remote_copy(pieces_ref.at[flip(e, j)], ws.at[rows], p_send.at[j], p_recv.at[j],
                device_id=device_at(q, r, flip(e, j)), device_id_type=MESH)
            copy.start()
            p_copies.append(copy)
        ws[pl.ds(pl.multiple_of(place * block_rows + e * shard_rows, 16), shard_rows), :] = pieces_ref[e]
    else:
        ws[pl.ds(mine, block_rows), :] = pieces_ref[...]
    x_copies[2].start()
    x_copies[1].start()
    xs[token_rows(e), :] = tokens_ref[...]
    w_copies = dp_copies(ws, block_rows, lambda d: pl.multiple_of(d * block_rows, 16), total // 3, w_send, w_recv)
    for copy in p_copies:
        copy.wait_recv()
    for p in range(3):
        dp_start(w_copies, (p, 0, 0))
    wo_copies = {}
    if exchange:
        def out_row(d):
            return pl.multiple_of((d * E + e) * shard_rows, 16)
        wouts[pl.ds(out_row(place), shard_rows), :] = wout_ref[...]
        wo_copies = dp_copies(wouts, shard_rows, out_row, width // 3, wo_send, wo_recv)
        for p in range(3):
            dp_start(wo_copies, (p, 0, 0))

    lane = lax.broadcasted_iota(jnp.int32, (rows_here, 128), 1)
    rank = jnp.zeros((rows_here, 128), jnp.int32)
    for j in range(top_count):
        rank = rank + jnp.where(routes_ref[:, j:j + 1] == lane, priority_ref[:, j:j + 1] + 1, 0)
    rank = rank - 1
    before = (lax.broadcasted_iota(jnp.int32, (rows_here, rows_here), 1)
              < lax.broadcasted_iota(jnp.int32, (rows_here, rows_here), 0)).astype(F32).astype(BF16)
    base = jnp.zeros((1, 128), F32)
    slot = jnp.zeros((rows_here, 128), F32)
    for level in range(top_count):
        hot = (rank == level).astype(F32)
        slot = slot + hot * (base + mm(before, hot.astype(BF16)))
        base = base + jnp.sum(hot, axis=0, keepdims=True)
    named = rank >= 0
    slot = jnp.where(named & (slot < capacity), slot, -1.0)

    x_copies[2].wait_recv()
    x_copies[3].start()
    order = dp_order(w_copies)
    wo_order = dp_order(wo_copies)
    for key in order:
        w_copies[key].wait_recv()
        dp_start(w_copies, key)
    x_copies[1].wait_recv()
    x_copies[3].wait_recv()
    x_back = pltpu.make_async_copy(xs, x_out, own_sem.at[0])
    w_back = pltpu.make_async_copy(ws, w_out, own_sem.at[1])
    x_back.start()
    w_back.start()
    wx_copies = {}
    if exchange:
        for d in range(dp):
            for j in (1, 2, 3):
                owner = e if j < 3 else flip(e, 2)
                rows = pl.ds(pl.multiple_of((d * E + owner) * shard_rows, 16), shard_rows)
                wx_copies[d, j] = pltpu.make_async_remote_copy(wouts.at[rows], wouts.at[rows], wx_send.at[d, j], wx_recv.at[d, j],
                    device_id=device_at(q, r, flip(e, j if j < 3 else 1)), device_id_type=MESH)
    def out_step(step):
        if not exchange:
            return
        third = -(-len(wo_order) // 2)
        if step < 2:
            for key in wo_order[step * third:(step + 1) * third]:
                wo_copies[key].wait_recv()
                dp_start(wo_copies, key)
        if step == 1:
            for d in range(dp):
                wx_copies[d, 2].start()
            for d in range(dp):
                wx_copies[d, 1].start()
        if step == 3:
            for d in range(dp):
                wx_copies[d, 2].wait_recv()
                wx_copies[d, 3].start()

    small = ws[:, total - 128:].astype(F32).T
    gain_attn = small[experts:experts + 1, :]
    gain_moe = small[experts + 1:experts + 2, :]
    gains_ref[0:1, :] = gain_attn
    gains_ref[1:2, :] = gain_moe

    def send_block(b):
        rows = pl.ds(b * rows_here, rows_here)
        @pl.when(e == b)
        def _():
            os[b] = o_ref[rows, :]
        @pl.when(e != b)
        def _():
            pltpu.make_async_remote_copy(o_ref.at[rows], os.at[e], o_send.at[b], o_recv.at[e],
                device_id=device_at(q, r, b), device_id_type=MESH).start()
    sent = 0
    for i in range(length // block):
        rows = pl.ds(i * block, block)
        x = xs[rows, :].astype(F32)
        scale = lax.rsqrt(jnp.mean(x * x, axis=1, keepdims=True) + epsilon)
        h1 = (x * scale * gain_attn).astype(BF16)
        h1s[rows, :] = h1
        qkv = mm(h1, ws[:, :total - 128])
        qk = qkv[:, :q_cols + k_cols]
        turns = (q_cols + k_cols) // 128
        cosine = jnp.concatenate([cos_ref[rows, :]] * turns, axis=1)
        sine = jnp.concatenate([sin_ref[rows, :]] * turns, axis=1)
        qk = (qk * cosine + swap_halves(qk) * sine).astype(BF16)
        v = qkv[:, q_cols + k_cols:].astype(BF16)
        for h in range(heads):
            q_ref[h, rows, :] = qk[:, h * HD:(h + 1) * HD]
        vt = v.astype(F32).T.astype(BF16)
        for h in range(kv_heads):
            k_ref[h, rows, :] = qk[:, q_cols + h * HD:q_cols + (h + 1) * HD]
            v_ref[h, rows, :] = v[:, h * HD:(h + 1) * HD]
            vt_ref[h, :, rows] = vt[h * HD:(h + 1) * HD, :]
        keys = (i + 1) * block
        bias = bias_block(seg_ref[:, rows], keys, i * block)
        outs = []
        for h in range(heads):
            g = h // group
            st = mm(k_ref[g, pl.ds(0, keys), :], q_ref[h, rows, :] * BF16(HD ** -0.5), NT) + bias
            top = jnp.max(st, axis=0, keepdims=True)
            p = jnp.exp(st - top)
            sums = jnp.sum(p, axis=0, keepdims=True)
            outs.append(mm(vt_ref[g, :, pl.ds(0, keys)], p.astype(BF16)) / sums)
            lse_ref[pl.ds(h, 1), rows] = top + jnp.log(sums)
        o_ref[rows, :] = jnp.concatenate(outs, axis=0).T.astype(BF16)
        while sent < E and (sent + 1) * rows_here <= keys:
            send_block(sent)
            sent += 1
        out_step(i)
    h1_back = pltpu.make_async_copy(h1s, h1_ref, own_sem.at[2])
    h1_back.start()
    if exchange:
        for d in range(dp):
            wx_copies[d, 1].wait_recv()
            wx_copies[d, 3].wait_recv()
    else:
        fill = pltpu.make_async_copy(wout_ref, wouts, own_sem.at[3])
        fill.start()
        fill.wait()
    wout_back = pltpu.make_async_copy(wouts, wout_out, own_sem.at[3])
    wout_back.start()
    def o_descriptor(b):
        return pltpu.make_async_remote_copy(o_ref.at[pl.ds(0, rows_here)], os.at[b], o_send.at[b], o_recv.at[b],
            device_id=device_at(q, r, flip(e, 1)), device_id_type=MESH)
    middle = xs[token_rows(e), :].astype(F32)
    for b in range(E):
        @pl.when(e != b)
        def _():
            o_descriptor(b).wait_recv()
    for b in range(E):
        middle = middle + mm(os[b], wouts[b * q_cols:(b + 1) * q_cols, :])
    middle_ref[...] = middle
    scale = lax.rsqrt(jnp.mean(middle * middle, axis=1, keepdims=True) + epsilon)
    h2 = (middle * scale * gain_moe).astype(BF16)
    h2_ref[...] = h2
    logits = jnp.where(named, mm(h2, ws[:, total - 128:]), masked_score)
    powers = jnp.where(named, jnp.exp(logits - jnp.max(logits, axis=1, keepdims=True)), 0.0)
    probs = powers / jnp.sum(powers, axis=1, keepdims=True)
    probs_ref[...] = probs
    slot_rows = slot.T
    prob_rows = probs.T
    local = experts // E
    table_ref[...] = jnp.zeros_like(table_ref)
    for dest_r in range(QUAD):
        for dest_e in range(E):
            for at, expert in enumerate(device_experts(local, dest_r)):
                row = dest_e * local + expert
                table_ref[dest_r * E + dest_e, at:at + 1, :] = slot_rows[row:row + 1, :]
                table_ref[dest_r * E + dest_e, 4 + at:5 + at, :] = prob_rows[row:row + 1, :]
    for b in range(E):
        @pl.when(e != b)
        def _():
            o_descriptor(b).wait_send()
    for copy in p_copies + list(x_copies.values()) + list(w_copies.values()) + list(wo_copies.values()) + list(wx_copies.values()):
        copy.wait_send()
    for copy in (x_back, w_back, h1_back, wout_back):
        copy.wait()

def start_call(tokens, pieces, w_out, routes, priority, segments, cosine, sine, experts, capacity, q_cols, k_cols, exchange):
    E, quads = lax.axis_size("expert"), lax.axis_size("q")
    dp = quads * QUAD
    rows_here, width = tokens.shape
    length = rows_here * E
    shard_rows = width // (dp * E)
    total = pieces.shape[-1]
    V, A = pl.BlockSpec(memory_space=pltpu.VMEM), pl.BlockSpec(memory_space=pl.ANY)
    heads, kv_heads = q_cols // HD, k_cols // HD
    S = jax.ShapeDtypeStruct
    sem = pltpu.SemaphoreType.DMA
    dims = (experts, capacity, routes.shape[1], q_cols, k_cols, rows_here, shard_rows)
    kernel = functools.partial(start_kernel, dims, exchange)
    return pl.pallas_call(kernel,
        out_shape=(S((length, width), BF16), S((width, total), BF16), S((width, width), BF16), S((length, width), BF16),
            S((heads, length, HD), BF16), S((kv_heads, length, HD), BF16), S((kv_heads, length, HD), BF16),
            S((length, q_cols), BF16), S((-(-heads // 8) * 8, length), F32), S((rows_here, width), F32), S((rows_here, width), BF16),
            S((QUAD * E, 8, rows_here), F32), S((rows_here, 128), F32), S((8, width), F32)),
        in_specs=[V, V, V if exchange else A, V, V, V, V, V], out_specs=(A, A, A, A) + (V,) * 10,
        scratch_shapes=[pltpu.VMEM((length, width), BF16), pltpu.VMEM((width, total), BF16), pltpu.VMEM((width, width), BF16),
            pltpu.VMEM((kv_heads, HD, length), BF16), pltpu.VMEM((length, width), BF16), pltpu.VMEM((E, rows_here, q_cols), BF16), sem((4,)),
            sem((4,)), sem((4,)), sem((4,)), sem((4,)), sem((3, quads, QUAD)), sem((3, quads, QUAD)), sem((E,)), sem((E,)),
            sem((3, quads, QUAD)), sem((3, quads, QUAD)), sem((dp, 4)), sem((dp, 4))],
        compiler_params=pltpu.CompilerParams(vmem_limit_bytes=58 << 20, collective_id=4, has_side_effects=True),
        cost_estimate=CHEAP,
        name="start")(tokens, pieces, w_out, routes, priority, segments.reshape(1, -1), cosine, sine)


DENSE_ORDERS = ((1, 2, "q"), (2, 1, "q"))

def back_kernel(dims, exchange, *refs):
    (experts, q_cols, k_cols, slots) = dims
    (dr_ref, dg_ref, probs_ref, h2_ref, middle_ref, cot_ref, gains_ref, tokens_ref, wout_ref, q_ref, k_ref, v_ref, lse_ref,
     cos_ref, sin_ref, seg_ref, h1_ref, xall_ref, wall_ref, mixed_ref) = refs[:20]
    refs = refs[20:]
    if exchange:
        (tokens_out, gq_ref, gk_ref, gv_ref, small_ref, gout_ref) = refs[:6]
        refs = refs[6:]
    else:
        (tokens_out, dense_ref, gout_ref) = refs[:3]
        refs = refs[3:]
    (h1s, xs, ws, mixeds, load_sem, dgt, dats, dos, do_out, kt_ref, dk_ref, dv_ref, dqkv, dx1s, small, part, core_in, y_in,
     g1, g2, r1, r2, f1,
     do_send, do_recv, dat_send, dat_recv, part_send, part_recv, g1_send, g1_recv, g2_send, g2_recv, f_send, f_recv) = refs
    E, quads = lax.axis_size("expert"), lax.axis_size("q")
    q, r, e = lax.axis_index("q"), member_r(), lax.axis_index("expert")
    dp = quads * QUAD
    rows_here, width = dr_ref.shape
    length = rows_here * E
    heads, kv_heads = q_cols // HD, k_cols // HD
    group = heads // kv_heads
    total = ws.shape[1]
    qkv_cols = total - 128
    factor = HD ** -0.5
    block = 256
    loads = [pltpu.make_async_copy(a, b, load_sem.at[i])
             for i, (a, b) in enumerate(((wall_ref, ws), (mixed_ref, mixeds), (h1_ref, h1s), (xall_ref, xs.at[pl.ds(0, length)])))]
    load_out = pltpu.make_async_copy(wout_ref, xs, load_sem.at[4])
    load_out.start()
    for load in loads[:3]:
        load.start()
    barrier = pltpu.get_barrier_semaphore()
    friends = [device_at(q, r, flip(e, j)) for j in (1, 2, 3)] + [device_at(q, flip(r, m), e) for m in (1, 2)]
    friends += [device_at((q + k) % quads, r, e) for k in range(1, quads)]
    for friend in friends:
        pl.semaphore_signal(barrier, inc=1, device_id=friend, device_id_type=MESH)
    pl.semaphore_wait(barrier, len(friends))

    dgt[...] = jnp.zeros_like(dgt)
    local = experts // E
    whole = local // QUAD
    for mask in range(QUAD * E):
        from_r, from_e = flip(r, mask >> 2), flip(e, mask & 3)
        for k in range(slots):
            if k < whole:
                row = from_e * local + from_r * whole + k
            else:
                row = from_e * local + QUAD * whole + from_r // (QUAD // (local - QUAD * whole))
            dgt[pl.ds(row, 1), :] += dg_ref[mask, k:k + 1, :]
    dg = dgt[...].T
    probs = probs_ref[...]
    dz = (probs * (dg - jnp.sum(probs * dg, axis=1, keepdims=True))).astype(BF16)
    loads[0].wait()
    dh2 = dr_ref[...] + mm(dz, ws[:, qkv_cols:], NT)
    gain_attn, gain_moe = gains_ref[0:1, :], gains_ref[1:2, :]
    middle = middle_ref[...]
    scale = lax.rsqrt(jnp.mean(middle * middle, axis=1, keepdims=True) + epsilon)
    unit = middle * scale
    grad_moe_gain = jnp.sum(dh2 * unit, axis=0, keepdims=True)
    grad_unit = dh2 * gain_moe
    dx1 = cot_ref[...].astype(F32) + scale * (grad_unit - unit * jnp.mean(grad_unit * unit, axis=1, keepdims=True))
    dx1s[...] = dx1
    dat = dx1.astype(BF16)

    def token_rows(who):
        return pl.ds(pl.multiple_of(who * rows_here, 16), rows_here)
    load_out.wait()
    for b in range(E):
        do = mm(dat, xs[b * q_cols:(b + 1) * q_cols, :], NT).astype(BF16)
        do_out[b] = do
        @pl.when(e == b)
        def _():
            dos[token_rows(e), :] = do_out[b]
        @pl.when(e != b)
        def _():
            pltpu.make_async_remote_copy(do_out.at[b], dos.at[token_rows(e)], do_send.at[b], do_recv.at[e],
                device_id=device_at(q, r, b), device_id_type=MESH).start()
    loads[3].start()
    def do_descriptor(b):
        return pltpu.make_async_remote_copy(do_out.at[b], dos.at[pl.ds(b * rows_here, rows_here)], do_send.at[b], do_recv.at[b],
            device_id=device_at(q, r, flip(e, 1)), device_id_type=MESH)
    dats[token_rows(e), :] = dat
    dat_copies = {}
    for j in (1, 2, 3):
        rows = token_rows(e if j < 3 else flip(e, 2))
        dat_copies[j] = pltpu.make_async_remote_copy(dats.at[rows], dats.at[rows], dat_send.at[j], dat_recv.at[j],
            device_id=device_at(q, r, flip(e, j if j < 3 else 1)), device_id_type=MESH)
    dat_copies[2].start()
    dat_copies[1].start()
    small[...] = mm(h2_ref[...], dz, TN)
    dk_ref[...] = jnp.zeros_like(dk_ref)
    dv_ref[...] = jnp.zeros_like(dv_ref)
    for g in range(kv_heads):
        kt_ref[g] = k_ref[g].astype(F32).T.astype(BF16)

    seen = 0
    for i in range(length // block):
        rows = pl.ds(i * block, block)
        keys = (i + 1) * block
        while seen * rows_here < keys:
            @pl.when(e != seen)
            def _():
                do_descriptor(seen).wait_recv()
            seen += 1
        span = pl.ds(0, keys)
        bias = bias_block(seg_ref[:, rows], keys, i * block)
        dqs = []
        for h in range(heads):
            g = h // group
            qh = q_ref[h, rows, :]
            do = dos[rows, h * HD:(h + 1) * HD]
            st = mm(k_ref[g, span, :], qh * BF16(factor), NT) + bias
            p = jnp.exp(st - lse_ref[pl.ds(h, 1), rows])
            dpt = mm(v_ref[g, span, :], do, NT)
            inner = jnp.sum(p * dpt, axis=0, keepdims=True)
            ds = (p * (dpt - inner)).astype(BF16)
            dv_ref[g, span, :] += mm(p.astype(BF16), do)
            dk_ref[g, span, :] += mm(ds, qh)
            dqs.append(mm(kt_ref[g, :, span], ds))
        dq = jnp.concatenate(dqs, axis=0).T * factor
        cosine = jnp.concatenate([cos_ref[rows, :]] * (q_cols // 128), axis=1)
        sine = jnp.concatenate([sin_ref[rows, :]] * (q_cols // 128), axis=1)
        dqkv[rows, :q_cols] = (dq * cosine - swap_halves(dq) * sine).astype(BF16)
        if i == 1:
            dat_copies[2].wait_recv()
            dat_copies[3].start()
    dk = jnp.concatenate([dk_ref[g] for g in range(kv_heads)], axis=1) * factor
    cosine = jnp.concatenate([cos_ref[...]] * (k_cols // 128), axis=1)
    sine = jnp.concatenate([sin_ref[...]] * (k_cols // 128), axis=1)
    dqkv[:, q_cols:q_cols + k_cols] = (dk * cosine - swap_halves(dk) * sine).astype(BF16)
    dqkv[:, q_cols + k_cols:] = jnp.concatenate([dv_ref[g] for g in range(kv_heads)], axis=1).astype(BF16)

    grad_attn_gain = jnp.zeros((1, width), F32)
    loads[3].wait()
    part_copies = {}
    own = None
    for j in (3, 1, 2, 0):
        rows = token_rows(flip(e, j))
        dh1 = mm(dqkv[rows, :], ws[:, :qkv_cols], NT)
        x = xs[rows, :].astype(F32)
        scale = lax.rsqrt(jnp.mean(x * x, axis=1, keepdims=True) + epsilon)
        grad_attn_gain = grad_attn_gain + jnp.sum(dh1 * (x * scale), axis=0, keepdims=True)
        if j & 1:
            part[j - 1] = dh1.astype(BF16)
            part_copies[j] = pltpu.make_async_remote_copy(part.at[j - 1], core_in.at[j // 2], part_send.at[j], part_recv.at[j],
                device_id=device_at(q, r, flip(e, 1)), device_id_type=MESH)
            part_copies[j].start()
        elif j == 2:
            part_copies[3].wait_recv()
            part[1] = (dh1 + core_in[1].astype(F32)).astype(BF16)
            part_copies[2] = pltpu.make_async_remote_copy(part.at[1], y_in, part_send.at[2], part_recv.at[2],
                device_id=device_at(q, r, flip(e, 2)), device_id_type=MESH)
            part_copies[2].start()
        else:
            own = dh1

    rows_out = lax.broadcasted_iota(jnp.int32, (128, width), 0)
    gains = jnp.where(rows_out == experts, grad_attn_gain, 0.0) + jnp.where(rows_out == experts + 1, grad_moe_gain, 0.0)
    small_all = small[...] + gains.T
    loads[2].wait()
    share = width // dp
    grad = mm(h1s[...], dqkv[...], TN).astype(BF16)
    for d in range(dp):
        g1[d, :, :qkv_cols] = grad[d * share:(d + 1) * share]
        g1[d, :, qkv_cols:] = small_all[d * share:(d + 1) * share].astype(BF16)
    dat_copies[1].wait_recv()
    dat_copies[3].wait_recv()
    loads[1].wait()
    grad = mm(mixeds[...], dats[...], TN)
    out_share = q_cols // dp
    if exchange:
        for d in range(dp):
            g2[d] = grad[d * out_share:(d + 1) * out_share].astype(BF16)
    else:
        gout_ref[...] = grad.astype(BF16)
    arrays = [(g1, r1, g1_send, g1_recv)] + ([(g2, r2, g2_send, g2_recv)] if exchange else [])
    keys = [(k, m) for k in range(quads) for m in range(QUAD)]
    def at(k, m):
        return place_at((q + k) % quads, flip(r, m))
    def has(key, dim):
        return key[0] if dim == "q" else key[1] & dim
    def first(p, key):
        return [n for n, dim in enumerate(DENSE_ORDERS[p]) if has(key, dim)][0]
    def sources(p, key, upto):
        found = []
        for dim in DENSE_ORDERS[p][:upto]:
            found += [(k, key[1]) for k in range(1, quads)] if dim == "q" else [(key[0], key[1] | dim)]
        return found
    copies = {}
    for n, (grad_ref, landing, send, recv) in enumerate(arrays):
        half = grad_ref.shape[2] // 2
        for p in range(2):
            for k, m in keys[1:]:
                dim = DENSE_ORDERS[p][first(p, (k, m))]
                device = device_at((q + k) % quads, r, e) if dim == "q" else device_at(q, flip(r, dim), e)
                copies[n, p, k, m] = pltpu.make_async_remote_copy(grad_ref.at[at(k, m), :, pl.ds(p * half, half)],
                    landing.at[p, k, m], send.at[p, k, m], recv.at[p, k, m], device_id=device, device_id_type=MESH)
    numbers = range(len(arrays))
    def reduced(n, p, key):
        grad_ref, landing = arrays[n][:2]
        half = grad_ref.shape[2] // 2
        sum_now = grad_ref[at(*key), :, p * half:(p + 1) * half].astype(F32)
        for k, m in sources(p, key, 3 if key == (0, 0) else first(p, key)):
            copies[n, p, k, m].wait_recv()
            sum_now = sum_now + landing[p, k, m].astype(F32)
        return sum_now
    def send_on(level):
        for p in range(2):
            now = [key for key in keys[1:] if first(p, key) == level]
            now.sort(key=lambda key: -sum(1 for dim in DENSE_ORDERS[p] if has(key, dim)))
            for k, m in now:
                for n in numbers:
                    if level:
                        half = arrays[n][0].shape[2] // 2
                        arrays[n][0][at(k, m), :, p * half:(p + 1) * half] = reduced(n, p, (k, m)).astype(BF16)
                    copies[n, p, k, m].start()
    send_on(0)
    send_on(1)
    part_copies[1].wait_recv()
    part_copies[2].wait_recv()
    dh1 = own + core_in[0].astype(F32) + y_in[...].astype(F32)
    x = tokens_ref[...].astype(F32)
    scale = lax.rsqrt(jnp.mean(x * x, axis=1, keepdims=True) + epsilon)
    unit = x * scale
    grad_unit = dh1 * gain_attn
    tokens_out[...] = dx1s[...] + scale * (grad_unit - unit * jnp.mean(grad_unit * unit, axis=1, keepdims=True))
    send_on(2)
    final = {(n, p): reduced(n, p, (0, 0)) for n in numbers for p in range(2)}
    dense = jnp.concatenate([final[0, 0], final[0, 1]], axis=1)
    if exchange:
        gout_ref[...] = jnp.concatenate([final[1, 0], final[1, 1]], axis=1).astype(BF16)
        g1[at(0, 0)] = dense.astype(BF16)
        shard = share // E
        f_copies = []
        for j in (1, 2, 3):
            rows = pl.ds(pl.multiple_of(flip(e, j) * shard, 16), shard)
            copy = pltpu.make_async_remote_copy(g1.at[at(0, 0), rows], f1.at[e], f_send.at[j], f_recv.at[j],
                device_id=device_at(q, r, flip(e, j)), device_id_type=MESH)
            copy.start()
            f_copies.append(copy)
        f1[e] = g1[at(0, 0), pl.ds(pl.multiple_of(e * shard, 16), shard), :]
        for copy in f_copies:
            copy.wait_recv()
        tail = jnp.zeros((shard, 128), F32)
        for b in range(E):
            piece = f1[b].astype(F32)
            gq_ref[:, b * q_cols:(b + 1) * q_cols] = piece[:, :q_cols]
            gk_ref[:, b * k_cols:(b + 1) * k_cols] = piece[:, q_cols:q_cols + k_cols]
            gv_ref[:, b * k_cols:(b + 1) * k_cols] = piece[:, q_cols + k_cols:qkv_cols]
            tail = tail + piece[:, qkv_cols:]
        small_ref[...] = tail
        for copy in f_copies:
            copy.wait_send()
    else:
        dense_ref[...] = dense.astype(BF16)
    for b in range(E):
        @pl.when(e != b)
        def _():
            do_descriptor(b).wait_send()
    for copy in list(dat_copies.values()) + list(part_copies.values()) + list(copies.values()):
        copy.wait_send()

def back_call(dr_sum, dg_back, probs, h2, middle, cotangent, gains, tokens, out_full, query, key, value, log_total,
              cosine, sine, segments, h1_all, x_all, w_all, mixed, experts, q_cols, k_cols, slots, exchange):
    E, quads = lax.axis_size("expert"), lax.axis_size("q")
    dp = quads * QUAD
    rows_here, width = tokens.shape
    length = rows_here * E
    total = w_all.shape[1]
    heads, kv_heads = q_cols // HD, k_cols // HD
    share, out_share = width // dp, q_cols // dp
    shard = share // E
    V, A = pl.BlockSpec(memory_space=pltpu.VMEM), pl.BlockSpec(memory_space=pl.ANY)
    S, M, sem = jax.ShapeDtypeStruct, pltpu.VMEM, pltpu.SemaphoreType.DMA
    if exchange:
        outs = (S((rows_here, width), F32), S((shard, q_cols * E), F32), S((shard, k_cols * E), F32), S((shard, k_cols * E), F32),
            S((shard, 128), F32), S((out_share, width), BF16))
        second = [M((dp, out_share, width), BF16), M((2, quads, QUAD, out_share, width // 2), BF16)]
    else:
        outs = (S((rows_here, width), F32), S((share, total), BF16), S((q_cols, width), BF16))
        second = [M((16, 128), BF16)] * 2
    scratch = [M((length, width), BF16), M((width, width), BF16), M((width, total), BF16), M((length, q_cols), BF16), sem((5,)),
        M((128, rows_here), F32), M((length, width), BF16), M((length, q_cols), BF16), M((E, rows_here, q_cols), BF16),
        M((kv_heads, HD, length), BF16), M((kv_heads, length, HD), F32), M((kv_heads, length, HD), F32), M((length, total - 128), BF16),
        M((rows_here, width), F32), M((width, 128), F32), M((3, rows_here, width), BF16), M((2, rows_here, width), BF16),
        M((rows_here, width), BF16),
        M((dp, share, total), BF16), second[0],
        M((2, quads, QUAD, share, total // 2), BF16), second[1], M((E, shard, total), BF16)]
    scratch += [sem((4,))] * 6 + [sem((2, quads, 4))] * 4 + [sem((4,))] * 2
    return pl.pallas_call(functools.partial(back_kernel, (experts, q_cols, k_cols, slots), exchange),
        out_shape=outs, in_specs=[V] * 8 + [A] + [V] * 7 + [A] * 4, out_specs=(V,) * len(outs), scratch_shapes=scratch,
        compiler_params=pltpu.CompilerParams(vmem_limit_bytes=60 << 20, collective_id=5, has_side_effects=True),
        cost_estimate=CHEAP,
        name="backward")(dr_sum, dg_back, probs, h2, middle, cotangent, gains, tokens, out_full, query, key, value, log_total,
            cosine, sine, segments.reshape(1, -1), h1_all, x_all, w_all, mixed)


ALL = ("q", "rh", "rl", "expert")
DP = ("q", "rh", "rl")
GROUP = ("rh", "rl", "expert")


def shards(
    tokens, w_query, w_key, w_value, w_out, w_router, gain_attn, gain_moe,
    w_gate, w_up, w_down, segments, routes, priority, cotangent,
):
    rows_here, width = tokens.shape
    E = lax.axis_size("expert")
    R = QUAD
    Q = lax.axis_size("q")
    e = lax.axis_index("expert")
    r = member_r()
    shard_rows = w_query.shape[0]
    local = w_gate.shape[0]
    experts = local * E
    ffn = w_gate.shape[2]
    capacity = rows_here * routes.shape[1] // experts
    length = rows_here * E
    sources = R * E
    q_cols = w_query.shape[1] // E
    k_cols = w_key.shape[1] // E
    exchange = shard_rows % 16 == 0
    small = jnp.concatenate([w_router, gain_attn[:, None], gain_moe[:, None]], axis=1)
    small = jnp.pad(small, ((0, 0), (0, 128 - small.shape[1])))
    pieces = jnp.concatenate(
        [w.reshape(shard_rows, E, -1) for w in (w_query, w_key, w_value)]
        + [jnp.broadcast_to(small[:, None], (shard_rows, E, 128))],
        axis=2,
    )
    pieces = jnp.transpose(pieces, (1, 0, 2))
    out_part = w_out
    if not exchange:
        pieces = lax.all_to_all(pieces, "expert", split_axis=0, concat_axis=0, tiled=True)
        pieces = pieces.reshape(E * shard_rows, -1)
        out_part = lax.all_gather(w_out, ALL, axis=0, tiled=True)
    dm_all = lax.all_gather(cotangent, GROUP, axis=0, tiled=True).reshape(
        sources, rows_here, width
    )
    cosine, sine = rope_tables(jnp.arange(length, dtype=jnp.int32), HD)
    cosine = jnp.tile(cosine, (1, 4))
    sine = jnp.tile(jnp.concatenate([-sine, sine], axis=1), (1, 2))
    (x_all, w_all, out_full, h1_all, query, key, value, mixed, log_total, middle, h2, table, probs, gains) = start_call(
        tokens, pieces, out_part, routes, priority, segments, cosine, sine, experts, capacity, q_cols, k_cols, exchange
    )
    qkv_cols = q_cols + 2 * k_cols
    dp = Q * R
    whole = local // R
    rest = local - whole * R
    ways = R // rest if rest else 1
    slots = whole + (1 if rest else 0)

    rows, dm_rows, weight, tables = gather_rows(h2, table, dm_all, slots, capacity, 1)
    def scalars(places):
        return jnp.stack(places + [r % ways]).astype(jnp.int32)

    banks = (w_gate, w_up, w_down)
    done = []
    if rest:
        part = expert_call(rows, dm_rows, weight, whole, 1, *banks, scalars([R * whole + r // ways]), dp, ways)
        part_moved = lax.all_to_all(part[3], DP, split_axis=0, concat_axis=0, tiled=True)
    done.append(expert_call(rows, dm_rows, weight, 0, whole, *banks, scalars([r * whole + s for s in range(whole)]), dp, 1))
    moved = [lax.all_to_all(done[0][3], DP, split_axis=0, concat_axis=0, tiled=True)]
    if rest:
        done.append(part)
        moved.append(part_moved)
    y_rows, dr_rows, dg_rows = ([d[n] for d in done] for n in range(3))
    dr_sum, dg_back = combine_rows(dr_rows, tables, dg_rows, capacity, 2)
    out = back_call(
        dr_sum, dg_back, probs, h2, middle, cotangent, gains, tokens, out_full, query, key, value, log_total,
        cosine, sine, segments, h1_all, x_all, w_all, mixed, experts, q_cols, k_cols, slots, exchange
    )
    if exchange:
        grad_tokens, grad_query, grad_key, grad_value, small_own, out_sum = out
    else:
        grad_tokens, qkv_sum, out_sum = out
        qkv_own = lax.all_to_all(
            qkv_sum.reshape(E, shard_rows, -1), "expert", split_axis=0, concat_axis=0, tiled=True
        )
        qkv_own = jnp.transpose(qkv_own, (1, 0, 2)).astype(F32)
        small_own = jnp.sum(qkv_own[:, :, qkv_cols:], axis=1)
        grad_query = qkv_own[:, :, :q_cols].reshape(shard_rows, -1)
        grad_key = qkv_own[:, :, q_cols : q_cols + k_cols].reshape(shard_rows, -1)
        grad_value = qkv_own[:, :, q_cols + k_cols : qkv_cols].reshape(shard_rows, -1)
        out_sum = lax.psum_scatter(out_sum, DP, scatter_dimension=0, tiled=True)
    perm = [(p * E + x, dp * x + p) for p in range(dp) for x in range(E)]
    out_own = lax.ppermute(out_sum, ALL, perm).astype(F32)
    late = lax.optimization_barrier((tuple(y_rows), grad_tokens))
    y_sum = combine_rows(list(late[0]), tables, None, capacity, 3)
    outputs = (middle + y_sum).astype(BF16)
    moved, _ = lax.optimization_barrier((moved, outputs))
    gate_share, up_share, down_share = place_call(moved, local, ffn, width)
    return (
        outputs,
        grad_tokens,
        grad_query,
        grad_key,
        grad_value,
        out_own,
        small_own[:, :experts],
        small_own[:, experts],
        small_own[:, experts + 1],
        gate_share,
        up_share,
        down_share,
    )


def solution(mesh):
    dp, ex = mesh.devices.shape
    fine = Mesh(mesh.devices.reshape(dp // QUAD, 2, 2, ex), ALL)
    row, flat = P(ALL, None), P(ALL)
    bank = P("expert", None, None)
    spread = P("expert", DP, None)
    return jax.shard_map(
        shards,
        mesh=fine,
        in_specs=(row,) * 6 + (flat,) * 2 + (bank,) * 3 + (P(DP),) + (row,) * 3,
        out_specs=(row,) * 7 + (flat,) * 2 + (spread,) * 3,
        check_vma=False,
    )
```

```python
import functools

import jax
import jax.numpy as jnp
import numpy as np
from jax import lax
from jax.experimental import pallas as pl
from jax.experimental.pallas import tpu as pltpu
from jax.sharding import Mesh
from jax.sharding import PartitionSpec as P

HD = 64
QUAD = 4
F32 = jnp.float32
BF16 = jnp.bfloat16

CHEAP = pl.CostEstimate(flops=1 << 20, bytes_accessed=1 << 16, transcendentals=0)

epsilon = 1e-06
rope_base = 10000.0
masked_score = -1e30


def rope_tables(length):
    frequency = np.float32(rope_base) ** (np.float32(-2.0) * np.arange(HD // 2, dtype=np.float32) / np.float32(HD))
    angles = np.arange(length, dtype=np.float32)[:, None] * frequency[None, :].astype(np.float32)
    cosine, sine = np.cos(angles).astype(np.float32), np.sin(angles).astype(np.float32)
    return np.tile(cosine, (1, 4)), np.tile(np.concatenate([-sine, sine], axis=1), (1, 2))


NT=(((1,),(1,)),((),()))
NN=(((1,),(0,)),((),()))
TN=(((0,),(0,)),((),()))

def mm(a,b,dims=NN):
    return lax.dot_general(a,b,dims,preferred_element_type=F32)

def swap_halves(x):
    lane=lax.broadcasted_iota(jnp.int32,(x.shape[0],128),1)
    low=(lane%HD)<HD//2
    parts=[]
    for c in range(x.shape[1]//128):
        g=x[:,c*128:(c+1)*128]
        parts.append(jnp.where(low,pltpu.roll(g,128-HD//2,1),pltpu.roll(g,HD//2,1)))
    return jnp.concatenate(parts,axis=1)

def bias_block(seg_row, keys, first):
    n=seg_row.shape[1]
    s=lax.broadcasted_iota(jnp.int32,(keys,n),0)
    t=lax.broadcasted_iota(jnp.int32,(keys,n),1)+first
    return jnp.where((s<=t)&(s>=seg_row),0.0,masked_score)

MESH=pl.DeviceIdType.MESH
CORE = 1
GATHER_ORDERS = ((2, 4, 8), (4, 8, 2), (8, 2, 4))
SUM_ORDERS = ((4, 2, 8), (2, 4, 8))

def member_r():
    return lax.axis_index("rh") * 2 + lax.axis_index("rl")

def device_at(q, r, e):
    return (q, r // 2, r % 2, e)

def place_at(q, r):
    return q * QUAD + r

def flip(value, mask):
    low, high = value % 2, value // 2
    if mask & 1:
        low = 1 - low
    if mask & 2:
        high = 1 - high
    return high * 2 + low

def group_device(mask):
    return device_at(lax.axis_index("q"), flip(member_r(), mask >> 2), flip(lax.axis_index("expert"), mask & 3))

def group_member(mask):
    return flip(member_r(), mask >> 2) * 4 + flip(lax.axis_index("expert"), mask & 3)

def greet_devices(devices):
    barrier = pltpu.get_barrier_semaphore()
    for device in devices:
        pl.semaphore_signal(barrier, inc=1, device_id=device, device_id_type=MESH)
    pl.semaphore_wait(barrier, len(devices))

def greet(masks):
    greet_devices([group_device(mask) for mask in masks])

DM_ORDERS = ((2, 4, 8), (2, 8, 4))

def last_hop(order, mask):
    if mask & CORE:
        return CORE
    return [bit for bit in order if mask & bit][-1]

def block_copies(own_ref, held_ref, orders, send, recv):
    part_width = own_ref.shape[1] // len(orders)
    copies = {}
    for p, order in enumerate(orders):
        columns = pl.ds(p * part_width, part_width)
        for mask in range(1, 16):
            hop = last_hop(order, mask)
            source = own_ref.at[:, columns] if mask == hop else held_ref.at[mask ^ hop, :, columns]
            copies[p, mask] = pltpu.make_async_remote_copy(source, held_ref.at[mask, :, columns], send.at[p, mask], recv.at[p, mask],
                device_id=group_device(hop), device_id_type=MESH)
    return copies

def block_start(copies, orders, arrived):
    p, mask = arrived
    for nxt in range(1, 16):
        if nxt != mask and nxt ^ last_hop(orders[p], nxt) == mask:
            copies[p, nxt].start()

def gather_order(orders):
    parts = range(len(orders))
    free = {2: 0.0, 4: 0.0, 8: 0.0}
    arrived, todo = {(p, 0): 0.0 for p in parts}, [(p, m) for p in parts for m in range(2, 16, 2)]
    order = []
    while todo:
        best = None
        for p, m in todo:
            hop = last_hop(orders[p], m)
            if (p, m ^ hop) in arrived:
                key = (max(free[hop], arrived[p, m ^ hop]), orders[p].index(hop), p, m)
                if best is None or key < best:
                    best = key
        start, _, p, m = best
        hop = last_hop(orders[p], m)
        free[hop] = start + 1
        arrived[p, m] = start + 1
        todo.remove((p, m))
        order.append((start + 1, p, m))
    return [(p, m) for _, p, m in sorted(order)]

def one_hot(table, capacity, slots):
    place = lax.broadcasted_iota(jnp.int32, (capacity, table.shape[1]), 0).astype(F32)
    return [table[k:k + 1, :] == place for k in range(slots)]

def gather_kernel(slots, capacity, h2_ref, table_ref, dm_ref, rows_ref, dm_rows_ref, weight_ref, tables_ref,
                  held, arrived, dm_held, send, recv, table_send, table_recv, dm_sem):
    width = h2_ref.shape[1]
    part_width = width // len(GATHER_ORDERS)
    greet(range(1, 16))
    tables = []
    for mask in range(1, 16):
        copy = pltpu.make_async_remote_copy(table_ref.at[group_member(mask)], arrived.at[mask],
            table_send.at[mask], table_recv.at[mask], device_id=group_device(mask), device_id_type=MESH)
        copy.start()
        tables.append(copy)
    arrived[0] = table_ref[group_member(0)]
    copies = block_copies(h2_ref, held, GATHER_ORDERS, send, recv)
    order = gather_order(GATHER_ORDERS)
    for p, mask in order + [(p, CORE) for p in range(len(GATHER_ORDERS))]:
        if mask == last_hop(GATHER_ORDERS[p], mask):
            copies[p, mask].start()
    def dm_copy(mask):
        return pltpu.make_async_copy(dm_ref.at[mask], dm_held.at[mask % 2], dm_sem.at[mask % 2])
    dm_copy(0).start()
    for copy in tables:
        copy.wait_recv()
    def hots(mask):
        return one_hot(arrived[mask], capacity, slots)
    def place(target, mask, hot, block, columns):
        got = mm(jnp.concatenate([h.astype(BF16) for h in hot], axis=0), block).astype(BF16)
        for k in range(slots):
            target[k, pl.ds(mask * capacity, capacity), columns] = got[k * capacity:(k + 1) * capacity]
    def dm_step(mask):
        if mask + 1 < 16:
            dm_copy(mask + 1).start()
        dm_copy(mask).wait()
        hot = hots(mask)
        place(dm_rows_ref, mask, hot, dm_held[mask % 2], slice(None))
        if mask == 0:
            place(rows_ref, 0, hot, h2_ref[...], slice(None))
        table = arrived[mask]
        for k in range(slots):
            weight_ref[k, pl.ds(mask * capacity, capacity), :] = jnp.sum(
                jnp.where(hot[k], table[4 + k:5 + k, :], 0.0), axis=1, keepdims=True)
        tables_ref[mask] = table
    todo = list(range(16))
    dm_step(todo.pop(0))
    dm_step(todo.pop(0))
    def arrive(p, mask):
        copies[p, mask].wait_recv()
        block_start(copies, GATHER_ORDERS, (p, mask))
        columns = pl.ds(p * part_width, part_width)
        place(rows_ref, mask, hots(mask), held[mask, :, columns], columns)
    for step, (p, mask) in enumerate(order):
        arrive(p, mask)
        if todo:
            dm_step(todo.pop(0))
    for p in range(len(GATHER_ORDERS)):
        arrive(p, CORE)
    for p, mask in order:
        arrive(p, mask | CORE)
    for copy in tables:
        copy.wait_send()
    for key in copies:
        copies[key].wait_send()

def gather_rows(h2, table, dm_all, slots, capacity, collective_id):
    tokens, width = h2.shape
    V = pl.BlockSpec(memory_space=pltpu.VMEM)
    rows = jax.ShapeDtypeStruct((slots, 16 * capacity, width), BF16)
    return pl.pallas_call(functools.partial(gather_kernel, slots, capacity),
        out_shape=(rows, rows, jax.ShapeDtypeStruct((slots, 16 * capacity, 1), F32), jax.ShapeDtypeStruct(table.shape, F32)),
        in_specs=[V, V, pl.BlockSpec(memory_space=pl.ANY)], out_specs=(V,) * 4,
        scratch_shapes=[pltpu.VMEM((16, tokens, width), BF16), pltpu.VMEM(table.shape, F32),
            pltpu.VMEM((2, tokens, width), BF16), pltpu.SemaphoreType.DMA((len(GATHER_ORDERS), 16)), pltpu.SemaphoreType.DMA((len(GATHER_ORDERS), 16)),
            pltpu.SemaphoreType.DMA((16,)), pltpu.SemaphoreType.DMA((16,)), pltpu.SemaphoreType.DMA((2,))],
        compiler_params=pltpu.CompilerParams(vmem_limit_bytes=58 << 20, collective_id=collective_id, has_side_effects=True),
        cost_estimate=CHEAP,
        name="gather_rows")(h2, table, dm_all)

def expert_kernel(chunks, dp, ways, s_ref, x_ref, dm_ref, weight_ref, wg_ref, wu_ref, wd_ref,
                  y_ref, dr_ref, dg_ref, grads, xs, dms, mgs, das, *banks):
    i = pl.program_id(1)
    block = x_ref.shape[1]
    if ways > 1:
        wg, wu, wd = banks
        ff = wg.shape[1]
        part = ff // dp
        @pl.when(i == 0)
        def _():
            shape = (ff * ways, ff)
            row, col = lax.broadcasted_iota(jnp.int32, shape, 0), lax.broadcasted_iota(jnp.int32, shape, 1)
            pick = (row == (col // part * ways + s_ref[s_ref.shape[0] - 1]) * part + col % part).astype(F32).astype(BF16)
            wg[...] = mm(wg_ref[0], pick).astype(BF16)
            wu[...] = mm(wu_ref[0], pick).astype(BF16)
            wd[...] = mm(pick, wd_ref[0], TN).astype(BF16)
    else:
        wg, wu, wd = wg_ref.at[0], wu_ref.at[0], wd_ref.at[0]
        ff = wg.shape[1]
    @pl.when(i < chunks)
    def _():
        x, dmr, w = x_ref[0], dm_ref[0], weight_ref[0]
        rows = pl.ds(pl.multiple_of(i * block, block), block)
        xs[rows, :] = x
        dms[rows, :] = dmr
        ga = mm(x, wg[...])
        ua = mm(x, wu[...])
        u = mm(dmr, wd[...], NT)
        sig = 1.0 / (1.0 + jnp.exp(-ga))
        silu = ga * sig
        m = silu * ua
        mg = (m * w).astype(BF16)
        dg_ref[0] = jnp.sum(m * u, axis=1, keepdims=True)
        dmh = u * w
        da = (dmh * ua * (sig * (1.0 + ga * (1.0 - sig)))).astype(BF16)
        du = (dmh * silu).astype(BF16)
        mgs[rows, :] = mg
        das[rows, :ff] = da
        das[rows, ff:] = du
        y_ref[0] = mm(mg, wd[...]).astype(BF16)
        dr_ref[0] = (mm(da, wg[...], NT) + mm(du, wu[...], NT)).astype(BF16)
    @pl.when(i == chunks)
    def _():
        width = xs.shape[1]
        share, down_share = width // dp, ff // dp
        for half in range(2):
            grad = mm(xs[...], das[:, half * ff:(half + 1) * ff], TN).astype(BF16)
            for d in range(dp):
                grads[d, 0, half * share:(half + 1) * share, :] = grad[d * share:(d + 1) * share]
        down = mm(mgs[...], dms[...], TN).astype(BF16)
        for d in range(dp):
            for c in range(width // ff):
                first = 2 * share + c * down_share
                grads[d, 0, first:first + down_share, :] = down[d * down_share:(d + 1) * down_share, c * ff:(c + 1) * ff]

def expert_call(rows, dm_rows, weight, first, count, w_gate, w_up, w_down, scalars, dp, ways, block=512):
    _, total, width = rows.shape
    ff = w_gate.shape[2] // ways
    chunks = total // block
    row = lambda n, i, s: (first + n, jnp.minimum(i, chunks - 1), 0)
    out = lambda n, i, s: (n, jnp.minimum(i, chunks - 1), 0)
    bank = lambda a: pl.BlockSpec((1,) + a.shape[1:], lambda n, i, s: (s[n], 0, 0))
    share = width // dp
    S, M = jax.ShapeDtypeStruct, pltpu.VMEM
    return pl.pallas_call(functools.partial(expert_kernel, chunks, dp, ways),
        grid_spec=pltpu.PrefetchScalarGridSpec(num_scalar_prefetch=1, grid=(count, chunks + 1),
            in_specs=[pl.BlockSpec((1, block, width), row), pl.BlockSpec((1, block, width), row), pl.BlockSpec((1, block, 1), row),
                bank(w_gate), bank(w_up), bank(w_down)],
            out_specs=(pl.BlockSpec((1, block, width), out), pl.BlockSpec((1, block, width), out), pl.BlockSpec((1, block, 1), out),
                pl.BlockSpec((dp, 1, 3 * share, ff), lambda n, i, s: (0, n, 0, 0))),
            scratch_shapes=[M((total, width), BF16), M((total, width), BF16), M((total, ff), BF16), M((total, 2 * ff), BF16)]
                + ([M((width, ff), BF16), M((width, ff), BF16), M((ff, width), BF16)] if ways > 1 else [])),
        out_shape=(S((count, total, width), BF16), S((count, total, width), BF16), S((count, total, 1), F32),
            S((dp, count, 3 * share, ff), BF16)),
        compiler_params=pltpu.CompilerParams(vmem_limit_bytes=58 << 20, dimension_semantics=("arbitrary", "arbitrary")),
        cost_estimate=CHEAP,
        name="expert_part" if ways > 1 else "experts")(scalars, rows, dm_rows, weight, w_gate, w_up, w_down)

def place_kernel(whole, rest, ways, order_ref, *refs):
    moved, (gate_ref, up_ref, down_ref) = refs[:-3], refs[-3:]
    i = pl.program_id(0)
    share, down_share = gate_ref.shape[1], down_ref.shape[1]
    width, ff = down_ref.shape[2], gate_ref.shape[2]
    quads = moved[0].shape[2]
    @pl.when(i < QUAD)
    def _():
        for s in range(whole):
            block = sum(moved[0][s, 0, k].astype(F32) for k in range(quads))
            gate_ref[s] = block[:share]
            up_ref[s] = block[share:2 * share]
            for c in range(width // ff):
                first = 2 * share + c * down_share
                down_ref[s, :, c * ff:(c + 1) * ff] = block[first:first + down_share]
    if rest:
        @pl.when(i == QUAD)
        def _():
            cols = ff // ways
            part = down_share // ways
            for x in range(rest):
                gate = jnp.zeros((2 * share, ff), F32)
                for h in range(ways):
                    col = lax.broadcasted_iota(jnp.int32, (cols, ff), 0)
                    spot = (col // part * ways + h) * part + col % part
                    pick = (lax.broadcasted_iota(jnp.int32, (cols, ff), 1) == spot).astype(F32).astype(BF16)
                    down = jnp.zeros((share, cols), F32)
                    for k in range(quads):
                        block = moved[1][k, x * ways + h, 0]
                        gate = gate + mm(block[:2 * share], pick)
                        down = down + block[2 * share:].astype(F32)
                    for c in range(width // cols):
                        down_ref[x, h * part:(h + 1) * part, c * cols:(c + 1) * cols] = down[c * part:(c + 1) * part]
                gate_ref[x] = gate[:share]
                up_ref[x] = gate[share:]

def place_call(moved, shared, order, local, ffn, width):
    whole, _, quads, rows, _ = moved.shape
    rest = local - whole * QUAD
    ways = QUAD // rest if rest else 1
    share = rows // 3
    down_share = ffn * share // width
    shared = [a.reshape((quads, QUAD) + a.shape[1:]) for a in shared]
    full = lambda a: pl.BlockSpec(a.shape, lambda i, s: (0, 0, 0, 0, 0))
    out = lambda a, b: pl.BlockSpec((whole, a, b), lambda i, s: (i, 0, 0))
    S = jax.ShapeDtypeStruct
    return pl.pallas_call(functools.partial(place_kernel, whole, rest, ways),
        grid_spec=pltpu.PrefetchScalarGridSpec(num_scalar_prefetch=1, grid=(QUAD + (1 if rest else 0),),
            in_specs=[pl.BlockSpec((whole, 1, quads, rows, ffn), lambda i, s: (0, s[jnp.minimum(i, QUAD - 1)], 0, 0, 0))]
                + [full(a) for a in shared],
            out_specs=(out(share, ffn), out(share, ffn), out(down_share, width))),
        out_shape=(S((local, share, ffn), F32), S((local, share, ffn), F32), S((local, down_share, width), F32)),
        compiler_params=pltpu.CompilerParams(vmem_limit_bytes=58 << 20, dimension_semantics=("arbitrary",)),
        cost_estimate=CHEAP, name="place_gradients")(order, moved, *shared)

def relative_device(k, m):
    return device_at((lax.axis_index("q") + k) % lax.axis_size("q"), flip(member_r(), m), lax.axis_index("expert"))

def carry_keys(quads, slots, with_x):
    ms = (1, 3) if with_x else (0, 2)
    return [(s, k, m) for s in slots for m in ms for k in range(quads) if (k, m) != (0, 0)]

def carry_copies(grads_ref, moved_ref, keys, send, recv):
    quads = lax.axis_size("q")
    copies = []
    for s, k, m in keys:
        q, r = (lax.axis_index("q") + k) % quads, flip(member_r(), m)
        copies.append(pltpu.make_async_remote_copy(grads_ref.at[place_at(q, r), s], moved_ref.at[s, m, (quads - k) % quads],
            send.at[s, m, k], recv.at[s, m, (quads - k) % quads], device_id=relative_device(k, m), device_id_type=MESH))
    return copies

def carry_start(copies, keys, late):
    outer = lax.axis_index("q") % 2 == lax.axis_index("rh")
    for copy, (_, k, _m) in zip(copies, keys):
        if not k:
            if not late:
                copy.start()
        elif late:
            pl.when(jnp.logical_not(outer))(copy.start)
        else:
            pl.when(outer)(copy.start)

def carry_plan(quads, whole):
    z, x = carry_keys(quads, range(whole), False), carry_keys(quads, range(whole), True)
    first = [key for key in z if key[0] == 0]
    second = [key for key in x if key[0] == 0 or key[1] == 0] + [key for key in z if key[0] and (key[1] == 0 or key[2] == 0)]
    third = [key for key in x + z if key not in first and key not in second]
    return first, second, third

def first_hop(part, mask):
    return [bit for bit in SUM_ORDERS[part] if mask & bit][0]

def combine_kernel(banks, slots, capacity, with_dg, carried, *refs):
    rows, refs = refs[:banks], refs[banks:]
    tables_ref, refs = refs[0], refs[1:]
    if with_dg:
        dg_refs, grads_ref, refs = refs[:banks], refs[banks], refs[banks + 1:]
        out_ref, dg_out, moved_ref, refs = refs[0], refs[1], refs[2], refs[3:]
    else:
        middle_ref, grads_ref, _, out_ref, moved_ref, refs = refs[0], refs[1], refs[2], refs[3], refs[4], refs[5:]
    core_out, core_in, held, got, core_send, core_recv, send, recv, carry_send, carry_recv, own_sem = refs[:11]
    if with_dg:
        dg_hold, dg_in, dg_send, dg_recv = refs[11:]
    width = out_ref.shape[1]
    part_width = width // len(SUM_ORDERS)
    masks = list(range(1, 16)) if with_dg else [1, 2, 4, 8]
    far = sorted({(k, m) for _, k, m in carried if k or m * 4 not in masks})
    greet_devices([group_device(mask) for mask in masks] + [relative_device(k, m) for k, m in far])
    carries = carry_copies(grads_ref, moved_ref, carried, carry_send, carry_recv)
    straight = [n for n, key in enumerate(carried) if not key[2] & 1]
    turning = [n for n, key in enumerate(carried) if key[2] & 1]
    def carry(chosen, late):
        carry_start([carries[n] for n in chosen], [carried[n] for n in chosen], late)
    carry(straight, False)
    own_copies = []
    if with_dg:
        for s in range(moved_ref.shape[0]):
            own_copies.append(pltpu.make_async_copy(grads_ref.at[place_at(lax.axis_index("q"), member_r()), s],
                moved_ref.at[s, 0, 0], own_sem.at[s]))
            own_copies[-1].start()
    def hots(mask):
        return one_hot(tables_ref[mask], capacity, slots)
    def block_sum(mask, hot):
        return mm(jnp.concatenate([h.astype(BF16) for h in hot], axis=0),
            jnp.concatenate([a[n, pl.ds(mask * capacity, capacity), :] for a in rows for n in range(a.shape[0])], axis=0), TN)
    dg_copies = []
    def dg_step(mask, hot):
        if not with_dg:
            return
        for k in range(slots):
            col = [(a, n) for a in dg_refs for n in range(a.shape[0])][k]
            col = col[0][col[1], pl.ds(mask * capacity, capacity), :]
            dg_hold[mask, k:k + 1, :] = jnp.sum(jnp.where(hot[k], col, 0.0), axis=0, keepdims=True)
        if mask == 0:
            return
        copy = pltpu.make_async_remote_copy(dg_hold.at[mask], dg_in.at[mask], dg_send.at[mask], dg_recv.at[mask],
            device_id=group_device(mask), device_id_type=MESH)
        copy.start()
        dg_copies.append(copy)
    listed = sorted(range(0, 16, 2), key=lambda m: (-bin(m).count("1"), m))
    if with_dg:
        dg_hold[...] = jnp.zeros_like(dg_hold)
    core = {}
    for mask in listed:
        hot = hots(mask | CORE)
        core_out[mask // 2] = block_sum(mask | CORE, hot).astype(BF16)
        core[mask] = pltpu.make_async_remote_copy(core_out.at[mask // 2], core_in.at[mask // 2], core_send.at[mask // 2],
            core_recv.at[mask // 2], device_id=group_device(CORE), device_id_type=MESH)
        core[mask].start()
        dg_step(mask | CORE, hot)
    copies = {}
    for p in range(len(SUM_ORDERS)):
        for mask in range(2, 16, 2):
            copies[p, mask] = pltpu.make_async_remote_copy(held.at[p, mask // 2], got.at[p, mask // 2], send.at[p, mask // 2],
                recv.at[p, mask // 2], device_id=group_device(first_hop(p, mask)), device_id_type=MESH)
    for mask in listed:
        hot = hots(mask)
        own = block_sum(mask, hot)
        core[mask].wait_recv()
        own = (own + core_in[mask // 2].astype(F32)).astype(BF16)
        for p in range(len(SUM_ORDERS)):
            held[p, mask // 2] = own[:, p * part_width:(p + 1) * part_width]
            if mask & SUM_ORDERS[p][0]:
                copies[p, mask].start()
        dg_step(mask, hot)
    carry(turning, False)
    carry(straight + turning, True)
    def add(p, target, sources):
        total = held[p, target // 2].astype(F32)
        for source in sources:
            copies[p, source].wait_recv()
            total = total + got[p, source // 2].astype(F32)
        return total
    def forward(p, target, sources):
        held[p, target // 2] = add(p, target, sources).astype(BF16)
        copies[p, target].start()
    for both in (True, False):
        for p in range(len(SUM_ORDERS)):
            a, b, c = SUM_ORDERS[p]
            target = b | c if both else b
            forward(p, target, [target | a])
    for p in range(len(SUM_ORDERS)):
        a, b, c = SUM_ORDERS[p]
        forward(p, c, [c | a, c | b])
    for p in range(len(SUM_ORDERS)):
        a, b, c = SUM_ORDERS[p]
        columns = pl.ds(p * part_width, part_width)
        total = add(p, 0, [a, b, c])
        out_ref[:, columns] = total if with_dg else (middle_ref[:, columns] + total).astype(BF16)
    if with_dg:
        dg_out[0] = dg_hold[0]
        for copy in dg_copies:
            copy.wait_recv()
        for mask in range(1, 16):
            dg_out[mask] = dg_in[mask]
        for copy in dg_copies:
            copy.wait_send()
    for mask in listed:
        core[mask].wait_send()
    for key in copies:
        copies[key].wait_send()
    for copy in carries:
        copy.wait()
    for copy in own_copies:
        copy.wait()

def combine_rows(rows, tables, dgs, middle, grads, moved, carried, capacity, collective_id):
    banks, slots = len(rows), sum(a.shape[0] for a in rows)
    tokens, width = tables.shape[2], rows[0].shape[2]
    V, A = pl.BlockSpec(memory_space=pltpu.VMEM), pl.BlockSpec(memory_space=pl.ANY)
    with_dg = dgs is not None
    quads, whole = grads.shape[0] // QUAD, grads.shape[1]
    out = jax.ShapeDtypeStruct((tokens, width), F32 if with_dg else BF16)
    moved_shape = jax.ShapeDtypeStruct((whole, QUAD, quads) + grads.shape[2:], grads.dtype)
    table = pltpu.VMEM(tables.shape, F32)
    sem = pltpu.SemaphoreType.DMA
    parts = len(SUM_ORDERS)
    operands = list(rows) + [tables] + (list(dgs) + [grads] if with_dg else [middle, grads, moved])
    return pl.pallas_call(functools.partial(combine_kernel, banks, slots, capacity, with_dg, carried),
        out_shape=(out, jax.ShapeDtypeStruct(tables.shape, F32), moved_shape) if with_dg else (out, moved_shape),
        in_specs=[V] * (banks + 1 + (banks if with_dg else 1)) + [A] * (1 if with_dg else 2),
        out_specs=(V, V, A) if with_dg else (V, A),
        input_output_aliases={} if with_dg else {banks + 3: 1},
        scratch_shapes=[pltpu.VMEM((8, tokens, width), BF16), pltpu.VMEM((8, tokens, width), BF16),
            pltpu.VMEM((parts, 8, tokens, width // parts), BF16), pltpu.VMEM((parts, 8, tokens, width // parts), BF16),
            sem((8,)), sem((8,)), sem((parts, 8)), sem((parts, 8)), sem((whole, QUAD, quads)), sem((whole, QUAD, quads)), sem((whole,))]
            + ([table, table, sem((16,)), sem((16,))] if with_dg else []),
        compiler_params=pltpu.CompilerParams(vmem_limit_bytes=58 << 20, collective_id=collective_id, has_side_effects=True),
        cost_estimate=CHEAP,
        name="combine_with_dg" if with_dg else "combine_rows")(*operands)

DP_ORDERS = (("q", 1, 2), ("q", 2, 1), ("q", 2, 1))


def device_experts(local, r):
    whole = local // QUAD
    rest = local - whole * QUAD
    return [r * whole + s for s in range(whole)] + ([QUAD * whole + r // (QUAD // rest)] if rest else [])


def dp_last(part, k, m):
    return [dim for dim in DP_ORDERS[part] if (k if dim == "q" else m & dim)][-1]

def dp_source(part, k, m):
    dim = dp_last(part, k, m)
    return (0, m) if dim == "q" else (k, m ^ dim)

def dp_origin(k, m):
    return place_at((lax.axis_index("q") + k) % lax.axis_size("q"), flip(member_r(), m))

def dp_copies(ref, rows, first, part_width, send, recv):
    quads = lax.axis_size("q")
    copies = {}
    for p in range(3):
        columns = pl.ds(p * part_width, part_width)
        for k in range(quads):
            for m in range(QUAD):
                if (k, m) == (0, 0):
                    continue
                dim = dp_last(p, k, m)
                block = ref.at[pl.ds(first(dp_origin(*dp_source(p, k, m))), rows), columns]
                q, r, e = lax.axis_index("q"), member_r(), lax.axis_index("expert")
                device = device_at((q + quads - k) % quads, r, e) if dim == "q" else device_at(q, flip(r, dim), e)
                copies[p, k, m] = pltpu.make_async_remote_copy(block, block, send.at[p, k, m], recv.at[p, k, m],
                    device_id=device, device_id_type=MESH)
    return copies

def dp_order(copies):
    def hops(key):
        p, k, m = key
        return (1 if k else 0) + bin(m).count("1")
    return sorted(copies, key=lambda key: (hops(key), DP_ORDERS[key[0]].index(dp_last(*key)), key[0], key))

def dp_start(copies, arrived):
    for key in dp_order(copies):
        if arrived[0] == key[0] and dp_source(*key) == arrived[1:]:
            copies[key].start()

def start_kernel(dims, exchange, *refs):
    (experts, capacity, top_count, q_cols, k_cols, rows_here, shard_rows) = dims
    (tokens_ref, pieces_ref, wout_ref, cot_ref, routes_ref, priority_ref, seg_ref, cos_ref, sin_ref,
     x_out, w_out, wout_out, h1_ref, q_ref, k_ref, v_ref, o_ref, lse_ref, middle_ref, h2_ref, table_ref, probs_ref, gains_ref, dm_ref,
     xs, ws, wouts, vt_ref, h1s, os, own_sem,
     x_send, x_recv, p_send, p_recv, w_send, w_recv, o_send, o_recv, wo_send, wo_recv, wx_send, wx_recv, dm_send, dm_recv, dm_sem) = refs
    E = lax.axis_size("expert")
    quads = lax.axis_size("q")
    dp = quads * QUAD
    q, r, e = lax.axis_index("q"), member_r(), lax.axis_index("expert")
    place = place_at(q, r)
    length, width = xs.shape
    total = ws.shape[1]
    block_rows = ws.shape[0] // dp
    heads, kv_heads = q_cols // HD, k_cols // HD
    group = heads // kv_heads
    block = 256

    barrier = pltpu.get_barrier_semaphore()
    friends = [device_at(q, r, flip(e, j)) for j in (1, 2, 3)] + [device_at(q, flip(r, m), e) for m in (1, 2)]
    friends += [device_at((q + k) % quads, r, e) for k in range(1, quads)]
    dm_copies = block_copies(cot_ref, dm_ref, DM_ORDERS, dm_send, dm_recv)
    dm_order = gather_order(DM_ORDERS)
    def dm_arrive(wanted):
        for key in wanted:
            dm_copies[key].wait_recv()
            block_start(dm_copies, DM_ORDERS, key)
    for friend in friends:
        pl.semaphore_signal(barrier, inc=1, device_id=friend, device_id_type=MESH)
    pl.semaphore_wait(barrier, len(friends))

    def token_rows(who):
        return pl.ds(pl.multiple_of(who * rows_here, 16), rows_here)

    x_copies = {}
    for j in (1, 2, 3):
        source = tokens_ref if j < 3 else xs.at[token_rows(flip(e, 2))]
        target = e if j < 3 else flip(e, 2)
        x_copies[j] = pltpu.make_async_remote_copy(source, xs.at[token_rows(target)], x_send.at[j], x_recv.at[j],
            device_id=device_at(q, r, flip(e, j if j < 3 else 1)), device_id_type=MESH)
    p_copies = []
    mine = pl.multiple_of(place * block_rows, 16)
    if exchange:
        for j in (1, 2, 3):
            rows = pl.ds(pl.multiple_of(place * block_rows + e * shard_rows, 16), shard_rows)
            copy = pltpu.make_async_remote_copy(pieces_ref.at[flip(e, j)], ws.at[rows], p_send.at[j], p_recv.at[j],
                device_id=device_at(q, r, flip(e, j)), device_id_type=MESH)
            copy.start()
            p_copies.append(copy)
        ws[pl.ds(pl.multiple_of(place * block_rows + e * shard_rows, 16), shard_rows), :] = pieces_ref[e]
    else:
        ws[pl.ds(mine, block_rows), :] = pieces_ref[...]
    x_copies[2].start()
    x_copies[1].start()
    for p in range(len(DM_ORDERS)):
        dm_copies[p, 2].start()
        dm_copies[p, CORE].start()
    dm_own = pltpu.make_async_copy(cot_ref, dm_ref.at[0], dm_sem)
    dm_own.start()
    xs[token_rows(e), :] = tokens_ref[...]
    w_copies = dp_copies(ws, block_rows, lambda d: pl.multiple_of(d * block_rows, 16), total // 3, w_send, w_recv)
    for copy in p_copies:
        copy.wait_recv()
    for p in range(3):
        dp_start(w_copies, (p, 0, 0))
    wo_copies = {}
    if exchange:
        def out_row(d):
            return pl.multiple_of((d * E + e) * shard_rows, 16)
        wouts[pl.ds(out_row(place), shard_rows), :] = wout_ref[...]
        wo_copies = dp_copies(wouts, shard_rows, out_row, width // 3, wo_send, wo_recv)
        for p in range(3):
            dp_start(wo_copies, (p, 0, 0))

    lane = lax.broadcasted_iota(jnp.int32, (rows_here, 128), 1)
    rank = jnp.zeros((rows_here, 128), jnp.int32)
    routes, priority = routes_ref[...].T, priority_ref[...].T
    for j in range(top_count):
        rank = rank + jnp.where(routes[:, j:j + 1] == lane, priority[:, j:j + 1] + 1, 0)
    rank = rank - 1
    before = (lax.broadcasted_iota(jnp.int32, (rows_here, rows_here), 1)
              < lax.broadcasted_iota(jnp.int32, (rows_here, rows_here), 0)).astype(F32).astype(BF16)
    base = jnp.zeros((1, 128), F32)
    slot = jnp.zeros((rows_here, 128), F32)
    for level in range(top_count):
        hot = (rank == level).astype(F32)
        slot = slot + hot * (base + mm(before, hot.astype(BF16)))
        base = base + jnp.sum(hot, axis=0, keepdims=True)
    named = rank >= 0
    slot = jnp.where(named & (slot < capacity), slot, -1.0)

    x_copies[2].wait_recv()
    x_copies[3].start()
    order = dp_order(w_copies)
    wo_order = dp_order(wo_copies)
    for key in order:
        w_copies[key].wait_recv()
        dp_start(w_copies, key)
    x_copies[1].wait_recv()
    x_copies[3].wait_recv()
    x_back = pltpu.make_async_copy(xs, x_out, own_sem.at[0])
    w_back = pltpu.make_async_copy(ws, w_out, own_sem.at[1])
    x_back.start()
    w_back.start()
    wx_copies = {}
    if exchange:
        for d in range(dp):
            for j in (1, 2, 3):
                owner = e if j < 3 else flip(e, 2)
                rows = pl.ds(pl.multiple_of((d * E + owner) * shard_rows, 16), shard_rows)
                wx_copies[d, j] = pltpu.make_async_remote_copy(wouts.at[rows], wouts.at[rows], wx_send.at[d, j], wx_recv.at[d, j],
                    device_id=device_at(q, r, flip(e, j if j < 3 else 1)), device_id_type=MESH)
    def out_step(step):
        if step == 2:
            dm_arrive([key for key in dm_order if key[1] == 2])
        if step == 4:
            dm_arrive([key for key in dm_order if key[1] in (4, 8)])
        if not exchange:
            if step == 1:
                for p, (_, b, c) in enumerate(DM_ORDERS):
                    dm_copies[p, b].start()
                    dm_copies[p, c].start()
            return
        third = -(-len(wo_order) // 2)
        if step < 2:
            for key in wo_order[step * third:(step + 1) * third]:
                wo_copies[key].wait_recv()
                dp_start(wo_copies, key)
        if step == 1:
            for p, (_, b, c) in enumerate(DM_ORDERS):
                dm_copies[p, b].start()
            for p, (_, b, c) in enumerate(DM_ORDERS):
                dm_copies[p, c].start()
            for d in range(dp):
                wx_copies[d, 2].start()
            for d in range(dp):
                wx_copies[d, 1].start()
        if step == 3:
            for d in range(dp):
                wx_copies[d, 2].wait_recv()
                wx_copies[d, 3].start()

    small = ws[:, total - 128:].astype(F32).T
    gain_attn = small[experts:experts + 1, :]
    gain_moe = small[experts + 1:experts + 2, :]
    gains_ref[0:1, :] = gain_attn
    gains_ref[1:2, :] = gain_moe

    def send_block(b):
        rows = pl.ds(b * rows_here, rows_here)
        @pl.when(e == b)
        def _():
            os[b] = o_ref[rows, :]
        @pl.when(e != b)
        def _():
            pltpu.make_async_remote_copy(o_ref.at[rows], os.at[e], o_send.at[b], o_recv.at[e],
                device_id=device_at(q, r, b), device_id_type=MESH).start()
    sent = 0
    for i in range(length // block):
        rows = pl.ds(i * block, block)
        x = xs[rows, :].astype(F32)
        scale = lax.rsqrt(jnp.mean(x * x, axis=1, keepdims=True) + epsilon)
        h1 = (x * scale * gain_attn).astype(BF16)
        h1s[rows, :] = h1
        qkv = mm(h1, ws[:, :total - 128])
        qk = qkv[:, :q_cols + k_cols]
        turns = (q_cols + k_cols) // 128
        cosine = jnp.concatenate([cos_ref[rows, :]] * turns, axis=1)
        sine = jnp.concatenate([sin_ref[rows, :]] * turns, axis=1)
        qk = (qk * cosine + swap_halves(qk) * sine).astype(BF16)
        v = qkv[:, q_cols + k_cols:].astype(BF16)
        for h in range(heads):
            q_ref[h, rows, :] = qk[:, h * HD:(h + 1) * HD]
        vt = v.astype(F32).T.astype(BF16)
        for h in range(kv_heads):
            k_ref[h, rows, :] = qk[:, q_cols + h * HD:q_cols + (h + 1) * HD]
            v_ref[h, rows, :] = v[:, h * HD:(h + 1) * HD]
            vt_ref[h, :, rows] = vt[h * HD:(h + 1) * HD, :]
        keys = (i + 1) * block
        bias = bias_block(seg_ref[:, rows], keys, i * block)
        outs = []
        for h in range(heads):
            g = h // group
            st = mm(k_ref[g, pl.ds(0, keys), :], q_ref[h, rows, :] * BF16(HD ** -0.5), NT) + bias
            top = jnp.max(st, axis=0, keepdims=True)
            p = jnp.exp(st - top)
            sums = jnp.sum(p, axis=0, keepdims=True)
            outs.append(mm(vt_ref[g, :, pl.ds(0, keys)], p.astype(BF16)) / sums)
            lse_ref[pl.ds(h, 1), rows] = top + jnp.log(sums)
        o_ref[rows, :] = jnp.concatenate(outs, axis=0).T.astype(BF16)
        while sent < E and (sent + 1) * rows_here <= keys:
            send_block(sent)
            sent += 1
        out_step(i)
    h1_back = pltpu.make_async_copy(h1s, h1_ref, own_sem.at[2])
    h1_back.start()
    if exchange:
        for d in range(dp):
            wx_copies[d, 1].wait_recv()
            wx_copies[d, 3].wait_recv()
    else:
        fill = pltpu.make_async_copy(wout_ref, wouts, own_sem.at[3])
        fill.start()
        fill.wait()
    wout_back = pltpu.make_async_copy(wouts, wout_out, own_sem.at[3])
    wout_back.start()
    def o_descriptor(b):
        return pltpu.make_async_remote_copy(o_ref.at[pl.ds(0, rows_here)], os.at[b], o_send.at[b], o_recv.at[b],
            device_id=device_at(q, r, flip(e, 1)), device_id_type=MESH)
    middle = xs[token_rows(e), :].astype(F32)
    for b in range(E):
        @pl.when(e != b)
        def _():
            o_descriptor(b).wait_recv()
    for b in range(E):
        middle = middle + mm(os[b], wouts[b * q_cols:(b + 1) * q_cols, :])
    middle_ref[...] = middle
    scale = lax.rsqrt(jnp.mean(middle * middle, axis=1, keepdims=True) + epsilon)
    h2 = (middle * scale * gain_moe).astype(BF16)
    h2_ref[...] = h2
    logits = jnp.where(named, mm(h2, ws[:, total - 128:]), masked_score)
    powers = jnp.where(named, jnp.exp(logits - jnp.max(logits, axis=1, keepdims=True)), 0.0)
    probs = powers / jnp.sum(powers, axis=1, keepdims=True)
    probs_ref[...] = probs
    slot_rows = slot.T
    prob_rows = probs.T
    local = experts // E
    table_ref[...] = jnp.zeros_like(table_ref)
    for dest_r in range(QUAD):
        for dest_e in range(E):
            for at, expert in enumerate(device_experts(local, dest_r)):
                row = dest_e * local + expert
                table_ref[dest_r * E + dest_e, at:at + 1, :] = slot_rows[row:row + 1, :]
                table_ref[dest_r * E + dest_e, 4 + at:5 + at, :] = prob_rows[row:row + 1, :]
    dm_arrive([key for key in dm_order if key[1] not in (2, 4, 8)])
    for key in dm_copies:
        if key[1] & CORE:
            dm_copies[key].wait_recv()
    for key in dm_copies:
        dm_copies[key].wait_send()
    dm_own.wait()
    for b in range(E):
        @pl.when(e != b)
        def _():
            o_descriptor(b).wait_send()
    for copy in p_copies + list(x_copies.values()) + list(w_copies.values()) + list(wo_copies.values()) + list(wx_copies.values()):
        copy.wait_send()
    for copy in (x_back, w_back, h1_back, wout_back):
        copy.wait()

def start_call(tokens, pieces, w_out, cotangent, routes, priority, segments, cosine, sine, experts, capacity, q_cols, k_cols, exchange):
    E, quads = lax.axis_size("expert"), lax.axis_size("q")
    dp = quads * QUAD
    rows_here, width = tokens.shape
    length = rows_here * E
    shard_rows = width // (dp * E)
    total = pieces.shape[-1]
    V, A = pl.BlockSpec(memory_space=pltpu.VMEM), pl.BlockSpec(memory_space=pl.ANY)
    heads, kv_heads = q_cols // HD, k_cols // HD
    S = jax.ShapeDtypeStruct
    sem = pltpu.SemaphoreType.DMA
    dims = (experts, capacity, routes.shape[0], q_cols, k_cols, rows_here, shard_rows)
    kernel = functools.partial(start_kernel, dims, exchange)
    return pl.pallas_call(kernel,
        out_shape=(S((length, width), BF16), S((width, total), BF16), S((width, width), BF16), S((length, width), BF16),
            S((heads, length, HD), BF16), S((kv_heads, length, HD), BF16), S((kv_heads, length, HD), BF16),
            S((length, q_cols), BF16), S((-(-heads // 8) * 8, length), F32), S((rows_here, width), F32), S((rows_here, width), BF16),
            S((QUAD * E, 8, rows_here), F32), S((rows_here, 128), F32), S((8, width), F32),
            S((QUAD * E, rows_here, width), BF16)),
        in_specs=[V, V, V if exchange else A, A, V, V, V, V, V], out_specs=(A, A, A, A) + (V,) * 10 + (A,),
        scratch_shapes=[pltpu.VMEM((length, width), BF16), pltpu.VMEM((width, total), BF16), pltpu.VMEM((width, width), BF16),
            pltpu.VMEM((kv_heads, HD, length), BF16), pltpu.VMEM((length, width), BF16), pltpu.VMEM((E, rows_here, q_cols), BF16), sem((4,)),
            sem((4,)), sem((4,)), sem((4,)), sem((4,)), sem((3, quads, QUAD)), sem((3, quads, QUAD)), sem((E,)), sem((E,)),
            sem((3, quads, QUAD)), sem((3, quads, QUAD)), sem((dp, 4)), sem((dp, 4)),
            sem((len(DM_ORDERS), 16)), sem((len(DM_ORDERS), 16)), sem],
        compiler_params=pltpu.CompilerParams(vmem_limit_bytes=58 << 20, collective_id=4, has_side_effects=True),
        cost_estimate=CHEAP,
        name="start")(tokens, pieces, w_out, cotangent, routes, priority, segments.reshape(1, -1), cosine, sine)


DENSE_ORDERS = ((1, 2, "q"), (2, 1, "q"))

def back_kernel(dims, exchange, carried, *refs):
    (experts, q_cols, k_cols, slots) = dims
    (dr_ref, dg_ref, probs_ref, h2_ref, middle_ref, cot_ref, gains_ref, tokens_ref, wout_ref, q_ref, k_ref, v_ref, lse_ref,
     cos_ref, sin_ref, seg_ref, h1_ref, xall_ref, wall_ref, mixed_ref, grads_ref, _) = refs[:22]
    refs = refs[22:]
    if exchange:
        (tokens_out, gq_ref, gk_ref, gv_ref, small_ref, gout_ref, moved_ref) = refs[:7]
        refs = refs[7:]
    else:
        (tokens_out, dense_ref, gout_ref, moved_ref) = refs[:4]
        refs = refs[4:]
    (h1s, xs, ws, mixeds, load_sem, dgt, dats, dos, do_out, kt_ref, dk_ref, dv_ref, dqkv, dx1s, small, part, core_in, y_in,
     g1, g2, r1, r2, f1,
     do_send, do_recv, dat_send, dat_recv, part_send, part_recv, g1_send, g1_recv, g2_send, g2_recv, f_send, f_recv, carry_send, carry_recv) = refs
    E, quads = lax.axis_size("expert"), lax.axis_size("q")
    q, r, e = lax.axis_index("q"), member_r(), lax.axis_index("expert")
    dp = quads * QUAD
    rows_here, width = dr_ref.shape
    length = rows_here * E
    heads, kv_heads = q_cols // HD, k_cols // HD
    group = heads // kv_heads
    total = ws.shape[1]
    qkv_cols = total - 128
    factor = HD ** -0.5
    block = 256
    loads = [pltpu.make_async_copy(a, b, load_sem.at[i])
             for i, (a, b) in enumerate(((wall_ref, ws), (mixed_ref, mixeds), (h1_ref, h1s), (xall_ref, xs.at[pl.ds(0, length)])))]
    load_out = pltpu.make_async_copy(wout_ref, xs, load_sem.at[4])
    load_out.start()
    for load in loads[:3]:
        load.start()
    near = [(0, 1), (0, 2)] + [(k, 0) for k in range(1, quads)]
    far = sorted({(k, m) for _, k, m in carried} - set(near))
    greet_devices([device_at(q, r, flip(e, j)) for j in (1, 2, 3)] + [relative_device(k, m) for k, m in near + far])
    carries = carry_copies(grads_ref, moved_ref, carried, carry_send, carry_recv)
    carry_start(carries, carried, False)

    dgt[...] = jnp.zeros_like(dgt)
    local = experts // E
    whole = local // QUAD
    for mask in range(QUAD * E):
        from_r, from_e = flip(r, mask >> 2), flip(e, mask & 3)
        for k in range(slots):
            if k < whole:
                row = from_e * local + from_r * whole + k
            else:
                row = from_e * local + QUAD * whole + from_r // (QUAD // (local - QUAD * whole))
            dgt[pl.ds(row, 1), :] += dg_ref[mask, k:k + 1, :]
    dg = dgt[...].T
    probs = probs_ref[...]
    dz = (probs * (dg - jnp.sum(probs * dg, axis=1, keepdims=True))).astype(BF16)
    loads[0].wait()
    dh2 = dr_ref[...] + mm(dz, ws[:, qkv_cols:], NT)
    gain_attn, gain_moe = gains_ref[0:1, :], gains_ref[1:2, :]
    middle = middle_ref[...]
    scale = lax.rsqrt(jnp.mean(middle * middle, axis=1, keepdims=True) + epsilon)
    unit = middle * scale
    grad_moe_gain = jnp.sum(dh2 * unit, axis=0, keepdims=True)
    grad_unit = dh2 * gain_moe
    dx1 = cot_ref[...].astype(F32) + scale * (grad_unit - unit * jnp.mean(grad_unit * unit, axis=1, keepdims=True))
    dx1s[...] = dx1
    dat = dx1.astype(BF16)

    def token_rows(who):
        return pl.ds(pl.multiple_of(who * rows_here, 16), rows_here)
    load_out.wait()
    for b in range(E):
        do = mm(dat, xs[b * q_cols:(b + 1) * q_cols, :], NT).astype(BF16)
        do_out[b] = do
        @pl.when(e == b)
        def _():
            dos[token_rows(e), :] = do_out[b]
        @pl.when(e != b)
        def _():
            pltpu.make_async_remote_copy(do_out.at[b], dos.at[token_rows(e)], do_send.at[b], do_recv.at[e],
                device_id=device_at(q, r, b), device_id_type=MESH).start()
    loads[3].start()
    def do_descriptor(b):
        return pltpu.make_async_remote_copy(do_out.at[b], dos.at[pl.ds(b * rows_here, rows_here)], do_send.at[b], do_recv.at[b],
            device_id=device_at(q, r, flip(e, 1)), device_id_type=MESH)
    dats[token_rows(e), :] = dat
    dat_copies = {}
    for j in (1, 2, 3):
        rows = token_rows(e if j < 3 else flip(e, 2))
        dat_copies[j] = pltpu.make_async_remote_copy(dats.at[rows], dats.at[rows], dat_send.at[j], dat_recv.at[j],
            device_id=device_at(q, r, flip(e, j if j < 3 else 1)), device_id_type=MESH)
    dat_copies[2].start()
    dat_copies[1].start()
    small[...] = mm(h2_ref[...], dz, TN)
    dk_ref[...] = jnp.zeros_like(dk_ref)
    dv_ref[...] = jnp.zeros_like(dv_ref)
    for g in range(kv_heads):
        kt_ref[g] = k_ref[g].astype(F32).T.astype(BF16)

    seen = 0
    for i in range(length // block):
        rows = pl.ds(i * block, block)
        keys = (i + 1) * block
        while seen * rows_here < keys:
            @pl.when(e != seen)
            def _():
                do_descriptor(seen).wait_recv()
            seen += 1
        span = pl.ds(0, keys)
        bias = bias_block(seg_ref[:, rows], keys, i * block)
        dqs = []
        for h in range(heads):
            g = h // group
            qh = q_ref[h, rows, :]
            do = dos[rows, h * HD:(h + 1) * HD]
            st = mm(k_ref[g, span, :], qh * BF16(factor), NT) + bias
            p = jnp.exp(st - lse_ref[pl.ds(h, 1), rows])
            dpt = mm(v_ref[g, span, :], do, NT)
            inner = jnp.sum(p * dpt, axis=0, keepdims=True)
            ds = (p * (dpt - inner)).astype(BF16)
            dv_ref[g, span, :] += mm(p.astype(BF16), do)
            dk_ref[g, span, :] += mm(ds, qh)
            dqs.append(mm(kt_ref[g, :, span], ds))
        dq = jnp.concatenate(dqs, axis=0).T * factor
        cosine = jnp.concatenate([cos_ref[rows, :]] * (q_cols // 128), axis=1)
        sine = jnp.concatenate([sin_ref[rows, :]] * (q_cols // 128), axis=1)
        dqkv[rows, :q_cols] = (dq * cosine - swap_halves(dq) * sine).astype(BF16)
        if i == 1:
            dat_copies[2].wait_recv()
            dat_copies[3].start()
            carry_start(carries, carried, True)
    dk = jnp.concatenate([dk_ref[g] for g in range(kv_heads)], axis=1) * factor
    cosine = jnp.concatenate([cos_ref[...]] * (k_cols // 128), axis=1)
    sine = jnp.concatenate([sin_ref[...]] * (k_cols // 128), axis=1)
    dqkv[:, q_cols:q_cols + k_cols] = (dk * cosine - swap_halves(dk) * sine).astype(BF16)
    dqkv[:, q_cols + k_cols:] = jnp.concatenate([dv_ref[g] for g in range(kv_heads)], axis=1).astype(BF16)

    grad_attn_gain = jnp.zeros((1, width), F32)
    loads[3].wait()
    part_copies = {}
    own = None
    for j in (3, 1, 2, 0):
        rows = token_rows(flip(e, j))
        dh1 = mm(dqkv[rows, :], ws[:, :qkv_cols], NT)
        x = xs[rows, :].astype(F32)
        scale = lax.rsqrt(jnp.mean(x * x, axis=1, keepdims=True) + epsilon)
        grad_attn_gain = grad_attn_gain + jnp.sum(dh1 * (x * scale), axis=0, keepdims=True)
        if j & 1:
            part[j - 1] = dh1.astype(BF16)
            part_copies[j] = pltpu.make_async_remote_copy(part.at[j - 1], core_in.at[j // 2], part_send.at[j], part_recv.at[j],
                device_id=device_at(q, r, flip(e, 1)), device_id_type=MESH)
            part_copies[j].start()
        elif j == 2:
            part_copies[3].wait_recv()
            part[1] = (dh1 + core_in[1].astype(F32)).astype(BF16)
            part_copies[2] = pltpu.make_async_remote_copy(part.at[1], y_in, part_send.at[2], part_recv.at[2],
                device_id=device_at(q, r, flip(e, 2)), device_id_type=MESH)
            part_copies[2].start()
        else:
            own = dh1

    rows_out = lax.broadcasted_iota(jnp.int32, (128, width), 0)
    gains = jnp.where(rows_out == experts, grad_attn_gain, 0.0) + jnp.where(rows_out == experts + 1, grad_moe_gain, 0.0)
    small_all = small[...] + gains.T
    loads[2].wait()
    share = width // dp
    grad = mm(h1s[...], dqkv[...], TN).astype(BF16)
    for d in range(dp):
        g1[d, :, :qkv_cols] = grad[d * share:(d + 1) * share]
        g1[d, :, qkv_cols:] = small_all[d * share:(d + 1) * share].astype(BF16)
    dat_copies[1].wait_recv()
    dat_copies[3].wait_recv()
    loads[1].wait()
    grad = mm(mixeds[...], dats[...], TN)
    out_share = q_cols // dp
    if exchange:
        for d in range(dp):
            g2[d] = grad[d * out_share:(d + 1) * out_share].astype(BF16)
    else:
        gout_ref[...] = grad.astype(BF16)
    arrays = [(g1, r1, g1_send, g1_recv)] + ([(g2, r2, g2_send, g2_recv)] if exchange else [])
    keys = [(k, m) for k in range(quads) for m in range(QUAD)]
    def at(k, m):
        return place_at((q + k) % quads, flip(r, m))
    def has(key, dim):
        return key[0] if dim == "q" else key[1] & dim
    def first(p, key):
        return [n for n, dim in enumerate(DENSE_ORDERS[p]) if has(key, dim)][0]
    def sources(p, key, upto):
        found = []
        for dim in DENSE_ORDERS[p][:upto]:
            found += [(k, key[1]) for k in range(1, quads)] if dim == "q" else [(key[0], key[1] | dim)]
        return found
    copies = {}
    for n, (grad_ref, landing, send, recv) in enumerate(arrays):
        half = grad_ref.shape[2] // 2
        for p in range(2):
            for k, m in keys[1:]:
                dim = DENSE_ORDERS[p][first(p, (k, m))]
                device = device_at((q + k) % quads, r, e) if dim == "q" else device_at(q, flip(r, dim), e)
                copies[n, p, k, m] = pltpu.make_async_remote_copy(grad_ref.at[at(k, m), :, pl.ds(p * half, half)],
                    landing.at[p, k, m], send.at[p, k, m], recv.at[p, k, m], device_id=device, device_id_type=MESH)
    numbers = range(len(arrays))
    def reduced(n, p, key):
        grad_ref, landing = arrays[n][:2]
        half = grad_ref.shape[2] // 2
        sum_now = grad_ref[at(*key), :, p * half:(p + 1) * half].astype(F32)
        for k, m in sources(p, key, 3 if key == (0, 0) else first(p, key)):
            copies[n, p, k, m].wait_recv()
            sum_now = sum_now + landing[p, k, m].astype(F32)
        return sum_now
    def send_on(level):
        for p in range(2):
            now = [key for key in keys[1:] if first(p, key) == level]
            now.sort(key=lambda key: -sum(1 for dim in DENSE_ORDERS[p] if has(key, dim)))
            for k, m in now:
                for n in numbers:
                    if level:
                        half = arrays[n][0].shape[2] // 2
                        arrays[n][0][at(k, m), :, p * half:(p + 1) * half] = reduced(n, p, (k, m)).astype(BF16)
                    copies[n, p, k, m].start()
    send_on(0)
    send_on(1)
    part_copies[1].wait_recv()
    part_copies[2].wait_recv()
    dh1 = own + core_in[0].astype(F32) + y_in[...].astype(F32)
    x = tokens_ref[...].astype(F32)
    scale = lax.rsqrt(jnp.mean(x * x, axis=1, keepdims=True) + epsilon)
    unit = x * scale
    grad_unit = dh1 * gain_attn
    tokens_out[...] = dx1s[...] + scale * (grad_unit - unit * jnp.mean(grad_unit * unit, axis=1, keepdims=True))
    send_on(2)
    final = {(n, p): reduced(n, p, (0, 0)) for n in numbers for p in range(2)}
    dense = jnp.concatenate([final[0, 0], final[0, 1]], axis=1)
    if exchange:
        gout_ref[...] = jnp.concatenate([final[1, 0], final[1, 1]], axis=1).astype(BF16)
        g1[at(0, 0)] = dense.astype(BF16)
        shard = share // E
        f_copies = []
        for j in (1, 2, 3):
            rows = pl.ds(pl.multiple_of(flip(e, j) * shard, 16), shard)
            copy = pltpu.make_async_remote_copy(g1.at[at(0, 0), rows], f1.at[e], f_send.at[j], f_recv.at[j],
                device_id=device_at(q, r, flip(e, j)), device_id_type=MESH)
            copy.start()
            f_copies.append(copy)
        f1[e] = g1[at(0, 0), pl.ds(pl.multiple_of(e * shard, 16), shard), :]
        for copy in f_copies:
            copy.wait_recv()
        tail = jnp.zeros((shard, 128), F32)
        for b in range(E):
            piece = f1[b].astype(F32)
            gq_ref[:, b * q_cols:(b + 1) * q_cols] = piece[:, :q_cols]
            gk_ref[:, b * k_cols:(b + 1) * k_cols] = piece[:, q_cols:q_cols + k_cols]
            gv_ref[:, b * k_cols:(b + 1) * k_cols] = piece[:, q_cols + k_cols:qkv_cols]
            tail = tail + piece[:, qkv_cols:]
        small_ref[...] = tail
        for copy in f_copies:
            copy.wait_send()
    else:
        dense_ref[...] = dense.astype(BF16)
    for b in range(E):
        @pl.when(e != b)
        def _():
            do_descriptor(b).wait_send()
    for copy in list(dat_copies.values()) + list(part_copies.values()) + list(copies.values()):
        copy.wait_send()
    for copy in carries:
        copy.wait()

def back_call(dr_sum, dg_back, probs, h2, middle, cotangent, gains, tokens, out_full, query, key, value, log_total,
              cosine, sine, segments, h1_all, x_all, w_all, mixed, grads, moved, carried, experts, q_cols, k_cols, slots, exchange):
    E, quads = lax.axis_size("expert"), lax.axis_size("q")
    dp = quads * QUAD
    rows_here, width = tokens.shape
    length = rows_here * E
    total = w_all.shape[1]
    heads, kv_heads = q_cols // HD, k_cols // HD
    share, out_share = width // dp, q_cols // dp
    shard = share // E
    V, A = pl.BlockSpec(memory_space=pltpu.VMEM), pl.BlockSpec(memory_space=pl.ANY)
    S, M, sem = jax.ShapeDtypeStruct, pltpu.VMEM, pltpu.SemaphoreType.DMA
    if exchange:
        outs = (S((rows_here, width), F32), S((shard, q_cols * E), F32), S((shard, k_cols * E), F32), S((shard, k_cols * E), F32),
            S((shard, 128), F32), S((out_share, width), BF16))
        second = [M((dp, out_share, width), BF16), M((2, quads, QUAD, out_share, width // 2), BF16)]
    else:
        outs = (S((rows_here, width), F32), S((share, total), BF16), S((q_cols, width), BF16))
        second = [M((16, 128), BF16)] * 2
    scratch = [M((length, width), BF16), M((width, width), BF16), M((width, total), BF16), M((length, q_cols), BF16), sem((5,)),
        M((128, rows_here), F32), M((length, width), BF16), M((length, q_cols), BF16), M((E, rows_here, q_cols), BF16),
        M((kv_heads, HD, length), BF16), M((kv_heads, length, HD), F32), M((kv_heads, length, HD), F32), M((length, total - 128), BF16),
        M((rows_here, width), F32), M((width, 128), F32), M((3, rows_here, width), BF16), M((2, rows_here, width), BF16),
        M((rows_here, width), BF16),
        M((dp, share, total), BF16), second[0],
        M((2, quads, QUAD, share, total // 2), BF16), second[1], M((E, shard, total), BF16)]
    scratch += [sem((4,))] * 6 + [sem((2, quads, 4))] * 4 + [sem((4,))] * 2 + [sem(moved.shape[:3])] * 2
    outs += (S(moved.shape, moved.dtype),)
    return pl.pallas_call(functools.partial(back_kernel, (experts, q_cols, k_cols, slots), exchange, carried),
        out_shape=outs, in_specs=[V] * 8 + [A] + [V] * 7 + [A] * 6, out_specs=(V,) * (len(outs) - 1) + (A,), scratch_shapes=scratch,
        input_output_aliases={21: len(outs) - 1},
        compiler_params=pltpu.CompilerParams(vmem_limit_bytes=60 << 20, collective_id=5, has_side_effects=True),
        cost_estimate=CHEAP,
        name="backward")(dr_sum, dg_back, probs, h2, middle, cotangent, gains, tokens, out_full, query, key, value, log_total,
            cosine, sine, segments.reshape(1, -1), h1_all, x_all, w_all, mixed, grads, moved)


ALL = ("q", "rh", "rl", "expert")
DP = ("q", "rh", "rl")
GROUP = ("rh", "rl", "expert")


def shards(
    tokens, w_query, w_key, w_value, w_out, w_router, gain_attn, gain_moe,
    w_gate, w_up, w_down, segments, routes, priority, cotangent,
):
    rows_here, width = tokens.shape
    E = lax.axis_size("expert")
    R = QUAD
    Q = lax.axis_size("q")
    e = lax.axis_index("expert")
    r = member_r()
    shard_rows = w_query.shape[0]
    local = w_gate.shape[0]
    experts = local * E
    ffn = w_gate.shape[2]
    capacity = rows_here * routes.shape[1] // experts
    length = rows_here * E
    sources = R * E
    q_cols = w_query.shape[1] // E
    k_cols = w_key.shape[1] // E
    exchange = shard_rows % 16 == 0
    small = jnp.concatenate([w_router, gain_attn[:, None], gain_moe[:, None]], axis=1)
    small = jnp.pad(small, ((0, 0), (0, 128 - small.shape[1])))
    pieces = jnp.concatenate(
        [w.reshape(shard_rows, E, -1) for w in (w_query, w_key, w_value)]
        + [jnp.broadcast_to(small[:, None], (shard_rows, E, 128))],
        axis=2,
    )
    pieces = jnp.transpose(pieces, (1, 0, 2))
    out_part = w_out
    if not exchange:
        pieces = lax.all_to_all(pieces, "expert", split_axis=0, concat_axis=0, tiled=True)
        pieces = pieces.reshape(E * shard_rows, -1)
        out_part = lax.all_gather(w_out, ALL, axis=0, tiled=True)
    cosine, sine = (jnp.asarray(t) for t in rope_tables(length))
    (x_all, w_all, out_full, h1_all, query, key, value, mixed, log_total, middle, h2, table, probs, gains, dm_all) = start_call(
        tokens, pieces, out_part, cotangent, routes.T, priority.T, segments, cosine, sine, experts, capacity, q_cols, k_cols, exchange
    )
    qkv_cols = q_cols + 2 * k_cols
    dp = Q * R
    whole = local // R
    rest = local - whole * R
    ways = R // rest if rest else 1
    slots = whole + (1 if rest else 0)

    rows, dm_rows, weight, tables = gather_rows(h2, table, dm_all, slots, capacity, 1)
    def scalars(places):
        return jnp.stack(places + [r % ways]).astype(jnp.int32)

    banks = (w_gate, w_up, w_down)
    done = []
    if rest:
        part = expert_call(rows, dm_rows, weight, whole, 1, *banks, scalars([R * whole + r // ways]), dp, ways)
        part_moved = lax.all_to_all(part[3], DP, split_axis=0, concat_axis=0, tiled=True)
    done.append(expert_call(rows, dm_rows, weight, 0, whole, *banks, scalars([r * whole + s for s in range(whole)]), dp, 1))
    grads = done[0][3]
    if rest:
        done.append(part)
    plan = carry_plan(Q, whole)
    y_rows, dr_rows, dg_rows = ([d[n] for d in done] for n in range(3))
    dr_sum, dg_back, moved = combine_rows(dr_rows, tables, dg_rows, None, grads, None, plan[0], capacity, 2)
    if rest:
        (dr_sum, part_moved) = lax.optimization_barrier((dr_sum, part_moved))
    out = back_call(
        dr_sum, dg_back, probs, h2, middle, cotangent, gains, tokens, out_full, query, key, value, log_total,
        cosine, sine, segments, h1_all, x_all, w_all, mixed, grads, moved, plan[1],
        experts, q_cols, k_cols, slots, exchange
    )
    moved = out[-1]
    if exchange:
        grad_tokens, grad_query, grad_key, grad_value, small_own, out_sum = out[:-1]
    else:
        grad_tokens, qkv_sum, out_sum = out[:-1]
        qkv_own = lax.all_to_all(
            qkv_sum.reshape(E, shard_rows, -1), "expert", split_axis=0, concat_axis=0, tiled=True
        )
        qkv_own = jnp.transpose(qkv_own, (1, 0, 2)).astype(F32)
        small_own = jnp.sum(qkv_own[:, :, qkv_cols:], axis=1)
        grad_query = qkv_own[:, :, :q_cols].reshape(shard_rows, -1)
        grad_key = qkv_own[:, :, q_cols : q_cols + k_cols].reshape(shard_rows, -1)
        grad_value = qkv_own[:, :, q_cols + k_cols : qkv_cols].reshape(shard_rows, -1)
        out_sum = lax.psum_scatter(out_sum, DP, scatter_dimension=0, tiled=True)
    perm = [(p * E + x, dp * x + p) for p in range(dp) for x in range(E)]
    out_own = lax.ppermute(out_sum, ALL, perm).astype(F32)
    outputs, moved = combine_rows(y_rows, tables, None, middle, grads, moved, plan[2], capacity, 3)
    order = jnp.stack([r ^ m for m in range(R)]).astype(jnp.int32)
    gate_share, up_share, down_share = place_call(moved, [part_moved] if rest else [], order, local, ffn, width)
    return (
        outputs,
        grad_tokens,
        grad_query,
        grad_key,
        grad_value,
        out_own,
        small_own[:, :experts],
        small_own[:, experts],
        small_own[:, experts + 1],
        gate_share,
        up_share,
        down_share,
    )


def solution(mesh):
    dp, ex = mesh.devices.shape
    fine = Mesh(mesh.devices.reshape(dp // QUAD, 2, 2, ex), ALL)
    row, flat = P(ALL, None), P(ALL)
    bank = P("expert", None, None)
    spread = P("expert", DP, None)
    return jax.shard_map(
        shards,
        mesh=fine,
        in_specs=(row,) * 6 + (flat,) * 2 + (bank,) * 3 + (P(DP),) + (row,) * 3,
        out_specs=(row,) * 7 + (flat,) * 2 + (spread,) * 3,
        check_vma=False,
    )
```

```python
import functools

import jax
import jax.numpy as jnp
import numpy as np
from jax import lax
from jax.experimental import pallas as pl
from jax.experimental.pallas import tpu as pltpu
from jax.sharding import Mesh
from jax.sharding import PartitionSpec as P

HD = 64
QUAD = 4
F32 = jnp.float32
BF16 = jnp.bfloat16

CHEAP = pl.CostEstimate(flops=1 << 20, bytes_accessed=1 << 16, transcendentals=0)

epsilon = 1e-06
rope_base = 10000.0
masked_score = -1e30


def rope_tables(length):
    frequency = np.float32(rope_base) ** (np.float32(-2.0) * np.arange(HD // 2, dtype=np.float32) / np.float32(HD))
    angles = np.arange(length, dtype=np.float32)[:, None] * frequency[None, :].astype(np.float32)
    cosine, sine = np.cos(angles).astype(np.float32), np.sin(angles).astype(np.float32)
    return np.tile(cosine, (1, 4)), np.tile(np.concatenate([-sine, sine], axis=1), (1, 2))


NT=(((1,),(1,)),((),()))
NN=(((1,),(0,)),((),()))
TN=(((0,),(0,)),((),()))

def mm(a,b,dims=NN):
    return lax.dot_general(a,b,dims,preferred_element_type=F32)

def swap_halves(x):
    lane=lax.broadcasted_iota(jnp.int32,(x.shape[0],128),1)
    low=(lane%HD)<HD//2
    parts=[]
    for c in range(x.shape[1]//128):
        g=x[:,c*128:(c+1)*128]
        parts.append(jnp.where(low,pltpu.roll(g,128-HD//2,1),pltpu.roll(g,HD//2,1)))
    return jnp.concatenate(parts,axis=1)

def bias_block(seg_row, keys, first):
    n=seg_row.shape[1]
    s=lax.broadcasted_iota(jnp.int32,(keys,n),0)
    t=lax.broadcasted_iota(jnp.int32,(keys,n),1)+first
    return jnp.where((s<=t)&(s>=seg_row),0.0,masked_score)

MESH=pl.DeviceIdType.MESH
CORE = 1
GATHER_ORDERS = ((2, 4, 8), (4, 8, 2), (8, 2, 4))
SUM_ORDERS = ((2, 4, 8), (4, 8, 2), (8, 2, 4))
LAST_ORDERS = ((4, 2, 8), (2, 4, 8))

def member_r():
    return lax.axis_index("rh") * 2 + lax.axis_index("rl")

def device_at(q, r, e):
    return (q, r // 2, r % 2, e)

def place_at(q, r):
    return q * QUAD + r

def flip(value, mask):
    low, high = value % 2, value // 2
    if mask & 1:
        low = 1 - low
    if mask & 2:
        high = 1 - high
    return high * 2 + low

def group_device(mask):
    return device_at(lax.axis_index("q"), flip(member_r(), mask >> 2), flip(lax.axis_index("expert"), mask & 3))

def group_member(mask):
    return flip(member_r(), mask >> 2) * 4 + flip(lax.axis_index("expert"), mask & 3)

def greet_devices(devices):
    barrier = pltpu.get_barrier_semaphore()
    for device in devices:
        pl.semaphore_signal(barrier, inc=1, device_id=device, device_id_type=MESH)
    pl.semaphore_wait(barrier, len(devices))

def greet(masks):
    greet_devices([group_device(mask) for mask in masks])

DM_ORDERS = ((2, 4, 8), (4, 8, 2), (8, 2, 4))

def last_hop(order, mask):
    if mask & CORE:
        return CORE
    return [bit for bit in order if mask & bit][-1]

def block_copies(own_ref, held_ref, orders, send, recv, first=0, last=None):
    part_width = ((last or own_ref.shape[1]) - first) // len(orders)
    copies = {}
    for p, order in enumerate(orders):
        columns = pl.ds(p * part_width, part_width)
        for mask in range(1, 16):
            hop = last_hop(order, mask)
            source = own_ref.at[:, pl.ds(first + p * part_width, part_width)] if mask == hop else held_ref.at[mask ^ hop, :, columns]
            copies[p, mask] = pltpu.make_async_remote_copy(source, held_ref.at[mask, :, columns], send.at[p, mask], recv.at[p, mask],
                device_id=group_device(hop), device_id_type=MESH)
    return copies

def block_start(copies, orders, arrived):
    p, mask = arrived
    for nxt in range(1, 16):
        if nxt != mask and nxt ^ last_hop(orders[p], nxt) == mask:
            copies[p, nxt].start()

def gather_order(orders):
    parts = range(len(orders))
    free = {2: 0.0, 4: 0.0, 8: 0.0}
    arrived, todo = {(p, 0): 0.0 for p in parts}, [(p, m) for p in parts for m in range(2, 16, 2)]
    order = []
    while todo:
        best = None
        for p, m in todo:
            hop = last_hop(orders[p], m)
            if (p, m ^ hop) in arrived:
                key = (max(free[hop], arrived[p, m ^ hop]), orders[p].index(hop), p, m)
                if best is None or key < best:
                    best = key
        start, _, p, m = best
        hop = last_hop(orders[p], m)
        free[hop] = start + 1
        arrived[p, m] = start + 1
        todo.remove((p, m))
        order.append((start + 1, p, m))
    return [(p, m) for _, p, m in sorted(order)]

def one_hot(table, capacity, slots):
    place = lax.broadcasted_iota(jnp.int32, (capacity, table.shape[1]), 0).astype(F32)
    return [table[k:k + 1, :] == place for k in range(slots)]

def gather_kernel(slots, capacity, h2_ref, table_ref, dm_ref, rows_ref, dm_rows_ref, weight_ref, tables_ref,
                  held, arrived, dm_held, send, recv, table_send, table_recv, dm_sem):
    width = h2_ref.shape[1]
    part_width = width // len(GATHER_ORDERS)
    greet(range(1, 16))
    tables = []
    for mask in range(1, 16):
        copy = pltpu.make_async_remote_copy(table_ref.at[group_member(mask)], arrived.at[mask],
            table_send.at[mask], table_recv.at[mask], device_id=group_device(mask), device_id_type=MESH)
        copy.start()
        tables.append(copy)
    arrived[0] = table_ref[group_member(0)]
    copies = block_copies(h2_ref, held, GATHER_ORDERS, send, recv)
    order = gather_order(GATHER_ORDERS)
    for p, mask in order + [(p, CORE) for p in range(len(GATHER_ORDERS))]:
        if mask == last_hop(GATHER_ORDERS[p], mask):
            copies[p, mask].start()
    def dm_copy(mask):
        return pltpu.make_async_copy(dm_ref.at[mask], dm_held.at[mask % 2], dm_sem.at[mask % 2])
    dm_copy(0).start()
    for copy in tables:
        copy.wait_recv()
    def hots(mask):
        return one_hot(arrived[mask], capacity, slots)
    def place(target, mask, hot, block, columns):
        got = mm(jnp.concatenate([h.astype(BF16) for h in hot], axis=0), block).astype(BF16)
        for k in range(slots):
            target[k, pl.ds(mask * capacity, capacity), columns] = got[k * capacity:(k + 1) * capacity]
    def dm_step(mask):
        if mask + 1 < 16:
            dm_copy(mask + 1).start()
        dm_copy(mask).wait()
        hot = hots(mask)
        place(dm_rows_ref, mask, hot, dm_held[mask % 2], slice(None))
        if mask == 0:
            place(rows_ref, 0, hot, h2_ref[...], slice(None))
        table = arrived[mask]
        for k in range(slots):
            weight_ref[k, pl.ds(mask * capacity, capacity), :] = jnp.sum(
                jnp.where(hot[k], table[4 + k:5 + k, :], 0.0), axis=1, keepdims=True)
        tables_ref[mask] = table
    todo = list(range(16))
    dm_step(todo.pop(0))
    dm_step(todo.pop(0))
    def arrive(p, mask):
        copies[p, mask].wait_recv()
        block_start(copies, GATHER_ORDERS, (p, mask))
        columns = pl.ds(p * part_width, part_width)
        place(rows_ref, mask, hots(mask), held[mask, :, columns], columns)
    for step, (p, mask) in enumerate(order):
        arrive(p, mask)
        if todo:
            dm_step(todo.pop(0))
    for p in range(len(GATHER_ORDERS)):
        arrive(p, CORE)
    for p, mask in order:
        arrive(p, mask | CORE)
    for copy in tables:
        copy.wait_send()
    for key in copies:
        copies[key].wait_send()

def gather_rows(h2, table, dm_all, slots, capacity, collective_id):
    tokens, width = h2.shape
    V = pl.BlockSpec(memory_space=pltpu.VMEM)
    rows = jax.ShapeDtypeStruct((slots, 16 * capacity, width), BF16)
    return pl.pallas_call(functools.partial(gather_kernel, slots, capacity),
        out_shape=(rows, rows, jax.ShapeDtypeStruct((slots, 16 * capacity, 1), F32), jax.ShapeDtypeStruct(table.shape, F32)),
        in_specs=[V, V, pl.BlockSpec(memory_space=pl.ANY)], out_specs=(V,) * 4,
        scratch_shapes=[pltpu.VMEM((16, tokens, width), BF16), pltpu.VMEM(table.shape, F32),
            pltpu.VMEM((2, tokens, width), BF16), pltpu.SemaphoreType.DMA((len(GATHER_ORDERS), 16)), pltpu.SemaphoreType.DMA((len(GATHER_ORDERS), 16)),
            pltpu.SemaphoreType.DMA((16,)), pltpu.SemaphoreType.DMA((16,)), pltpu.SemaphoreType.DMA((2,))],
        compiler_params=pltpu.CompilerParams(vmem_limit_bytes=58 << 20, collective_id=collective_id, has_side_effects=True),
        cost_estimate=CHEAP,
        name="gather_rows")(h2, table, dm_all)

def expert_kernel(chunks, dp, ways, s_ref, x_ref, dm_ref, weight_ref, wg_ref, wu_ref, wd_ref,
                  y_ref, dr_ref, dg_ref, grads, xs, dms, mgs, das, *banks):
    i = pl.program_id(1)
    block = x_ref.shape[1]
    if ways > 1:
        wg, wu, wd = banks
        ff = wg.shape[1]
        part = ff // dp
        @pl.when(i == 0)
        def _():
            shape = (ff * ways, ff)
            row, col = lax.broadcasted_iota(jnp.int32, shape, 0), lax.broadcasted_iota(jnp.int32, shape, 1)
            pick = (row == (col // part * ways + s_ref[s_ref.shape[0] - 1]) * part + col % part).astype(F32).astype(BF16)
            wg[...] = mm(wg_ref[0], pick).astype(BF16)
            wu[...] = mm(wu_ref[0], pick).astype(BF16)
            wd[...] = mm(pick, wd_ref[0], TN).astype(BF16)
    else:
        wg, wu, wd = wg_ref.at[0], wu_ref.at[0], wd_ref.at[0]
        ff = wg.shape[1]
    @pl.when(i < chunks)
    def _():
        x, dmr, w = x_ref[0], dm_ref[0], weight_ref[0]
        rows = pl.ds(pl.multiple_of(i * block, block), block)
        xs[rows, :] = x
        dms[rows, :] = dmr
        ga = mm(x, wg[...])
        ua = mm(x, wu[...])
        u = mm(dmr, wd[...], NT)
        sig = 1.0 / (1.0 + jnp.exp(-ga))
        silu = ga * sig
        m = silu * ua
        mg = (m * w).astype(BF16)
        dg_ref[0] = jnp.sum(m * u, axis=1, keepdims=True)
        dmh = u * w
        da = (dmh * ua * (sig * (1.0 + ga * (1.0 - sig)))).astype(BF16)
        du = (dmh * silu).astype(BF16)
        mgs[rows, :] = mg
        das[rows, :ff] = da
        das[rows, ff:] = du
        y_ref[0] = mm(mg, wd[...]).astype(BF16)
        dr_ref[0] = (mm(da, wg[...], NT) + mm(du, wu[...], NT)).astype(BF16)
    @pl.when(i == chunks)
    def _():
        width = xs.shape[1]
        share, down_share = width // dp, ff // dp
        for half in range(2):
            grad = mm(xs[...], das[:, half * ff:(half + 1) * ff], TN).astype(BF16)
            for d in range(dp):
                grads[d, 0, half * share:(half + 1) * share, :] = grad[d * share:(d + 1) * share]
        down = mm(mgs[...], dms[...], TN).astype(BF16)
        for d in range(dp):
            for c in range(width // ff):
                first = 2 * share + c * down_share
                grads[d, 0, first:first + down_share, :] = down[d * down_share:(d + 1) * down_share, c * ff:(c + 1) * ff]

def expert_call(rows, dm_rows, weight, first, count, w_gate, w_up, w_down, scalars, dp, ways, block=512):
    _, total, width = rows.shape
    ff = w_gate.shape[2] // ways
    chunks = total // block
    row = lambda n, i, s: (first + n, jnp.minimum(i, chunks - 1), 0)
    out = lambda n, i, s: (n, jnp.minimum(i, chunks - 1), 0)
    bank = lambda a: pl.BlockSpec((1,) + a.shape[1:], lambda n, i, s: (s[n], 0, 0))
    share = width // dp
    S, M = jax.ShapeDtypeStruct, pltpu.VMEM
    return pl.pallas_call(functools.partial(expert_kernel, chunks, dp, ways),
        grid_spec=pltpu.PrefetchScalarGridSpec(num_scalar_prefetch=1, grid=(count, chunks + 1),
            in_specs=[pl.BlockSpec((1, block, width), row), pl.BlockSpec((1, block, width), row), pl.BlockSpec((1, block, 1), row),
                bank(w_gate), bank(w_up), bank(w_down)],
            out_specs=(pl.BlockSpec((1, block, width), out), pl.BlockSpec((1, block, width), out), pl.BlockSpec((1, block, 1), out),
                pl.BlockSpec((dp, 1, 3 * share, ff), lambda n, i, s: (0, n, 0, 0))),
            scratch_shapes=[M((total, width), BF16), M((total, width), BF16), M((total, ff), BF16), M((total, 2 * ff), BF16)]
                + ([M((width, ff), BF16), M((width, ff), BF16), M((ff, width), BF16)] if ways > 1 else [])),
        out_shape=(S((count, total, width), BF16), S((count, total, width), BF16), S((count, total, 1), F32),
            S((dp, count, 3 * share, ff), BF16)),
        compiler_params=pltpu.CompilerParams(vmem_limit_bytes=58 << 20, dimension_semantics=("arbitrary", "arbitrary")),
        cost_estimate=CHEAP,
        name="expert_part" if ways > 1 else "experts")(scalars, rows, dm_rows, weight, w_gate, w_up, w_down)

def place_kernel(whole, rest, ways, order_ref, *refs):
    moved, (gate_ref, up_ref, down_ref) = refs[:-3], refs[-3:]
    i = pl.program_id(0)
    share, down_share = gate_ref.shape[1], down_ref.shape[1]
    width, ff = down_ref.shape[2], gate_ref.shape[2]
    quads = moved[0].shape[2]
    @pl.when(i < QUAD)
    def _():
        for s in range(whole):
            block = sum(moved[0][s, 0, k].astype(F32) for k in range(quads))
            gate_ref[s] = block[:share]
            up_ref[s] = block[share:2 * share]
            for c in range(width // ff):
                first = 2 * share + c * down_share
                down_ref[s, :, c * ff:(c + 1) * ff] = block[first:first + down_share]
    if rest:
        @pl.when(i == QUAD)
        def _():
            cols = ff // ways
            part = down_share // ways
            for x in range(rest):
                gate = jnp.zeros((2 * share, ff), F32)
                for h in range(ways):
                    col = lax.broadcasted_iota(jnp.int32, (cols, ff), 0)
                    spot = (col // part * ways + h) * part + col % part
                    pick = (lax.broadcasted_iota(jnp.int32, (cols, ff), 1) == spot).astype(F32).astype(BF16)
                    down = jnp.zeros((share, cols), F32)
                    for k in range(quads):
                        block = moved[1][k, x * ways + h, 0]
                        gate = gate + mm(block[:2 * share], pick)
                        down = down + block[2 * share:].astype(F32)
                    for c in range(width // cols):
                        down_ref[x, h * part:(h + 1) * part, c * cols:(c + 1) * cols] = down[c * part:(c + 1) * part]
                gate_ref[x] = gate[:share]
                up_ref[x] = gate[share:]

def place_call(moved, shared, order, local, ffn, width):
    whole, _, quads, rows, _ = moved.shape
    rest = local - whole * QUAD
    ways = QUAD // rest if rest else 1
    share = rows // 3
    down_share = ffn * share // width
    shared = [a.reshape((quads, QUAD) + a.shape[1:]) for a in shared]
    full = lambda a: pl.BlockSpec(a.shape, lambda i, s: (0, 0, 0, 0, 0))
    out = lambda a, b: pl.BlockSpec((whole, a, b), lambda i, s: (i, 0, 0))
    S = jax.ShapeDtypeStruct
    return pl.pallas_call(functools.partial(place_kernel, whole, rest, ways),
        grid_spec=pltpu.PrefetchScalarGridSpec(num_scalar_prefetch=1, grid=(QUAD + (1 if rest else 0),),
            in_specs=[pl.BlockSpec((whole, 1, quads, rows, ffn), lambda i, s: (0, s[jnp.minimum(i, QUAD - 1)], 0, 0, 0))]
                + [full(a) for a in shared],
            out_specs=(out(share, ffn), out(share, ffn), out(down_share, width))),
        out_shape=(S((local, share, ffn), F32), S((local, share, ffn), F32), S((local, down_share, width), F32)),
        compiler_params=pltpu.CompilerParams(vmem_limit_bytes=58 << 20, dimension_semantics=("arbitrary",)),
        cost_estimate=CHEAP, name="place_gradients")(order, moved, *shared)

def relative_device(k, m):
    return device_at((lax.axis_index("q") + k) % lax.axis_size("q"), flip(member_r(), m), lax.axis_index("expert"))

def carry_keys(quads, slots, with_x):
    ms = (1, 3) if with_x else (0, 2)
    return [(s, k, m) for s in slots for m in ms for k in range(quads) if (k, m) != (0, 0)]

def carry_copies(grads_ref, moved_ref, carried, send, recv):
    quads = lax.axis_size("q")
    copies = []
    for s, k, m, _ in carried:
        q, r = (lax.axis_index("q") + k) % quads, flip(member_r(), m)
        copies.append(pltpu.make_async_remote_copy(grads_ref.at[place_at(q, r), s], moved_ref.at[s, m, (quads - k) % quads],
            send.at[s, m, k], recv.at[s, m, (quads - k) % quads], device_id=relative_device(k, m), device_id_type=MESH))
    return copies

def is_outer():
    return lax.axis_index("q") % 2 == lax.axis_index("rh")

def carry_start(copies, carried, late):
    for copy, (_, k, _, who) in zip(copies, carried):
        if who != "all":
            if not late:
                pl.when(is_outer() if who == "outer" else jnp.logical_not(is_outer()))(copy.start)
        elif not k:
            if not late:
                copy.start()
        elif late:
            pl.when(jnp.logical_not(is_outer()))(copy.start)
        else:
            pl.when(is_outer())(copy.start)

def carry_wait(copies, carried):
    for copy, (_, _, _, who) in zip(copies, carried):
        if who == "all":
            copy.wait()
        else:
            pl.when(is_outer() if who == "outer" else jnp.logical_not(is_outer()))(copy.wait)

def carry_plan(quads, whole):
    first, second, third = [], [], []
    for key in carry_keys(quads, range(whole), False) + carry_keys(quads, range(whole), True):
        s, k, m = key
        rest = third if s and (k or m == 2) else second
        if m == 2 and k % 2:
            first.append(key + ("inner",))
            rest.append(key + ("outer",))
        else:
            rest.append(key + ("all",))
    return first, second, third

def first_hop(order, mask):
    return [bit for bit in order if mask & bit][0]

def combine_kernel(banks, slots, capacity, with_dg, carried, *refs):
    orders = SUM_ORDERS if with_dg else LAST_ORDERS
    rows, refs = refs[:banks], refs[banks:]
    tables_ref, refs = refs[0], refs[1:]
    if with_dg:
        dg_refs, grads_ref, refs = refs[:banks], refs[banks], refs[banks + 1:]
        out_ref, dg_out, moved_ref, refs = refs[0], refs[1], refs[2], refs[3:]
    else:
        middle_ref, grads_ref, _, out_ref, moved_ref, refs = refs[0], refs[1], refs[2], refs[3], refs[4], refs[5:]
    core_out, core_in, held, got, core_send, core_recv, send, recv, carry_send, carry_recv, own_sem = refs[:11]
    if with_dg:
        dg_hold, dg_in, dg_send, dg_recv = refs[11:]
    width = out_ref.shape[1]
    part_width = width // len(orders)
    masks = list(range(1, 16)) if with_dg else [1, 2, 4, 8]
    far = sorted({(k, m) for _, k, m, _ in carried if k or m * 4 not in masks})
    greet_devices([group_device(mask) for mask in masks] + [relative_device(k, m) for k, m in far])
    carries = carry_copies(grads_ref, moved_ref, carried, carry_send, carry_recv)
    straight = [n for n, key in enumerate(carried) if not key[2] & 1]
    turning = [n for n, key in enumerate(carried) if key[2] & 1]
    def carry(chosen, late):
        carry_start([carries[n] for n in chosen], [carried[n] for n in chosen], late)
    carry(straight, False)
    own_copies = []
    if with_dg:
        for s in range(moved_ref.shape[0]):
            own_copies.append(pltpu.make_async_copy(grads_ref.at[place_at(lax.axis_index("q"), member_r()), s],
                moved_ref.at[s, 0, 0], own_sem.at[s]))
            own_copies[-1].start()
    def hots(mask):
        return one_hot(tables_ref[mask], capacity, slots)
    def block_sum(mask, hot):
        return mm(jnp.concatenate([h.astype(BF16) for h in hot], axis=0),
            jnp.concatenate([a[n, pl.ds(mask * capacity, capacity), :] for a in rows for n in range(a.shape[0])], axis=0), TN)
    dg_copies = []
    def dg_step(mask, hot):
        if not with_dg:
            return
        for k in range(slots):
            col = [(a, n) for a in dg_refs for n in range(a.shape[0])][k]
            col = col[0][col[1], pl.ds(mask * capacity, capacity), :]
            dg_hold[mask, k:k + 1, :] = jnp.sum(jnp.where(hot[k], col, 0.0), axis=0, keepdims=True)
        if mask == 0:
            return
        copy = pltpu.make_async_remote_copy(dg_hold.at[mask], dg_in.at[mask], dg_send.at[mask], dg_recv.at[mask],
            device_id=group_device(mask), device_id_type=MESH)
        copy.start()
        dg_copies.append(copy)
    listed = sorted(range(0, 16, 2), key=lambda m: (-bin(m).count("1"), m))
    if with_dg:
        dg_hold[...] = jnp.zeros_like(dg_hold)
    core = {}
    for mask in listed:
        hot = hots(mask | CORE)
        core_out[mask // 2] = block_sum(mask | CORE, hot).astype(BF16)
        core[mask] = pltpu.make_async_remote_copy(core_out.at[mask // 2], core_in.at[mask // 2], core_send.at[mask // 2],
            core_recv.at[mask // 2], device_id=group_device(CORE), device_id_type=MESH)
        core[mask].start()
        dg_step(mask | CORE, hot)
    copies = {}
    for p in range(len(orders)):
        for mask in range(2, 16, 2):
            copies[p, mask] = pltpu.make_async_remote_copy(held.at[p, mask // 2], got.at[p, mask // 2], send.at[p, mask // 2],
                recv.at[p, mask // 2], device_id=group_device(first_hop(orders[p], mask)), device_id_type=MESH)
    for mask in listed:
        hot = hots(mask)
        own = block_sum(mask, hot)
        core[mask].wait_recv()
        own = (own + core_in[mask // 2].astype(F32)).astype(BF16)
        for p in range(len(orders)):
            held[p, mask // 2] = own[:, p * part_width:(p + 1) * part_width]
            if mask & orders[p][0]:
                copies[p, mask].start()
        dg_step(mask, hot)
    carry(turning, False)
    carry(straight + turning, True)
    def add(p, target, sources):
        total = held[p, target // 2].astype(F32)
        for source in sources:
            copies[p, source].wait_recv()
            total = total + got[p, source // 2].astype(F32)
        return total
    def forward(p, target, sources):
        held[p, target // 2] = add(p, target, sources).astype(BF16)
        copies[p, target].start()
    for both in (True, False):
        for p in range(len(orders)):
            a, b, c = orders[p]
            target = b | c if both else b
            forward(p, target, [target | a])
    for p in range(len(orders)):
        a, b, c = orders[p]
        forward(p, c, [c | a, c | b])
    for p in range(len(orders)):
        a, b, c = orders[p]
        columns = pl.ds(p * part_width, part_width)
        total = add(p, 0, [a, b, c])
        out_ref[:, columns] = total if with_dg else (middle_ref[:, columns] + total).astype(BF16)
    if with_dg:
        dg_out[0] = dg_hold[0]
        for copy in dg_copies:
            copy.wait_recv()
        for mask in range(1, 16):
            dg_out[mask] = dg_in[mask]
        for copy in dg_copies:
            copy.wait_send()
    for mask in listed:
        core[mask].wait_send()
    for key in copies:
        copies[key].wait_send()
    carry_wait(carries, carried)
    for copy in own_copies:
        copy.wait()

def combine_rows(rows, tables, dgs, middle, grads, moved, carried, capacity, collective_id):
    banks, slots = len(rows), sum(a.shape[0] for a in rows)
    tokens, width = tables.shape[2], rows[0].shape[2]
    V, A = pl.BlockSpec(memory_space=pltpu.VMEM), pl.BlockSpec(memory_space=pl.ANY)
    with_dg = dgs is not None
    quads, whole = grads.shape[0] // QUAD, grads.shape[1]
    out = jax.ShapeDtypeStruct((tokens, width), F32 if with_dg else BF16)
    moved_shape = jax.ShapeDtypeStruct((whole, QUAD, quads) + grads.shape[2:], grads.dtype)
    table = pltpu.VMEM(tables.shape, F32)
    sem = pltpu.SemaphoreType.DMA
    parts = len(SUM_ORDERS if with_dg else LAST_ORDERS)
    operands = list(rows) + [tables] + (list(dgs) + [grads] if with_dg else [middle, grads, moved])
    return pl.pallas_call(functools.partial(combine_kernel, banks, slots, capacity, with_dg, carried),
        out_shape=(out, jax.ShapeDtypeStruct(tables.shape, F32), moved_shape) if with_dg else (out, moved_shape),
        in_specs=[V] * (banks + 1 + (banks if with_dg else 1)) + [A] * (1 if with_dg else 2),
        out_specs=(V, V, A) if with_dg else (V, A),
        input_output_aliases={} if with_dg else {banks + 3: 1},
        scratch_shapes=[pltpu.VMEM((8, tokens, width), BF16), pltpu.VMEM((8, tokens, width), BF16),
            pltpu.VMEM((parts, 8, tokens, width // parts), BF16), pltpu.VMEM((parts, 8, tokens, width // parts), BF16),
            sem((8,)), sem((8,)), sem((parts, 8)), sem((parts, 8)), sem((whole, QUAD, quads)), sem((whole, QUAD, quads)), sem((whole,))]
            + ([table, table, sem((16,)), sem((16,))] if with_dg else []),
        compiler_params=pltpu.CompilerParams(vmem_limit_bytes=58 << 20, collective_id=collective_id, has_side_effects=True),
        cost_estimate=CHEAP,
        name="combine_with_dg" if with_dg else "combine_rows")(*operands)

DP_ORDERS = (("q", 1, 2), ("q", 2, 1), ("q", 2, 1))


def device_experts(local, r):
    whole = local // QUAD
    rest = local - whole * QUAD
    return [r * whole + s for s in range(whole)] + ([QUAD * whole + r // (QUAD // rest)] if rest else [])


def dp_last(part, k, m):
    return [dim for dim in DP_ORDERS[part] if (k if dim == "q" else m & dim)][-1]

def dp_source(part, k, m):
    dim = dp_last(part, k, m)
    return (0, m) if dim == "q" else (k, m ^ dim)

def dp_origin(k, m):
    return place_at((lax.axis_index("q") + k) % lax.axis_size("q"), flip(member_r(), m))

def dp_copies(ref, rows, first, part_width, send, recv):
    quads = lax.axis_size("q")
    copies = {}
    for p in range(3):
        columns = pl.ds(p * part_width, part_width)
        for k in range(quads):
            for m in range(QUAD):
                if (k, m) == (0, 0):
                    continue
                dim = dp_last(p, k, m)
                block = ref.at[pl.ds(first(dp_origin(*dp_source(p, k, m))), rows), columns]
                q, r, e = lax.axis_index("q"), member_r(), lax.axis_index("expert")
                device = device_at((q + quads - k) % quads, r, e) if dim == "q" else device_at(q, flip(r, dim), e)
                copies[p, k, m] = pltpu.make_async_remote_copy(block, block, send.at[p, k, m], recv.at[p, k, m],
                    device_id=device, device_id_type=MESH)
    return copies

def dp_order(copies):
    def hops(key):
        p, k, m = key
        return (1 if k else 0) + bin(m).count("1")
    return sorted(copies, key=lambda key: (hops(key), DP_ORDERS[key[0]].index(dp_last(*key)), key[0], key))

def dp_start(copies, arrived):
    for key in dp_order(copies):
        if arrived[0] == key[0] and dp_source(*key) == arrived[1:]:
            copies[key].start()

def start_kernel(dims, exchange, *refs):
    (experts, capacity, top_count, q_cols, k_cols, rows_here, shard_rows) = dims
    (tokens_ref, pieces_ref, wout_ref, cot_ref, routes_ref, priority_ref, seg_ref, cos_ref, sin_ref,
     x_out, w_out, wout_out, h1_ref, q_ref, k_ref, v_ref, o_ref, lse_ref, middle_ref, h2_ref, table_ref, probs_ref, gains_ref, dm_ref,
     xs, ws, wouts, vt_ref, h1s, os, own_sem,
     x_send, x_recv, p_send, p_recv, w_send, w_recv, o_send, o_recv, wo_send, wo_recv, wx_send, wx_recv, dm_send, dm_recv, dm_sem) = refs
    E = lax.axis_size("expert")
    quads = lax.axis_size("q")
    dp = quads * QUAD
    q, r, e = lax.axis_index("q"), member_r(), lax.axis_index("expert")
    place = place_at(q, r)
    length, width = xs.shape
    total = ws.shape[1]
    block_rows = ws.shape[0] // dp
    heads, kv_heads = q_cols // HD, k_cols // HD
    group = heads // kv_heads
    block = 256

    barrier = pltpu.get_barrier_semaphore()
    friends = [device_at(q, r, flip(e, j)) for j in (1, 2, 3)] + [device_at(q, flip(r, m), e) for m in (1, 2)]
    friends += [device_at((q + k) % quads, r, e) for k in range(1, quads)]
    dm_copies = block_copies(cot_ref, dm_ref, DM_ORDERS, dm_send, dm_recv)
    dm_order = gather_order(DM_ORDERS)
    def dm_arrive(wanted):
        for key in wanted:
            dm_copies[key].wait_recv()
            block_start(dm_copies, DM_ORDERS, key)
    for friend in friends:
        pl.semaphore_signal(barrier, inc=1, device_id=friend, device_id_type=MESH)
    pl.semaphore_wait(barrier, len(friends))

    def token_rows(who):
        return pl.ds(pl.multiple_of(who * rows_here, 16), rows_here)

    x_copies = {}
    for j in (1, 2, 3):
        source = tokens_ref if j < 3 else xs.at[token_rows(flip(e, 2))]
        target = e if j < 3 else flip(e, 2)
        x_copies[j] = pltpu.make_async_remote_copy(source, xs.at[token_rows(target)], x_send.at[j], x_recv.at[j],
            device_id=device_at(q, r, flip(e, j if j < 3 else 1)), device_id_type=MESH)
    p_copies = []
    mine = pl.multiple_of(place * block_rows, 16)
    if exchange:
        for j in (1, 2, 3):
            rows = pl.ds(pl.multiple_of(place * block_rows + e * shard_rows, 16), shard_rows)
            copy = pltpu.make_async_remote_copy(pieces_ref.at[flip(e, j)], ws.at[rows], p_send.at[j], p_recv.at[j],
                device_id=device_at(q, r, flip(e, j)), device_id_type=MESH)
            copy.start()
            p_copies.append(copy)
        ws[pl.ds(pl.multiple_of(place * block_rows + e * shard_rows, 16), shard_rows), :] = pieces_ref[e]
    else:
        ws[pl.ds(mine, block_rows), :] = pieces_ref[...]
    def out_rows(d, who):
        return pl.ds(pl.multiple_of((d * E + who) * shard_rows, 16), shard_rows)
    if exchange:
        y_copy = pltpu.make_async_remote_copy(wout_ref, wouts.at[out_rows(place, e)], wx_send.at[0, 3], wx_recv.at[0, 3],
            device_id=device_at(q, r, flip(e, 2)), device_id_type=MESH)
        y_copy.start()
    x_copies[2].start()
    x_copies[1].start()
    for p in range(len(DM_ORDERS)):
        dm_copies[p, 2].start()
        dm_copies[p, CORE].start()
    dm_own = pltpu.make_async_copy(cot_ref, dm_ref.at[0], dm_sem)
    dm_own.start()
    xs[token_rows(e), :] = tokens_ref[...]
    w_copies = dp_copies(ws, block_rows, lambda d: pl.multiple_of(d * block_rows, 16), total // 3, w_send, w_recv)
    for copy in p_copies:
        copy.wait_recv()
    for p in range(3):
        dp_start(w_copies, (p, 0, 0))
    wo_copies = []
    if exchange:
        wouts[out_rows(place, e), :] = wout_ref[...]
        for n, who in enumerate((e, flip(e, 2))):
            wo_copies.append(dp_copies(wouts, shard_rows, lambda d, who=who: pl.multiple_of((d * E + who) * shard_rows, 16),
                width // 3, wo_send.at[n], wo_recv.at[n]))
        for p in range(3):
            dp_start(wo_copies[0], (p, 0, 0))
        y_copy.wait_recv()
        for p in range(3):
            dp_start(wo_copies[1], (p, 0, 0))

    lane = lax.broadcasted_iota(jnp.int32, (rows_here, 128), 1)
    rank = jnp.zeros((rows_here, 128), jnp.int32)
    routes, priority = routes_ref[...].T, priority_ref[...].T
    for j in range(top_count):
        rank = rank + jnp.where(routes[:, j:j + 1] == lane, priority[:, j:j + 1] + 1, 0)
    rank = rank - 1
    before = (lax.broadcasted_iota(jnp.int32, (rows_here, rows_here), 1)
              < lax.broadcasted_iota(jnp.int32, (rows_here, rows_here), 0)).astype(F32).astype(BF16)
    base = jnp.zeros((1, 128), F32)
    slot = jnp.zeros((rows_here, 128), F32)
    for level in range(top_count):
        hot = (rank == level).astype(F32)
        slot = slot + hot * (base + mm(before, hot.astype(BF16)))
        base = base + jnp.sum(hot, axis=0, keepdims=True)
    named = rank >= 0
    slot = jnp.where(named & (slot < capacity), slot, -1.0)

    x_copies[2].wait_recv()
    x_copies[3].start()
    order = dp_order(w_copies)
    wo_order = dp_order(wo_copies[0]) if exchange else []
    for key in order:
        w_copies[key].wait_recv()
        dp_start(w_copies, key)
    x_copies[1].wait_recv()
    x_copies[3].wait_recv()
    x_back = pltpu.make_async_copy(xs, x_out, own_sem.at[0])
    w_back = pltpu.make_async_copy(ws, w_out, own_sem.at[1])
    x_back.start()
    w_back.start()
    wx_copies = {}
    if exchange:
        for d in range(dp):
            for n, who in enumerate((e, flip(e, 2))):
                block_ref = wouts.at[out_rows(d, who)]
                wx_copies[d, n] = pltpu.make_async_remote_copy(block_ref, block_ref, wx_send.at[d, n], wx_recv.at[d, n],
                    device_id=device_at(q, r, flip(e, 1)), device_id_type=MESH)
    def out_step(step):
        half = -(-len(wo_order) // 2)
        if step < 2:
            for key in wo_order[step * half:(step + 1) * half]:
                for some in wo_copies:
                    some[key].wait_recv()
                    dp_start(some, key)
        if step == 1:
            for p, mask in dm_order:
                if mask in (4, 8):
                    dm_copies[p, mask].start()
            for key in wx_copies:
                wx_copies[key].start()
            dm_arrive([key for key in dm_order if key[1] == 2])
        if step == 3:
            dm_arrive([key for key in dm_order if key[1] in (4, 8)])

    small = ws[:, total - 128:].astype(F32).T
    gain_attn = small[experts:experts + 1, :]
    gain_moe = small[experts + 1:experts + 2, :]
    gains_ref[0:1, :] = gain_attn
    gains_ref[1:2, :] = gain_moe

    def send_block(b):
        rows = pl.ds(b * rows_here, rows_here)
        @pl.when(e == b)
        def _():
            os[b] = o_ref[rows, :]
        @pl.when(e != b)
        def _():
            pltpu.make_async_remote_copy(o_ref.at[rows], os.at[e], o_send.at[b], o_recv.at[e],
                device_id=device_at(q, r, b), device_id_type=MESH).start()
    sent = 0
    for i in range(length // block):
        rows = pl.ds(i * block, block)
        x = xs[rows, :].astype(F32)
        scale = lax.rsqrt(jnp.mean(x * x, axis=1, keepdims=True) + epsilon)
        h1 = (x * scale * gain_attn).astype(BF16)
        h1s[rows, :] = h1
        qkv = mm(h1, ws[:, :total - 128])
        qk = qkv[:, :q_cols + k_cols]
        turns = (q_cols + k_cols) // 128
        cosine = jnp.concatenate([cos_ref[rows, :]] * turns, axis=1)
        sine = jnp.concatenate([sin_ref[rows, :]] * turns, axis=1)
        qk = (qk * cosine + swap_halves(qk) * sine).astype(BF16)
        v = qkv[:, q_cols + k_cols:].astype(BF16)
        for h in range(heads):
            q_ref[h, rows, :] = qk[:, h * HD:(h + 1) * HD]
        vt = v.astype(F32).T.astype(BF16)
        for h in range(kv_heads):
            k_ref[h, rows, :] = qk[:, q_cols + h * HD:q_cols + (h + 1) * HD]
            v_ref[h, rows, :] = v[:, h * HD:(h + 1) * HD]
            vt_ref[h, :, rows] = vt[h * HD:(h + 1) * HD, :]
        keys = (i + 1) * block
        bias = bias_block(seg_ref[:, rows], keys, i * block)
        outs = []
        for h in range(heads):
            g = h // group
            st = mm(k_ref[g, pl.ds(0, keys), :], q_ref[h, rows, :] * BF16(HD ** -0.5), NT) + bias
            top = jnp.max(st, axis=0, keepdims=True)
            p = jnp.exp(st - top)
            sums = jnp.sum(p, axis=0, keepdims=True)
            outs.append(mm(vt_ref[g, :, pl.ds(0, keys)], p.astype(BF16)) / sums)
            lse_ref[pl.ds(h, 1), rows] = top + jnp.log(sums)
        o_ref[rows, :] = jnp.concatenate(outs, axis=0).T.astype(BF16)
        while sent < E and (sent + 1) * rows_here <= keys:
            send_block(sent)
            sent += 1
        out_step(i)
    h1_back = pltpu.make_async_copy(h1s, h1_ref, own_sem.at[2])
    h1_back.start()
    if exchange:
        for key in wx_copies:
            wx_copies[key].wait_recv()
    else:
        fill = pltpu.make_async_copy(wout_ref, wouts, own_sem.at[3])
        fill.start()
        fill.wait()
    wout_back = pltpu.make_async_copy(wouts, wout_out, own_sem.at[3])
    wout_back.start()
    def o_descriptor(b):
        return pltpu.make_async_remote_copy(o_ref.at[pl.ds(0, rows_here)], os.at[b], o_send.at[b], o_recv.at[b],
            device_id=device_at(q, r, flip(e, 1)), device_id_type=MESH)
    middle = xs[token_rows(e), :].astype(F32)
    for b in range(E):
        @pl.when(e != b)
        def _():
            o_descriptor(b).wait_recv()
    for b in range(E):
        middle = middle + mm(os[b], wouts[b * q_cols:(b + 1) * q_cols, :])
    middle_ref[...] = middle
    scale = lax.rsqrt(jnp.mean(middle * middle, axis=1, keepdims=True) + epsilon)
    h2 = (middle * scale * gain_moe).astype(BF16)
    h2_ref[...] = h2
    logits = jnp.where(named, mm(h2, ws[:, total - 128:]), masked_score)
    powers = jnp.where(named, jnp.exp(logits - jnp.max(logits, axis=1, keepdims=True)), 0.0)
    probs = powers / jnp.sum(powers, axis=1, keepdims=True)
    probs_ref[...] = probs
    slot_rows = slot.T
    prob_rows = probs.T
    local = experts // E
    table_ref[...] = jnp.zeros_like(table_ref)
    for dest_r in range(QUAD):
        for dest_e in range(E):
            for at, expert in enumerate(device_experts(local, dest_r)):
                row = dest_e * local + expert
                table_ref[dest_r * E + dest_e, at:at + 1, :] = slot_rows[row:row + 1, :]
                table_ref[dest_r * E + dest_e, 4 + at:5 + at, :] = prob_rows[row:row + 1, :]
    dm_arrive([key for key in dm_order if key[1] not in (2, 4, 8)])
    for key in dm_copies:
        if key[1] & CORE:
            dm_copies[key].wait_recv()
    for key in dm_copies:
        dm_copies[key].wait_send()
    dm_own.wait()
    for b in range(E):
        @pl.when(e != b)
        def _():
            o_descriptor(b).wait_send()
    for copy in p_copies + list(x_copies.values()) + list(w_copies.values()) + list(wx_copies.values()):
        copy.wait_send()
    for some in wo_copies:
        for key in some:
            some[key].wait_send()
    if exchange:
        y_copy.wait_send()
    for copy in (x_back, w_back, h1_back, wout_back):
        copy.wait()

def start_call(tokens, pieces, w_out, cotangent, routes, priority, segments, cosine, sine, experts, capacity, q_cols, k_cols, exchange):
    E, quads = lax.axis_size("expert"), lax.axis_size("q")
    dp = quads * QUAD
    rows_here, width = tokens.shape
    length = rows_here * E
    shard_rows = width // (dp * E)
    total = pieces.shape[-1]
    V, A = pl.BlockSpec(memory_space=pltpu.VMEM), pl.BlockSpec(memory_space=pl.ANY)
    heads, kv_heads = q_cols // HD, k_cols // HD
    S = jax.ShapeDtypeStruct
    sem = pltpu.SemaphoreType.DMA
    dims = (experts, capacity, routes.shape[0], q_cols, k_cols, rows_here, shard_rows)
    kernel = functools.partial(start_kernel, dims, exchange)
    return pl.pallas_call(kernel,
        out_shape=(S((length, width), BF16), S((width, total), BF16), S((width, width), BF16), S((length, width), BF16),
            S((heads, length, HD), BF16), S((kv_heads, length, HD), BF16), S((kv_heads, length, HD), BF16),
            S((length, q_cols), BF16), S((-(-heads // 8) * 8, length), F32), S((rows_here, width), F32), S((rows_here, width), BF16),
            S((QUAD * E, 8, rows_here), F32), S((rows_here, 128), F32), S((8, width), F32),
            S((QUAD * E, rows_here, width), BF16)),
        in_specs=[V, V, V if exchange else A, A, V, V, V, V, V], out_specs=(A, A, A, A) + (V,) * 10 + (A,),
        scratch_shapes=[pltpu.VMEM((length, width), BF16), pltpu.VMEM((width, total), BF16), pltpu.VMEM((width, width), BF16),
            pltpu.VMEM((kv_heads, HD, length), BF16), pltpu.VMEM((length, width), BF16), pltpu.VMEM((E, rows_here, q_cols), BF16), sem((4,)),
            sem((4,)), sem((4,)), sem((4,)), sem((4,)), sem((3, quads, QUAD)), sem((3, quads, QUAD)), sem((E,)), sem((E,)),
            sem((2, 3, quads, QUAD)), sem((2, 3, quads, QUAD)), sem((dp, 4)), sem((dp, 4)),
            sem((len(DM_ORDERS), 16)), sem((len(DM_ORDERS), 16)), sem],
        compiler_params=pltpu.CompilerParams(vmem_limit_bytes=58 << 20, collective_id=4, has_side_effects=True),
        cost_estimate=CHEAP,
        name="start")(tokens, pieces, w_out, cotangent, routes, priority, segments.reshape(1, -1), cosine, sine)


DENSE_ORDERS = ((1, 2, "q"), (2, 1, "q"))

def back_kernel(dims, exchange, carried, *refs):
    (experts, q_cols, k_cols, slots) = dims
    (dr_ref, dg_ref, probs_ref, h2_ref, middle_ref, cot_ref, gains_ref, tokens_ref, wout_ref, q_ref, k_ref, v_ref, lse_ref,
     cos_ref, sin_ref, seg_ref, h1_ref, xall_ref, wall_ref, mixed_ref, grads_ref, _) = refs[:22]
    refs = refs[22:]
    if exchange:
        (tokens_out, gq_ref, gk_ref, gv_ref, small_ref, gout_ref, moved_ref) = refs[:7]
        refs = refs[7:]
    else:
        (tokens_out, dense_ref, gout_ref, moved_ref) = refs[:4]
        refs = refs[4:]
    (h1s, xs, ws, mixeds, load_sem, dgt, dats, dos, do_out, kt_ref, dk_ref, dv_ref, dqkv, dx1s, small, part, core_in, y_in,
     g1, g2, r1, r2, f1,
     do_send, do_recv, dat_send, dat_recv, part_send, part_recv, g1_send, g1_recv, g2_send, g2_recv, f_send, f_recv, carry_send, carry_recv) = refs
    E, quads = lax.axis_size("expert"), lax.axis_size("q")
    q, r, e = lax.axis_index("q"), member_r(), lax.axis_index("expert")
    dp = quads * QUAD
    rows_here, width = dr_ref.shape
    length = rows_here * E
    heads, kv_heads = q_cols // HD, k_cols // HD
    group = heads // kv_heads
    total = ws.shape[1]
    qkv_cols = total - 128
    factor = HD ** -0.5
    block = 256
    loads = [pltpu.make_async_copy(a, b, load_sem.at[i])
             for i, (a, b) in enumerate(((wall_ref, ws), (mixed_ref, mixeds), (h1_ref, h1s), (xall_ref, xs.at[pl.ds(0, length)])))]
    load_out = pltpu.make_async_copy(wout_ref, xs, load_sem.at[4])
    load_out.start()
    for load in loads[:3]:
        load.start()
    near = [(0, 1), (0, 2)] + [(k, 0) for k in range(1, quads)]
    far = sorted({(k, m) for _, k, m, _ in carried} - set(near))
    greet_devices([device_at(q, r, flip(e, j)) for j in (1, 2, 3)] + [relative_device(k, m) for k, m in near + far])
    carries = carry_copies(grads_ref, moved_ref, carried, carry_send, carry_recv)
    carry_start(carries, carried, False)

    dgt[...] = jnp.zeros_like(dgt)
    local = experts // E
    whole = local // QUAD
    for mask in range(QUAD * E):
        from_r, from_e = flip(r, mask >> 2), flip(e, mask & 3)
        for k in range(slots):
            if k < whole:
                row = from_e * local + from_r * whole + k
            else:
                row = from_e * local + QUAD * whole + from_r // (QUAD // (local - QUAD * whole))
            dgt[pl.ds(row, 1), :] += dg_ref[mask, k:k + 1, :]
    dg = dgt[...].T
    probs = probs_ref[...]
    dz = (probs * (dg - jnp.sum(probs * dg, axis=1, keepdims=True))).astype(BF16)
    loads[0].wait()
    dh2 = dr_ref[...] + mm(dz, ws[:, qkv_cols:], NT)
    gain_attn, gain_moe = gains_ref[0:1, :], gains_ref[1:2, :]
    middle = middle_ref[...]
    scale = lax.rsqrt(jnp.mean(middle * middle, axis=1, keepdims=True) + epsilon)
    unit = middle * scale
    grad_moe_gain = jnp.sum(dh2 * unit, axis=0, keepdims=True)
    grad_unit = dh2 * gain_moe
    dx1 = cot_ref[...].astype(F32) + scale * (grad_unit - unit * jnp.mean(grad_unit * unit, axis=1, keepdims=True))
    dx1s[...] = dx1
    dat = dx1.astype(BF16)

    def token_rows(who):
        return pl.ds(pl.multiple_of(who * rows_here, 16), rows_here)
    load_out.wait()
    for b in range(E):
        do = mm(dat, xs[b * q_cols:(b + 1) * q_cols, :], NT).astype(BF16)
        do_out[b] = do
        @pl.when(e == b)
        def _():
            dos[token_rows(e), :] = do_out[b]
        @pl.when(e != b)
        def _():
            pltpu.make_async_remote_copy(do_out.at[b], dos.at[token_rows(e)], do_send.at[b], do_recv.at[e],
                device_id=device_at(q, r, b), device_id_type=MESH).start()
    loads[3].start()
    def do_descriptor(b):
        return pltpu.make_async_remote_copy(do_out.at[b], dos.at[pl.ds(b * rows_here, rows_here)], do_send.at[b], do_recv.at[b],
            device_id=device_at(q, r, flip(e, 1)), device_id_type=MESH)
    dats[token_rows(e), :] = dat
    dat_copies = {}
    for j in (1, 2, 3):
        rows = token_rows(e if j < 3 else flip(e, 2))
        dat_copies[j] = pltpu.make_async_remote_copy(dats.at[rows], dats.at[rows], dat_send.at[j], dat_recv.at[j],
            device_id=device_at(q, r, flip(e, j if j < 3 else 1)), device_id_type=MESH)
    dat_copies[2].start()
    dat_copies[1].start()
    small[...] = mm(h2_ref[...], dz, TN)
    dk_ref[...] = jnp.zeros_like(dk_ref)
    dv_ref[...] = jnp.zeros_like(dv_ref)
    for g in range(kv_heads):
        kt_ref[g] = k_ref[g].astype(F32).T.astype(BF16)

    seen = 0
    for i in range(length // block):
        rows = pl.ds(i * block, block)
        keys = (i + 1) * block
        while seen * rows_here < keys:
            @pl.when(e != seen)
            def _():
                do_descriptor(seen).wait_recv()
            seen += 1
        span = pl.ds(0, keys)
        bias = bias_block(seg_ref[:, rows], keys, i * block)
        dqs = []
        for h in range(heads):
            g = h // group
            qh = q_ref[h, rows, :]
            do = dos[rows, h * HD:(h + 1) * HD]
            st = mm(k_ref[g, span, :], qh * BF16(factor), NT) + bias
            p = jnp.exp(st - lse_ref[pl.ds(h, 1), rows])
            dpt = mm(v_ref[g, span, :], do, NT)
            inner = jnp.sum(p * dpt, axis=0, keepdims=True)
            ds = (p * (dpt - inner)).astype(BF16)
            dv_ref[g, span, :] += mm(p.astype(BF16), do)
            dk_ref[g, span, :] += mm(ds, qh)
            dqs.append(mm(kt_ref[g, :, span], ds))
        dq = jnp.concatenate(dqs, axis=0).T * factor
        cosine = jnp.concatenate([cos_ref[rows, :]] * (q_cols // 128), axis=1)
        sine = jnp.concatenate([sin_ref[rows, :]] * (q_cols // 128), axis=1)
        dqkv[rows, :q_cols] = (dq * cosine - swap_halves(dq) * sine).astype(BF16)
        if i == 1:
            dat_copies[2].wait_recv()
            dat_copies[3].start()
            carry_start(carries, carried, True)
    dk = jnp.concatenate([dk_ref[g] for g in range(kv_heads)], axis=1) * factor
    cosine = jnp.concatenate([cos_ref[...]] * (k_cols // 128), axis=1)
    sine = jnp.concatenate([sin_ref[...]] * (k_cols // 128), axis=1)
    dqkv[:, q_cols:q_cols + k_cols] = (dk * cosine - swap_halves(dk) * sine).astype(BF16)
    dqkv[:, q_cols + k_cols:] = jnp.concatenate([dv_ref[g] for g in range(kv_heads)], axis=1).astype(BF16)

    grad_attn_gain = jnp.zeros((1, width), F32)
    loads[3].wait()
    part_copies = {}
    own = None
    for j in (3, 1, 2, 0):
        rows = token_rows(flip(e, j))
        dh1 = mm(dqkv[rows, :], ws[:, :qkv_cols], NT)
        x = xs[rows, :].astype(F32)
        scale = lax.rsqrt(jnp.mean(x * x, axis=1, keepdims=True) + epsilon)
        grad_attn_gain = grad_attn_gain + jnp.sum(dh1 * (x * scale), axis=0, keepdims=True)
        if j & 1:
            part[j - 1] = dh1.astype(BF16)
            part_copies[j] = pltpu.make_async_remote_copy(part.at[j - 1], core_in.at[j // 2], part_send.at[j], part_recv.at[j],
                device_id=device_at(q, r, flip(e, 1)), device_id_type=MESH)
            part_copies[j].start()
        elif j == 2:
            part_copies[3].wait_recv()
            part[1] = (dh1 + core_in[1].astype(F32)).astype(BF16)
            part_copies[2] = pltpu.make_async_remote_copy(part.at[1], y_in, part_send.at[2], part_recv.at[2],
                device_id=device_at(q, r, flip(e, 2)), device_id_type=MESH)
            part_copies[2].start()
        else:
            own = dh1

    rows_out = lax.broadcasted_iota(jnp.int32, (128, width), 0)
    gains = jnp.where(rows_out == experts, grad_attn_gain, 0.0) + jnp.where(rows_out == experts + 1, grad_moe_gain, 0.0)
    small_all = small[...] + gains.T
    loads[2].wait()
    share = width // dp
    grad = mm(h1s[...], dqkv[...], TN).astype(BF16)
    for d in range(dp):
        g1[d, :, :qkv_cols] = grad[d * share:(d + 1) * share]
        g1[d, :, qkv_cols:] = small_all[d * share:(d + 1) * share].astype(BF16)
    dat_copies[1].wait_recv()
    dat_copies[3].wait_recv()
    loads[1].wait()
    grad = mm(mixeds[...], dats[...], TN)
    out_share = q_cols // dp
    if exchange:
        for d in range(dp):
            g2[d] = grad[d * out_share:(d + 1) * out_share].astype(BF16)
    else:
        gout_ref[...] = grad.astype(BF16)
    arrays = [(g1, r1, g1_send, g1_recv)] + ([(g2, r2, g2_send, g2_recv)] if exchange else [])
    keys = [(k, m) for k in range(quads) for m in range(QUAD)]
    def at(k, m):
        return place_at((q + k) % quads, flip(r, m))
    def has(key, dim):
        return key[0] if dim == "q" else key[1] & dim
    def first(p, key):
        return [n for n, dim in enumerate(DENSE_ORDERS[p]) if has(key, dim)][0]
    def sources(p, key, upto):
        found = []
        for dim in DENSE_ORDERS[p][:upto]:
            found += [(k, key[1]) for k in range(1, quads)] if dim == "q" else [(key[0], key[1] | dim)]
        return found
    copies = {}
    for n, (grad_ref, landing, send, recv) in enumerate(arrays):
        half = grad_ref.shape[2] // 2
        for p in range(2):
            for k, m in keys[1:]:
                dim = DENSE_ORDERS[p][first(p, (k, m))]
                device = device_at((q + k) % quads, r, e) if dim == "q" else device_at(q, flip(r, dim), e)
                copies[n, p, k, m] = pltpu.make_async_remote_copy(grad_ref.at[at(k, m), :, pl.ds(p * half, half)],
                    landing.at[p, k, m], send.at[p, k, m], recv.at[p, k, m], device_id=device, device_id_type=MESH)
    numbers = range(len(arrays))
    def reduced(n, p, key):
        grad_ref, landing = arrays[n][:2]
        half = grad_ref.shape[2] // 2
        sum_now = grad_ref[at(*key), :, p * half:(p + 1) * half].astype(F32)
        for k, m in sources(p, key, 3 if key == (0, 0) else first(p, key)):
            copies[n, p, k, m].wait_recv()
            sum_now = sum_now + landing[p, k, m].astype(F32)
        return sum_now
    def send_on(level):
        for p in range(2):
            now = [key for key in keys[1:] if first(p, key) == level]
            now.sort(key=lambda key: -sum(1 for dim in DENSE_ORDERS[p] if has(key, dim)))
            for k, m in now:
                for n in numbers:
                    if level:
                        half = arrays[n][0].shape[2] // 2
                        arrays[n][0][at(k, m), :, p * half:(p + 1) * half] = reduced(n, p, (k, m)).astype(BF16)
                    copies[n, p, k, m].start()
    send_on(0)
    send_on(1)
    part_copies[1].wait_recv()
    part_copies[2].wait_recv()
    dh1 = own + core_in[0].astype(F32) + y_in[...].astype(F32)
    x = tokens_ref[...].astype(F32)
    scale = lax.rsqrt(jnp.mean(x * x, axis=1, keepdims=True) + epsilon)
    unit = x * scale
    grad_unit = dh1 * gain_attn
    tokens_out[...] = dx1s[...] + scale * (grad_unit - unit * jnp.mean(grad_unit * unit, axis=1, keepdims=True))
    send_on(2)
    final = {(n, p): reduced(n, p, (0, 0)) for n in numbers for p in range(2)}
    dense = jnp.concatenate([final[0, 0], final[0, 1]], axis=1)
    if exchange:
        gout_ref[...] = jnp.concatenate([final[1, 0], final[1, 1]], axis=1).astype(BF16)
        g1[at(0, 0)] = dense.astype(BF16)
        shard = share // E
        f_copies = []
        for j in (1, 2, 3):
            rows = pl.ds(pl.multiple_of(flip(e, j) * shard, 16), shard)
            copy = pltpu.make_async_remote_copy(g1.at[at(0, 0), rows], f1.at[e], f_send.at[j], f_recv.at[j],
                device_id=device_at(q, r, flip(e, j)), device_id_type=MESH)
            copy.start()
            f_copies.append(copy)
        f1[e] = g1[at(0, 0), pl.ds(pl.multiple_of(e * shard, 16), shard), :]
        for copy in f_copies:
            copy.wait_recv()
        tail = jnp.zeros((shard, 128), F32)
        for b in range(E):
            piece = f1[b].astype(F32)
            gq_ref[:, b * q_cols:(b + 1) * q_cols] = piece[:, :q_cols]
            gk_ref[:, b * k_cols:(b + 1) * k_cols] = piece[:, q_cols:q_cols + k_cols]
            gv_ref[:, b * k_cols:(b + 1) * k_cols] = piece[:, q_cols + k_cols:qkv_cols]
            tail = tail + piece[:, qkv_cols:]
        small_ref[...] = tail
        for copy in f_copies:
            copy.wait_send()
    else:
        dense_ref[...] = dense.astype(BF16)
    for b in range(E):
        @pl.when(e != b)
        def _():
            do_descriptor(b).wait_send()
    for copy in list(dat_copies.values()) + list(part_copies.values()) + list(copies.values()):
        copy.wait_send()
    carry_wait(carries, carried)

def back_call(dr_sum, dg_back, probs, h2, middle, cotangent, gains, tokens, out_full, query, key, value, log_total,
              cosine, sine, segments, h1_all, x_all, w_all, mixed, grads, moved, carried, experts, q_cols, k_cols, slots, exchange):
    E, quads = lax.axis_size("expert"), lax.axis_size("q")
    dp = quads * QUAD
    rows_here, width = tokens.shape
    length = rows_here * E
    total = w_all.shape[1]
    heads, kv_heads = q_cols // HD, k_cols // HD
    share, out_share = width // dp, q_cols // dp
    shard = share // E
    V, A = pl.BlockSpec(memory_space=pltpu.VMEM), pl.BlockSpec(memory_space=pl.ANY)
    S, M, sem = jax.ShapeDtypeStruct, pltpu.VMEM, pltpu.SemaphoreType.DMA
    if exchange:
        outs = (S((rows_here, width), F32), S((shard, q_cols * E), F32), S((shard, k_cols * E), F32), S((shard, k_cols * E), F32),
            S((shard, 128), F32), S((out_share, width), BF16))
        second = [M((dp, out_share, width), BF16), M((2, quads, QUAD, out_share, width // 2), BF16)]
    else:
        outs = (S((rows_here, width), F32), S((share, total), BF16), S((q_cols, width), BF16))
        second = [M((16, 128), BF16)] * 2
    scratch = [M((length, width), BF16), M((width, width), BF16), M((width, total), BF16), M((length, q_cols), BF16), sem((5,)),
        M((128, rows_here), F32), M((length, width), BF16), M((length, q_cols), BF16), M((E, rows_here, q_cols), BF16),
        M((kv_heads, HD, length), BF16), M((kv_heads, length, HD), F32), M((kv_heads, length, HD), F32), M((length, total - 128), BF16),
        M((rows_here, width), F32), M((width, 128), F32), M((3, rows_here, width), BF16), M((2, rows_here, width), BF16),
        M((rows_here, width), BF16),
        M((dp, share, total), BF16), second[0],
        M((2, quads, QUAD, share, total // 2), BF16), second[1], M((E, shard, total), BF16)]
    scratch += [sem((4,))] * 6 + [sem((2, quads, 4))] * 4 + [sem((4,))] * 2 + [sem(moved.shape[:3])] * 2
    outs += (S(moved.shape, moved.dtype),)
    return pl.pallas_call(functools.partial(back_kernel, (experts, q_cols, k_cols, slots), exchange, carried),
        out_shape=outs, in_specs=[V] * 8 + [A] + [V] * 7 + [A] * 6, out_specs=(V,) * (len(outs) - 1) + (A,), scratch_shapes=scratch,
        input_output_aliases={21: len(outs) - 1},
        compiler_params=pltpu.CompilerParams(vmem_limit_bytes=60 << 20, collective_id=5, has_side_effects=True),
        cost_estimate=CHEAP,
        name="backward")(dr_sum, dg_back, probs, h2, middle, cotangent, gains, tokens, out_full, query, key, value, log_total,
            cosine, sine, segments.reshape(1, -1), h1_all, x_all, w_all, mixed, grads, moved)


ALL = ("q", "rh", "rl", "expert")
DP = ("q", "rh", "rl")
GROUP = ("rh", "rl", "expert")


def shards(
    tokens, w_query, w_key, w_value, w_out, w_router, gain_attn, gain_moe,
    w_gate, w_up, w_down, segments, routes, priority, cotangent,
):
    rows_here, width = tokens.shape
    E = lax.axis_size("expert")
    R = QUAD
    Q = lax.axis_size("q")
    e = lax.axis_index("expert")
    r = member_r()
    shard_rows = w_query.shape[0]
    local = w_gate.shape[0]
    experts = local * E
    ffn = w_gate.shape[2]
    capacity = rows_here * routes.shape[1] // experts
    length = rows_here * E
    sources = R * E
    q_cols = w_query.shape[1] // E
    k_cols = w_key.shape[1] // E
    exchange = shard_rows % 16 == 0
    small = jnp.concatenate([w_router, gain_attn[:, None], gain_moe[:, None]], axis=1)
    small = jnp.pad(small, ((0, 0), (0, 128 - small.shape[1])))
    pieces = jnp.concatenate(
        [w.reshape(shard_rows, E, -1) for w in (w_query, w_key, w_value)]
        + [jnp.broadcast_to(small[:, None], (shard_rows, E, 128))],
        axis=2,
    )
    pieces = jnp.transpose(pieces, (1, 0, 2))
    out_part = w_out
    if not exchange:
        pieces = lax.all_to_all(pieces, "expert", split_axis=0, concat_axis=0, tiled=True)
        pieces = pieces.reshape(E * shard_rows, -1)
        out_part = lax.all_gather(w_out, ALL, axis=0, tiled=True)
    cosine, sine = (jnp.asarray(t) for t in rope_tables(length))
    (x_all, w_all, out_full, h1_all, query, key, value, mixed, log_total, middle, h2, table, probs, gains, dm_all) = start_call(
        tokens, pieces, out_part, cotangent, routes.T, priority.T, segments, cosine, sine, experts, capacity, q_cols, k_cols, exchange
    )
    qkv_cols = q_cols + 2 * k_cols
    dp = Q * R
    whole = local // R
    rest = local - whole * R
    ways = R // rest if rest else 1
    slots = whole + (1 if rest else 0)

    rows, dm_rows, weight, tables = gather_rows(h2, table, dm_all, slots, capacity, 1)
    def scalars(places):
        return jnp.stack(places + [r % ways]).astype(jnp.int32)

    banks = (w_gate, w_up, w_down)
    done = []
    if rest:
        part = expert_call(rows, dm_rows, weight, whole, 1, *banks, scalars([R * whole + r // ways]), dp, ways)
        part_moved = lax.all_to_all(part[3], DP, split_axis=0, concat_axis=0, tiled=True)
    done.append(expert_call(rows, dm_rows, weight, 0, whole, *banks, scalars([r * whole + s for s in range(whole)]), dp, 1))
    grads = done[0][3]
    if rest:
        done.append(part)
    plan = carry_plan(Q, whole)
    y_rows, dr_rows, dg_rows = ([d[n] for d in done] for n in range(3))
    dr_sum, dg_back, moved = combine_rows(dr_rows, tables, dg_rows, None, grads, None, plan[0], capacity, 2)
    if rest:
        (dr_sum, part_moved) = lax.optimization_barrier((dr_sum, part_moved))
    out = back_call(
        dr_sum, dg_back, probs, h2, middle, cotangent, gains, tokens, out_full, query, key, value, log_total,
        cosine, sine, segments, h1_all, x_all, w_all, mixed, grads, moved, plan[1],
        experts, q_cols, k_cols, slots, exchange
    )
    moved = out[-1]
    if exchange:
        grad_tokens, grad_query, grad_key, grad_value, small_own, out_sum = out[:-1]
    else:
        grad_tokens, qkv_sum, out_sum = out[:-1]
        qkv_own = lax.all_to_all(
            qkv_sum.reshape(E, shard_rows, -1), "expert", split_axis=0, concat_axis=0, tiled=True
        )
        qkv_own = jnp.transpose(qkv_own, (1, 0, 2)).astype(F32)
        small_own = jnp.sum(qkv_own[:, :, qkv_cols:], axis=1)
        grad_query = qkv_own[:, :, :q_cols].reshape(shard_rows, -1)
        grad_key = qkv_own[:, :, q_cols : q_cols + k_cols].reshape(shard_rows, -1)
        grad_value = qkv_own[:, :, q_cols + k_cols : qkv_cols].reshape(shard_rows, -1)
        out_sum = lax.psum_scatter(out_sum, DP, scatter_dimension=0, tiled=True)
    perm = [(p * E + x, dp * x + p) for p in range(dp) for x in range(E)]
    out_own = lax.ppermute(out_sum, ALL, perm).astype(F32)
    outputs, moved = combine_rows(y_rows, tables, None, middle, grads, moved, plan[2], capacity, 3)
    order = jnp.stack([r ^ m for m in range(R)]).astype(jnp.int32)
    gate_share, up_share, down_share = place_call(moved, [part_moved] if rest else [], order, local, ffn, width)
    return (
        outputs,
        grad_tokens,
        grad_query,
        grad_key,
        grad_value,
        out_own,
        small_own[:, :experts],
        small_own[:, experts],
        small_own[:, experts + 1],
        gate_share,
        up_share,
        down_share,
    )


def solution(mesh):
    dp, ex = mesh.devices.shape
    fine = Mesh(mesh.devices.reshape(dp // QUAD, 2, 2, ex), ALL)
    row, flat = P(ALL, None), P(ALL)
    bank = P("expert", None, None)
    spread = P("expert", DP, None)
    return jax.shard_map(
        shards,
        mesh=fine,
        in_specs=(row,) * 6 + (flat,) * 2 + (bank,) * 3 + (P(DP),) + (row,) * 3,
        out_specs=(row,) * 7 + (flat,) * 2 + (spread,) * 3,
        check_vma=False,
    )
```
